256 devices in a mesh: section: 4 (over z_hi), dp: 64 (over z_lo, x, y, core).
Axes of the slice: x: 4, y: 4, z: 8 (z_hi: 4, z_lo: 2; z = z_hi * 2 + z_lo), core: 2. Of those that a mesh axis runs over, the one named last changes fastest.
Arguments:
- acts: bfloat16 [4, 2, 4096, 4096], P('section', None, 'dp'), may hold values from -16 to 16
- cotangent: bfloat16 [2, 4096, 4096], P(None, 'dp'), may hold values from -16 to 16
- perm_up: int32 [4, 4096], P('section'), may hold values from 0 to 4095, each once within a row
- perm_dn: int32 [4, 4096], P('section'), may hold values from 0 to 4095, each once within a row
- left_up: bfloat16 [4, 4096, 256], P('section', 'dp'), may hold values from -0.375 to 0.375
- right_up: bfloat16 [4, 4096, 256], P('section', 'dp'), may hold values from -0.75 to 0.75
- right_dn: bfloat16 [4, 4096, 256], P('section', 'dp'), may hold values from -0.375 to 0.375
- left_dn: bfloat16 [4, 4096, 256], P('section', 'dp'), may hold values from -0.375 to 0.375
Outputs:
- input_grads: bfloat16 [4, 2, 4096, 4096], P('section', None, 'dp')
- grad_left_up: float32 [4, 4096, 256], P('section', 'dp')
- grad_right_up: float32 [4, 4096, 256], P('section', 'dp')
- grad_right_dn: float32 [4, 4096, 256], P('section', 'dp')
- grad_left_dn: float32 [4, 4096, 256], P('section', 'dp')
The draws below stay inside these ranges and needn't reach their ends.
Inputs may be any that keep to these rules, and one draw needn't show every extreme that they name: Every row of perm_up names each of 0 to 4095 once. Every row of perm_dn names each of 0 to 4095 once.
All inputs are finite; a program needn't handle non-finite values.
Results may differ from the reference program's by a relative error of at most 0.028.
Values may be sent and summed in bfloat16 or wider, within the bound.
No kernel may reach another device: no remote copies, remote signals or barrier semaphores. Data moves between devices by JAX's collectives and lax.ppermute only.
A program may use at most 128 MiB of HBM per device.

```python
import math
import jax
import jax.numpy as jnp
from jax import lax

D = 4096
FF = 16384
BLK = 256
MICRO = 2
DIN = 64
TOKENS = 4096
N_SECTION = 4


def strengthened(values, stream_key, source, target, shards_of, factor):
    owner, partner = [(jnp.arange(values.shape[dim]) // (values.shape[dim] // shards_of)).reshape([-1 if axis == dim else 1 for axis in range(values.ndim)]) for dim in (source, target)]
    chosen = jax.random.permutation(stream_key, shards_of)[partner]
    strong = (owner == chosen) | (owner == (partner + shards_of // 2) % shards_of)
    return jnp.where(strong, factor * values, values)


def levels(own_key, dims, shards, low, largest):
    level, own = 1.0, jax.random.fold_in(own_key, 6)
    for axis_at, parts in shards:
        draws = jnp.exp(jax.random.uniform(jax.random.fold_in(own, axis_at), (parts,), jnp.float32, low / len(shards), largest / len(shards)))
        level = level * jnp.repeat(draws, dims[axis_at] // parts).reshape([-1 if axis == axis_at else 1 for axis in range(len(dims))])
    return level


def gaussian(rng, shape, spread, most, cuts=(), kind=jnp.bfloat16):
    drawn = spread * jax.random.normal(rng, shape, jnp.float32)
    if cuts:
        drawn = drawn * levels(rng, shape, cuts, -0.22, 0.18)
    return jnp.clip(drawn, -most, most).astype(kind)


def heavy_noise(own_key, extent, deviation, reach, split, heavy, held_as=jnp.bfloat16):
    array = deviation * jax.random.normal(own_key, extent, jnp.float32)
    if split:
        array = array * levels(own_key, extent, split, -0.22, 0.18)
    return jnp.clip(strengthened(array, jax.random.fold_in(own_key, 3), *heavy), -reach, reach).astype(held_as)


def setup_inputs(seed: int = 0) -> dict:
    key_list = jax.random.split(jax.random.key(seed), 9)
    acts = heavy_noise(key_list[0], (N_SECTION, MICRO, TOKENS, D), 1.0, 16.0, ((0, 4), (2, 64)), (2, 3, 64, 4.0))
    cotangent = heavy_noise(key_list[1], (MICRO, TOKENS, D), 1.0, 16.0, ((1, 64),), (1, 2, 64, 4.0))
    perm_up = jax.vmap(lambda own: jax.random.permutation(own, D))(jax.random.split(key_list[2], N_SECTION)).reshape((N_SECTION, D)).astype(jnp.int32)
    perm_dn = jax.vmap(lambda own: jax.random.permutation(own, D))(jax.random.split(key_list[3], N_SECTION)).reshape((N_SECTION, D)).astype(jnp.int32)
    left_up = gaussian(key_list[4], (N_SECTION, D, BLK), BLK ** -0.5, 0.375, ((0, 4), (1, 64)))
    right_up = gaussian(key_list[5], (N_SECTION, D, BLK), DIN ** -0.5, 0.75, ((0, 4), (1, 64)))
    right_dn = gaussian(key_list[6], (N_SECTION, D, BLK), BLK ** -0.5, 0.375, ((0, 4), (1, 64)))
    left_dn = gaussian(key_list[7], (N_SECTION, D, BLK), BLK ** -0.5, 0.375, ((0, 4), (1, 64)))
    return dict(acts=acts, cotangent=cotangent, perm_up=perm_up, perm_dn=perm_dn, left_up=left_up, right_up=right_up, right_dn=right_dn, left_dn=left_dn)


epsilon = 1e-06

def inverse_of(permute):
    count = permute.shape[0]
    return jnp.zeros((count,), jnp.int32).at[permute].set(jnp.arange(count, dtype=jnp.int32))

def contract(form, first, second):
    return jnp.einsum(form, first.astype(jnp.float32), second.astype(jnp.float32))

def rounded(values):
    return lax.optimization_barrier(values.astype(jnp.bfloat16))

def layer_back(layer_in, grad_in, tables, weights):
    perm_first, perm_second, inv_first, inv_second = tables
    left_first, right_first, right_second, left_second = weights
    row_count = layer_in.shape[0]
    nblock, width, _ = left_first.shape
    nhidden, narrow, _ = right_first.shape
    in_float = layer_in.astype(jnp.float32)
    scaling = lax.rsqrt(lax.optimization_barrier(jnp.mean(in_float * in_float, axis=-1, keepdims=True)) + epsilon)
    normf = in_float * scaling
    normed = rounded(normf)
    up_mid = rounded(contract('tjb,jbo->tjo', normed.reshape(row_count, nblock, width), left_first)).reshape(row_count, -1)
    shuffled = jnp.take(up_mid, perm_first, axis=1).reshape(row_count, nhidden, narrow)
    hidden = contract('tki,kio->tko', shuffled, right_first)
    squashed = jax.nn.sigmoid(hidden)
    active = rounded(hidden * squashed)
    slope = rounded(squashed * (1.0 + hidden * (1.0 - squashed)))
    down_mid = rounded(contract('tko,kio->tki', active, right_second)).reshape(row_count, -1)
    placed = jnp.take(down_mid, perm_second, axis=1).reshape(row_count, nblock, width)
    grad_out = grad_in.reshape(row_count, nblock, width)
    grad_placed = rounded(contract('tjo,jio->tji', grad_out, left_second)).reshape(row_count, -1)
    grad_left_second = contract('tji,tjo->jio', placed, grad_out)
    grad_down = jnp.take(grad_placed, inv_second, axis=1).reshape(row_count, nhidden, narrow)
    grad_right_second = contract('tko,tki->kio', active, grad_down)
    grad_active = rounded(contract('tki,kio->tko', grad_down, right_second))
    grad_hidden = rounded(grad_active.astype(jnp.float32) * slope.astype(jnp.float32))
    grad_right_first = contract('tki,tko->kio', shuffled, grad_hidden)
    grad_shuffled = rounded(contract('tko,kio->tki', grad_hidden, right_first)).reshape(row_count, -1)
    grad_upmid = jnp.take(grad_shuffled, inv_first, axis=1).reshape(row_count, nblock, width)
    grad_left_first = contract('tjb,tjo->jbo', normed.reshape(row_count, nblock, width), grad_upmid)
    grad_norm = contract('tjo,jbo->tjb', grad_upmid, left_first).reshape(row_count, -1)
    inner = lax.optimization_barrier(jnp.mean(grad_norm * normf, axis=-1, keepdims=True))
    grad_input = grad_in.astype(jnp.float32) + scaling * (grad_norm - normf * inner)
    terms = (grad_left_first.reshape(-1, width), grad_right_first.reshape(-1, width), grad_right_second.reshape(-1, width), grad_left_second.reshape(-1, width))
    return (grad_input.astype(jnp.bfloat16), terms)

def reference(acts, cotangent, perm_up, perm_dn, left_up, right_up, right_dn, left_dn):
    section_count = acts.shape[0]
    micro_count = acts.shape[1]
    token_count = acts.shape[2]
    block_rows = math.gcd(token_count, 2048)
    nblock = D // BLK
    nhidden = FF // BLK
    narrow = D // nhidden
    input_list = [None] * section_count
    grad_list = [None] * section_count
    carried = cotangent
    for section_index in reversed(range(section_count)):
        weights = (left_up[section_index].reshape(nblock, BLK, BLK), right_up[section_index].reshape(nhidden, narrow, BLK), right_dn[section_index].reshape(nhidden, narrow, BLK), left_dn[section_index].reshape(nblock, BLK, BLK))
        tables = (perm_up[section_index], perm_dn[section_index], inverse_of(perm_up[section_index]), inverse_of(perm_dn[section_index]))
        summed = tuple((jnp.zeros((D, BLK), jnp.float32) for factor_index in range(4)))
        section_out = []
        for micro_index in range(micro_count):
            pieces = []
            for block_start in range(0, token_count, block_rows):
                layer_in = acts[section_index, micro_index, block_start:block_start + block_rows]
                grad_in = carried[micro_index, block_start:block_start + block_rows]
                grad_input, terms = layer_back(layer_in, grad_in, tables, weights)
                pieces.append(grad_input)
                summed = tuple((before + addend for before, addend in zip(summed, terms)))
            section_out.append(jnp.concatenate(pieces, axis=0))
        carried = jnp.stack(section_out)
        input_list[section_index] = carried
        grad_list[section_index] = summed
    return (jnp.stack(input_list), jnp.stack([entry[0] for entry in grad_list]), jnp.stack([entry[1] for entry in grad_list]), jnp.stack([entry[2] for entry in grad_list]), jnp.stack([entry[3] for entry in grad_list]))
```

```python
import jax
import jax.numpy as jnp
from jax import lax
from jax.sharding import PartitionSpec as P

FF = 16384


epsilon = 1e-06

Z_LO, X, Y, CORE = 2, 4, 4, 2
EXTENT = {"z": Z_LO, "x": X, "y": Y, "c": CORE}
STRIDE = {"z": X * Y * CORE, "x": Y * CORE, "y": CORE, "c": 1}


def place(axis):
    return lax.rem(lax.axis_index("dp") // STRIDE[axis], EXTENT[axis])


def shifted(block, axis, distance):
    stride, extent = STRIDE[axis], EXTENT[axis]
    route = []
    for device in range(Z_LO * X * Y * CORE):
        at = device // stride % extent
        route.append((device, device + ((at + distance) % extent - at) * stride))
    return lax.ppermute(block, "dp", route)


def from_behind(block, axis, distance):
    devices = range(lax.axis_size(axis))
    route = [(i - distance, i) for i in devices if i - distance in devices]
    return lax.ppermute(block, axis, route)


def gather_ring(block, axis):
    extent = EXTENT[axis]
    here = place(axis)
    pieces = [block] + [shifted(block, axis, -d) for d in range(1, extent)]
    whole = jnp.zeros((extent,) + block.shape, block.dtype)
    for d, piece in enumerate(pieces):
        whole = lax.dynamic_update_index_in_dim(whole, piece, lax.rem(here + d, extent), 0)
    return whole


def reduce_ring(block, axis, dim, kind):
    extent = EXTENT[axis]
    here = place(axis)
    total = lax.dynamic_index_in_dim(block, here, dim, keepdims=False).astype(jnp.float32)
    for d in range(1, extent):
        piece = lax.dynamic_index_in_dim(block, lax.rem(here + d, extent), dim, keepdims=False)
        total = total + shifted(piece, axis, d).astype(jnp.float32)
    return total.astype(kind)


def gather_factors(shards_in):
    packed = jnp.stack(shards_in)
    packed = gather_ring(packed, "z")
    first, second = packed[:, :2], packed[:, 2:]
    first = gather_ring(gather_ring(first, "y"), "x")
    second = gather_ring(gather_ring(second, "x"), "y")
    both = jnp.stack([first, second.swapaxes(0, 1)])
    both = gather_ring(both, "c")
    both = both.transpose(1, 5, 4, 2, 3, 0, 6, 7)
    return both.reshape(4, -1, both.shape[-1])


def scatter_factors(totals):
    rows, width = totals[0].shape
    packed = jnp.stack([t.astype(jnp.bfloat16) for t in totals])
    packed = packed.reshape(4, Z_LO, X, Y, CORE, -1, width)
    packed = reduce_ring(packed, "c", 4, jnp.bfloat16)
    first, second = packed[:2], packed[2:]
    first = reduce_ring(reduce_ring(first, "x", 2, jnp.bfloat16), "y", 2, jnp.bfloat16)
    second = reduce_ring(reduce_ring(second, "y", 3, jnp.bfloat16), "x", 2, jnp.bfloat16)
    return reduce_ring(jnp.concatenate([first, second]), "z", 1, jnp.float32)


def contract(form, first, second):
    return jnp.einsum(form, first, second, preferred_element_type=jnp.float32)


def inverse_of(permute):
    count = permute.shape[0]
    return (
        jnp.zeros((count,), jnp.int32)
        .at[permute]
        .set(jnp.arange(count, dtype=jnp.int32), mode="promise_in_bounds", unique_indices=True)
    )


def rows_at(array, index):
    return array.at[index].get(mode="promise_in_bounds", unique_indices=True)


def forward_part(rows_in, weights, tables):
    left_first, right_first, right_second, left_second = weights
    perm_first, perm_second, inv_first, inv_second = tables
    nblock, width, _ = left_first.shape
    nhidden, narrow, _ = right_first.shape
    count = rows_in.shape[0]
    in_float = rows_in.T.astype(jnp.float32)
    scaling = lax.rsqrt(jnp.mean(in_float * in_float, axis=0, keepdims=True) + epsilon)
    normf = in_float * scaling
    normed = normf.astype(jnp.bfloat16).reshape(nblock, width, count)
    up_mid = contract("jio,jit->jot", left_first, normed).astype(jnp.bfloat16).reshape(-1, count)
    shuffled = rows_at(up_mid, perm_first).reshape(nhidden, narrow, count)
    hidden = contract("kio,kit->kot", right_first, shuffled)
    squashed = jax.nn.sigmoid(hidden)
    active = (hidden * squashed).astype(jnp.bfloat16)
    slope = (squashed * (1.0 + hidden * (1.0 - squashed))).astype(jnp.bfloat16)
    down_mid = (
        contract("kio,kot->kit", right_second, active).astype(jnp.bfloat16).reshape(-1, count)
    )
    placed = rows_at(down_mid, perm_second).reshape(nblock, width, count)
    return (scaling, normf, normed, shuffled, active, slope, placed)


def backward_part(grad_rows, scaling, normf, slope, weights, tables):
    left_first, right_first, right_second, left_second = weights
    perm_first, perm_second, inv_first, inv_second = tables
    nblock, width, _ = left_first.shape
    nhidden, narrow, _ = right_first.shape
    count = grad_rows.shape[0]
    grad_col = grad_rows.T
    grad_out = grad_col.reshape(nblock, width, count)
    grad_placed = (
        contract("jio,jot->jit", left_second, grad_out).astype(jnp.bfloat16).reshape(-1, count)
    )
    grad_down = rows_at(grad_placed, inv_second).reshape(nhidden, narrow, count)
    grad_active = contract("kio,kit->kot", right_second, grad_down).astype(jnp.bfloat16)
    grad_hidden = (grad_active.astype(jnp.float32) * slope.astype(jnp.float32)).astype(jnp.bfloat16)
    grad_shuffled = (
        contract("kio,kot->kit", right_first, grad_hidden).astype(jnp.bfloat16).reshape(-1, count)
    )
    grad_upmid = rows_at(grad_shuffled, inv_first).reshape(nblock, width, count)
    grad_norm = contract("jio,jot->jit", left_first, grad_upmid).reshape(-1, count)
    inner = jnp.mean(grad_norm * normf, axis=0, keepdims=True)
    grad_input = grad_col.astype(jnp.float32) + scaling * (grad_norm - normf * inner)
    return (grad_input.astype(jnp.bfloat16).T, grad_out, grad_down, grad_hidden, grad_upmid)


def shards(acts, cotangent, perm_up, perm_dn, left_up, right_up, right_dn, left_dn):
    gathered = gather_factors((left_up[0], right_up[0], right_dn[0], left_dn[0]))
    model_width = gathered.shape[1]
    width = gathered.shape[2]
    nblock = model_width // width
    nhidden = FF // width
    narrow = model_width // nhidden
    weights = (
        gathered[0].reshape(nblock, width, width),
        gathered[1].reshape(nhidden, narrow, width),
        gathered[2].reshape(nhidden, narrow, width),
        gathered[3].reshape(nblock, width, width),
    )
    tables = (perm_up[0], perm_dn[0], inverse_of(perm_up[0]), inverse_of(perm_dn[0]))
    section_count = lax.axis_size("section")
    section_index = lax.axis_index("section")
    final_section = section_count - 1
    micro_count = acts.shape[1]
    tok_rows = acts.shape[2]
    local_acts = acts[0]
    all_rows = micro_count * tok_rows
    scaling, normf, normed, shuffled, active, slope, placed = forward_part(
        local_acts.reshape(all_rows, model_width), weights, tables
    )
    results = jnp.zeros_like(local_acts)
    incoming = jnp.zeros_like(local_acts)

    def whole_section(operands):
        grad_all, kept = operands
        grad_input = backward_part(
            grad_all.reshape(all_rows, model_width), scaling, normf, slope, weights, tables
        )[0]
        return grad_input.reshape(micro_count, tok_rows, model_width)

    def hold_section(operands):
        return operands[1]

    for step_index in range(section_count):
        grad_all = jnp.where(section_index == final_section, cotangent, incoming)
        results = lax.cond(
            section_index == final_section - step_index,
            whole_section,
            hold_section,
            (grad_all, results),
        )
        if step_index + 1 < section_count:
            incoming = from_behind(results, "section", -1)
    grad_all = jnp.where(section_index == final_section, cotangent, incoming)
    unused, grad_out, grad_down, grad_hidden, grad_upmid = backward_part(
        grad_all.reshape(all_rows, model_width), scaling, normf, slope, weights, tables
    )
    totals = (
        contract("jit,jot->jio", normed, grad_upmid).reshape(-1, width),
        contract("kit,kot->kio", shuffled, grad_hidden).reshape(-1, width),
        contract("kit,kot->kio", grad_down, active).reshape(-1, width),
        contract("jit,jot->jio", placed, grad_out).reshape(-1, width),
    )
    owned = scatter_factors(totals)
    return (results[None], owned[0][None], owned[1][None], owned[2][None], owned[3][None])


def solution(mesh):
    return jax.shard_map(
        shards,
        mesh=mesh,
        in_specs=(
            P("section", None, "dp", None),
            P(None, "dp", None),
            P("section", None),
            P("section", None),
            P("section", "dp", None),
            P("section", "dp", None),
            P("section", "dp", None),
            P("section", "dp", None),
        ),
        out_specs=(
            P("section", None, "dp", None),
            P("section", "dp", None),
            P("section", "dp", None),
            P("section", "dp", None),
            P("section", "dp", None),
        ),
        check_vma=False,
    )
```

```python
import functools
import jax
import jax.numpy as jnp
from jax import lax
from jax.experimental import pallas as pl
from jax.experimental.pallas import tpu as pltpu
from jax.sharding import PartitionSpec as P

FF = 16384
D = 4096
W = 256
NARROW = 64
NB = 16
NH = 64
epsilon = 1e-06
BF = jnp.bfloat16
F32 = jnp.float32
ANY = pl.BlockSpec(memory_space=pl.ANY)
SMEM = pl.BlockSpec(memory_space=pltpu.SMEM)
VMEM = pl.BlockSpec(memory_space=pltpu.VMEM)
ROWS_PER_STEP = 32
PARAMS = pltpu.CompilerParams(vmem_limit_bytes=56 * 2**20)


def dot(a, b, contract):
    return lax.dot_general(a, b, ((contract[:1], contract[1:]), ((), ())), preferred_element_type=F32)


def scatter_rows(index, source, target):
    def body(step, carry):
        base = step * ROWS_PER_STEP
        for u in range(ROWS_PER_STEP):
            target[pl.ds(index[base + u], 1), :] = source[pl.ds(base + u, 1), :]
        return carry

    lax.fori_loop(0, D // ROWS_PER_STEP, body, 0)


def gather_rows(index, source, target):
    def body(step, carry):
        base = step * ROWS_PER_STEP
        for u in range(ROWS_PER_STEP):
            target[pl.ds(base + u, 1), :] = source[pl.ds(index[base + u], 1), :]
        return carry

    lax.fori_loop(0, D // ROWS_PER_STEP, body, 0)


def scale_of(x_ref):
    total = jnp.zeros((x_ref.shape[0], W), F32)
    for j in range(NB):
        x = x_ref[:, j * W:(j + 1) * W].astype(F32)
        total = total + x * x
    return lax.rsqrt(jnp.sum(total, axis=1, keepdims=True) * (1.0 / D) + epsilon)


def up_body(perm_up, x_ref, left_hbm, right_hbm, shuffled_hbm, active_hbm, slope_hbm, scale_ref,
            left, right, mixed, moved, shuffled, active, slope, sems):
    copies = [
        pltpu.make_async_copy(left_hbm, left, sems.at[0]),
        pltpu.make_async_copy(right_hbm, right, sems.at[1]),
    ]
    for c in copies:
        c.start()
    scale = scale_of(x_ref)
    scale_ref[...] = scale
    copies[0].wait()
    for j in range(NB):
        normed = (x_ref[:, j * W:(j + 1) * W].astype(F32) * scale).astype(BF)
        mixed[j * W:(j + 1) * W, :] = dot(normed, left[j * W:(j + 1) * W, :], (1, 0)).T
    gather_rows(perm_up, mixed, moved)
    copies[1].wait()

    def block(k, carry):
        rows = pl.ds(pl.multiple_of(k * NARROW, NARROW), NARROW)
        part = moved[rows, :].astype(BF)
        shuffled[rows, :] = part
        hidden = dot(part, right[rows, :], (0, 0))
        squashed = jax.nn.sigmoid(hidden)
        active[k] = (hidden * squashed).astype(BF)
        slope[k] = (squashed * (1.0 + hidden * (1.0 - squashed))).astype(BF)
        return carry

    lax.fori_loop(0, NH, block, 0, unroll=4)
    outs = [
        pltpu.make_async_copy(shuffled, shuffled_hbm, sems.at[0]),
        pltpu.make_async_copy(active, active_hbm, sems.at[1]),
        pltpu.make_async_copy(slope, slope_hbm, sems.at[2]),
    ]
    for c in outs:
        c.start()
    for c in outs:
        c.wait()


def up_call(perm_up, x, left_up, right_up):
    count = x.shape[0]
    return pl.pallas_call(
        up_body,
        name="up_projection",
        out_shape=(
            jax.ShapeDtypeStruct((D, count), BF),
            jax.ShapeDtypeStruct((NH, count, W), BF),
            jax.ShapeDtypeStruct((NH, count, W), BF),
            jax.ShapeDtypeStruct((count, 1), F32),
        ),
        in_specs=[SMEM, VMEM, ANY, ANY],
        out_specs=(ANY, ANY, ANY, VMEM),
        scratch_shapes=[
            pltpu.VMEM((D, W), BF),
            pltpu.VMEM((D, W), BF),
            pltpu.VMEM((D, count), F32),
            pltpu.VMEM((D, count), F32),
            pltpu.VMEM((D, count), BF),
            pltpu.VMEM((NH, count, W), BF),
            pltpu.VMEM((NH, count, W), BF),
            pltpu.SemaphoreType.DMA((3,)),
        ],
        compiler_params=PARAMS,
    )(perm_up, x, left_up, right_up)


def place_body(perm_dn, active, right, placed, mixed, moved):
    def block(k, carry):
        rows = pl.ds(pl.multiple_of(k * NARROW, NARROW), NARROW)
        mixed[rows, :] = dot(right[rows, :], active[k], (1, 1))
        return carry

    lax.fori_loop(0, NH, block, 0, unroll=4)
    gather_rows(perm_dn, mixed, moved)
    for j in range(NB):
        placed[j * W:(j + 1) * W, :] = moved[j * W:(j + 1) * W, :].astype(BF)


def place_call(perm_dn, active, right_dn):
    count = active.shape[1]
    return pl.pallas_call(
        place_body,
        name="placed_rows",
        out_shape=jax.ShapeDtypeStruct((D, count), BF),
        in_specs=[SMEM, VMEM, VMEM],
        out_specs=VMEM,
        scratch_shapes=[pltpu.VMEM((D, count), F32), pltpu.VMEM((D, count), F32)],
        compiler_params=PARAMS,
    )(perm_dn, active, right_dn)


def back_body(micro, flag, perm_up, perm_dn, g_hbm, acts_hbm, slope_hbm, left_up_hbm, right_up_hbm, right_dn_hbm,
              left_dn_hbm, *rest):
    (out_hbm, g_keep_hbm, gdown_hbm, ghidden_hbm, gup_hbm,
     g, x, slope, left_up, right_up, right_dn, left_dn, mixed, moved, gdown, ghidden, gup, gnorm, out, sems) = rest[-20:]
    count = g.shape[0]

    @pl.when(flag[0] == 1)
    def work():
        loads = [
            pltpu.make_async_copy(g_hbm, g, sems.at[0]),
            pltpu.make_async_copy(left_dn_hbm, left_dn, sems.at[1]),
            pltpu.make_async_copy(right_dn_hbm, right_dn, sems.at[2]),
            pltpu.make_async_copy(slope_hbm.at[:, pl.ds(micro * count, count), :], slope, sems.at[3]),
            pltpu.make_async_copy(right_up_hbm, right_up, sems.at[4]),
            pltpu.make_async_copy(left_up_hbm, left_up, sems.at[5]),
            pltpu.make_async_copy(acts_hbm.at[pl.ds(micro * count, count), :], x, sems.at[6]),
        ]
        for c in loads:
            c.start()
        loads[0].wait()
        loads[1].wait()
        for j in range(NB):
            mixed[j * W:(j + 1) * W, :] = dot(left_dn[j * W:(j + 1) * W, :], g[:, j * W:(j + 1) * W], (1, 1))
        scatter_rows(perm_dn, mixed, moved)
        loads[2].wait()
        loads[3].wait()
        loads[4].wait()

        def block(k, carry):
            rows = pl.ds(pl.multiple_of(k * NARROW, NARROW), NARROW)
            part = moved[rows, :].astype(BF)
            gdown[rows, :] = part
            gactive = dot(part, right_dn[rows, :], (0, 0)).astype(BF)
            gh = (gactive.astype(F32) * slope[k].astype(F32)).astype(BF)
            ghidden[k] = gh
            mixed[rows, :] = dot(right_up[rows, :], gh, (1, 1))
            return carry

        lax.fori_loop(0, NH, block, 0, unroll=4)
        stores = [
            pltpu.make_async_copy(g, g_keep_hbm, sems.at[7]),
            pltpu.make_async_copy(gdown, gdown_hbm, sems.at[8]),
            pltpu.make_async_copy(ghidden, ghidden_hbm, sems.at[9]),
        ]
        for c in stores:
            c.start()
        scatter_rows(perm_up, mixed, moved)
        loads[5].wait()
        loads[6].wait()
        scale = scale_of(x)
        inner = jnp.zeros((count, W), F32)
        for j in range(NB):
            cols = slice(j * W, (j + 1) * W)
            gu = moved[cols, :].T.astype(BF)
            gup[:, cols] = gu
            gn = dot(gu, left_up[cols, :], (1, 1))
            gnorm[:, cols] = gn
            inner = inner + gn * (x[:, cols].astype(F32) * scale)
        mean = jnp.sum(inner, axis=1, keepdims=True) * (1.0 / D)
        for j in range(NB):
            cols = slice(j * W, (j + 1) * W)
            normf = x[:, cols].astype(F32) * scale
            out[:, cols] = (g[:, cols].astype(F32) + scale * (gnorm[:, cols] - normf * mean)).astype(BF)
        stores += [
            pltpu.make_async_copy(out, out_hbm, sems.at[10]),
            pltpu.make_async_copy(gup, gup_hbm, sems.at[11]),
        ]
        for c in stores[3:]:
            c.start()
        for c in stores:
            c.wait()


def back_call(micro, flag, perm_up, perm_dn, g, acts, slope, weights, state):
    left_up, right_up, right_dn, left_dn = weights
    count = g.shape[0]
    out_shape = (
        jax.ShapeDtypeStruct((count, D), BF),
        jax.ShapeDtypeStruct((count, D), BF),
        jax.ShapeDtypeStruct((D, count), BF),
        jax.ShapeDtypeStruct((NH, count, W), BF),
        jax.ShapeDtypeStruct((count, D), BF),
    )
    ins = (flag, perm_up, perm_dn, g, acts, slope, left_up, right_up, right_dn, left_dn)
    return pl.pallas_call(
        functools.partial(back_body, micro),
        name="backward_step",
        out_shape=out_shape,
        in_specs=[SMEM] * 3 + [ANY] * (7 + len(state)),
        out_specs=(ANY,) * 5,
        input_output_aliases={len(ins) + i: i for i in range(len(state))},
        scratch_shapes=[
            pltpu.VMEM((count, D), BF),
            pltpu.VMEM((count, D), BF),
            pltpu.VMEM((NH, count, W), BF),
            pltpu.VMEM((D, W), BF),
            pltpu.VMEM((D, W), BF),
            pltpu.VMEM((D, W), BF),
            pltpu.VMEM((D, W), BF),
            pltpu.VMEM((D, count), F32),
            pltpu.VMEM((D, count), F32),
            pltpu.VMEM((D, count), BF),
            pltpu.VMEM((NH, count, W), BF),
            pltpu.VMEM((count, D), BF),
            pltpu.VMEM((count, D), F32),
            pltpu.VMEM((count, D), BF),
            pltpu.SemaphoreType.DMA((12,)),
        ],
        compiler_params=PARAMS,
    )(*ins, *state)


PER = W // NARROW


def grads_body(where, x, scale, shuffled, active, placed, g0, g1, gdown0, gdown1, gh0, gh1, gup0, gup1, mine, other):
    core = where[0]
    count = g0.shape[0]
    normed = (x[...].astype(F32) * scale[...]).astype(BF)
    gup = jnp.concatenate([gup0[...], gup1[...]], axis=0)
    g = jnp.concatenate([g0[...], g1[...]], axis=0)
    left_up = dot(normed, gup, (0, 0)).astype(BF)
    left_dn = dot(placed[...], g, (1, 0)).astype(BF)

    def put(factor, r, value):
        @pl.when(core == r % 2)
        def _():
            mine[factor, 0, r // 2] = value

        @pl.when(core != r % 2)
        def _():
            other[factor, 0, r // 2] = value

    for r in range(PER):
        rows = slice(r * NARROW, (r + 1) * NARROW)
        put(0, r, left_up[rows])
        put(3, r, left_dn[rows])
        gh = jnp.concatenate([gh0[r], gh1[r]], axis=0)
        put(1, r, dot(shuffled[rows, :], gh, (1, 0)).astype(BF))
        both = dot(gdown0[rows, :], active[r, :count, :], (1, 0))
        both = both + dot(gdown1[rows, :], active[r, count:, :], (1, 0))
        put(2, r, both.astype(BF))


def grads_call(core, x, scale, shuffled, active, placed, state0, state1):
    count = state0[1].shape[0]
    all_count = 2 * count
    rows = lambda n: pl.BlockSpec((W, n), lambda j, w: (j, 0))
    cols = lambda n: pl.BlockSpec((n, W), lambda j, w: (0, j))
    cube = lambda n: pl.BlockSpec((PER, n, W), lambda j, w: (j, 0, 0))
    out = pl.BlockSpec((4, 1, 2, NARROW, W), lambda j, w: (0, j, 0, 0, 0))
    shape = jax.ShapeDtypeStruct((4, NB, 2, NARROW, W), BF)
    return pl.pallas_call(
        grads_body,
        name="factor_gradients",
        grid_spec=pltpu.PrefetchScalarGridSpec(
            num_scalar_prefetch=1,
            grid=(NB,),
            in_specs=[
                cols(all_count),
                pl.BlockSpec((all_count, 1), lambda j, w: (0, 0)),
                rows(all_count),
                cube(all_count),
                rows(all_count),
                cols(count), cols(count),
                rows(count), rows(count),
                cube(count), cube(count),
                cols(count), cols(count),
            ],
            out_specs=[out, out],
        ),
        out_shape=(shape, shape),
        compiler_params=PARAMS,
    )(core.reshape(1).astype(jnp.int32), x, scale, shuffled, active, placed, state0[1], state1[1], state0[2], state1[2],
      state0[3], state1[3], state0[4], state1[4])


Z_LO, X, Y, CORE = 2, 4, 4, 2
EXTENT = {"z": Z_LO, "x": X, "y": Y, "c": CORE}
STRIDE = {"z": X * Y * CORE, "x": Y * CORE, "y": CORE, "c": 1}


def place(axis):
    return lax.rem(lax.axis_index("dp") // STRIDE[axis], EXTENT[axis])


def shifted(block, axis, distance):
    stride, extent = STRIDE[axis], EXTENT[axis]
    route = []
    for device in range(Z_LO * X * Y * CORE):
        at = device // stride % extent
        route.append((device, device + ((at + distance) % extent - at) * stride))
    return lax.ppermute(block, "dp", route)


def gather_ring(block, axis):
    extent = EXTENT[axis]
    here = place(axis)
    pieces = [block] + [shifted(block, axis, -d) for d in range(1, extent)]
    whole = jnp.zeros((extent,) + block.shape, block.dtype)
    for d, piece in enumerate(pieces):
        whole = lax.dynamic_update_index_in_dim(whole, piece, lax.rem(here + d, extent), 0)
    return whole


def reduce_ring(block, axis, dim, kind):
    extent = EXTENT[axis]
    here = place(axis)
    total = lax.dynamic_index_in_dim(block, here, dim, keepdims=False).astype(jnp.float32)
    for d in range(1, extent):
        piece = lax.dynamic_index_in_dim(block, lax.rem(here + d, extent), dim, keepdims=False)
        total = total + shifted(piece, axis, d).astype(jnp.float32)
    return total.astype(kind)


def gather_factors(shards_in):
    packed = jnp.stack(shards_in)
    packed = gather_ring(packed, "z")
    first, second = packed[:, :2], packed[:, 2:]
    first = gather_ring(gather_ring(first, "y"), "x")
    second = gather_ring(gather_ring(second, "x"), "y")
    both = jnp.stack([first, second.swapaxes(0, 1)])
    both = gather_ring(both, "c")
    both = both.transpose(1, 5, 4, 2, 3, 0, 6, 7)
    return both.reshape(4, -1, both.shape[-1])


def scatter_factors(mine, other):
    width = mine.shape[-1]
    both = mine.astype(F32) + shifted(other, "c", 1).astype(F32)
    both = both.astype(BF).reshape(4, Z_LO, X, Y, -1, width)
    first, second = both[:2], both[2:]
    first = reduce_ring(reduce_ring(first, "x", 2, BF), "y", 2, BF)
    second = reduce_ring(reduce_ring(second, "y", 3, BF), "x", 2, BF)
    return reduce_ring(jnp.concatenate([first, second]), "z", 1, F32)


def shards(acts, cotangent, perm_up, perm_dn, left_up, right_up, right_dn, left_dn):
    gathered = gather_factors((left_up[0], right_up[0], right_dn[0], left_dn[0]))
    weights = tuple(gathered[i] for i in range(4))
    perm_up, perm_dn = perm_up[0], perm_dn[0]
    section_count = lax.axis_size("section")
    section_index = lax.axis_index("section")
    final_section = section_count - 1
    micro_count, tok_rows = acts.shape[1:3]
    x = acts[0].reshape(micro_count * tok_rows, D)
    shuffled, active, slope, scale = up_call(perm_up, x, weights[0], weights[1])
    incoming = [cotangent[m] for m in range(micro_count)]
    states = [()] * micro_count
    for step in range(section_count):
        own = final_section - step
        flag = (section_index == own).astype(jnp.int32).reshape(1)
        for m in range(micro_count):
            states[m] = back_call(m, flag, perm_up, perm_dn, incoming[m], x, slope, weights, states[m])
            if own:
                incoming[m] = lax.ppermute(states[m][0], "section", [(own, own - 1)])
        if step == 0:
            late, states[-1] = lax.optimization_barrier((active, states[-1]))
            placed = place_call(perm_dn, late, weights[2])
    core = place("c")
    mine, other = grads_call(core, x, scale, shuffled, active, placed, states[0], states[1])
    owned = scatter_factors(mine, other)
    results = jnp.stack([states[m][0] for m in range(micro_count)])
    return (results[None], owned[0][None], owned[1][None], owned[2][None], owned[3][None])


def solution(mesh):
    return jax.shard_map(
        shards,
        mesh=mesh,
        in_specs=(
            P("section", None, "dp", None),
            P(None, "dp", None),
            P("section", None),
            P("section", None),
            P("section", "dp", None),
            P("section", "dp", None),
            P("section", "dp", None),
            P("section", "dp", None),
        ),
        out_specs=(
            P("section", None, "dp", None),
            P("section", "dp", None),
            P("section", "dp", None),
            P("section", "dp", None),
            P("section", "dp", None),
        ),
        check_vma=False,
    )
```

```python
import functools
import jax
import jax.numpy as jnp
from jax import lax
from jax.experimental import pallas as pl
from jax.experimental.pallas import tpu as pltpu
from jax.sharding import PartitionSpec as P

D = 4096
W = 256
NARROW = 64
NB = 16
NH = 64
GROUP = W // NARROW
CHUNK = 64
epsilon = 1e-06
BF = jnp.bfloat16
F32 = jnp.float32
ANY = pl.BlockSpec(memory_space=pl.ANY)
SMEM = pl.BlockSpec(memory_space=pltpu.SMEM)
VMEM = pl.BlockSpec(memory_space=pltpu.VMEM)
ROWS_PER_STEP = 32
PARAMS = pltpu.CompilerParams(vmem_limit_bytes=56 * 2**20)

Z_LO, X, Y, CORE = 2, 4, 4, 2
EXTENT = {"z": Z_LO, "x": X, "y": Y, "c": CORE}
STRIDE = {"z": X * Y * CORE, "x": Y * CORE, "y": CORE, "c": 1}


def place(axis):
    return lax.rem(lax.axis_index("dp") // STRIDE[axis], EXTENT[axis])


def shifted(block, axis, distance):
    stride, extent = STRIDE[axis], EXTENT[axis]
    route = []
    for device in range(Z_LO * X * Y * CORE):
        at = device // stride % extent
        route.append((device, device + ((at + distance) % extent - at) * stride))
    return lax.ppermute(block, "dp", route)


def gather_ring(block, axis):
    return jnp.stack([block] + [shifted(block, axis, -d) for d in range(1, EXTENT[axis])])


def slot_tables():
    k = jnp.arange(Z_LO * X * Y * CORE, dtype=jnp.int32)
    dz = (k // STRIDE["z"] - place("z")) % Z_LO
    dx = (k // STRIDE["x"] - place("x")) % X
    dy = (k // STRIDE["y"] - place("y")) % Y
    dc = (k - place("c")) % CORE
    return jnp.concatenate(
        [(((dc * X + dx) * Y + dy) * Z_LO + dz) * NARROW, (((dc * Y + dy) * X + dx) * Z_LO + dz) * NARROW]
    ).astype(jnp.int32)


def gather_factors(left_up, right_up, right_dn, left_dn):
    packed = gather_ring(jnp.stack([left_up, right_dn, right_up, left_dn]), "z")
    along_y = gather_ring(packed[:, :2], "y")
    along_x = gather_ring(packed[:, 2:], "x")
    left_up, right_dn = along_y[:, :, 0], along_y[:, :, 1]
    right_up, left_dn = along_x[:, :, 0], along_x[:, :, 1]
    left_up = gather_ring(left_up, "x")
    right_up = gather_ring(right_up, "y")
    left_up, right_up, right_dn, left_dn = lax.optimization_barrier((left_up, right_up, right_dn, left_dn))
    right_dn = gather_ring(right_dn, "x")
    left_dn = gather_ring(left_dn, "y")
    both = []
    for factor in (left_up, right_up, right_dn, left_dn):
        own = factor.reshape(-1, W)
        both.append((own, shifted(own, "c", 1)))
    return both


def total_of(pieces):
    total = pieces[0].astype(F32)
    for piece in pieces[1:]:
        total = total + piece.astype(F32)
    return total


def reduce_ring(pieces, axis):
    return [pieces[0]] + [shifted(pieces[d], axis, d) for d in range(1, EXTENT[axis])]


def scatter_pair(pair, order):
    arrived = [shifted(other, "c", 1) for mine, other in pair]
    rings = []
    for (mine, other), got, axes in zip(pair, arrived, order):
        pieces = [total_of([mine[d], got[d]]).astype(BF) for d in range(EXTENT[axes[0]])]
        rings.append(reduce_ring(pieces, axes[0]))
    ends = []
    for ring, axes in zip(rings, order):
        pieces = [total_of([r[d] for r in ring]).astype(BF) for d in range(EXTENT[axes[1]])]
        ends.append(reduce_ring(pieces, axes[1]))
    sums = jnp.stack([total_of(ring) for ring in ends])
    far = shifted(sums[:, 1].astype(BF), "z", 1)
    return sums[:, 0] + far.astype(F32)


def dot(a, b, contract):
    return lax.dot_general(a, b, ((contract[:1], contract[1:]), ((), ())), preferred_element_type=F32)


def gather_rows(index, source, target):
    def body(step, carry):
        base = step * ROWS_PER_STEP
        for u in range(ROWS_PER_STEP):
            target[pl.ds(base + u, 1), :] = source[pl.ds(index[base + u], 1), :]
        return carry

    lax.fori_loop(0, D // ROWS_PER_STEP, body, 0)


def scale_of(x_ref):
    total = jnp.zeros((x_ref.shape[0], W), F32)
    for j in range(NB):
        x = x_ref[:, j * W:(j + 1) * W].astype(F32)
        total = total + x * x
    return lax.rsqrt(jnp.sum(total, axis=1, keepdims=True) * (1.0 / D) + epsilon)


def rows_of(ref, start):
    return ref[pl.ds(pl.multiple_of(start, NARROW), NARROW), :]


def left_block(ref, slots, table, j):
    return jnp.concatenate([rows_of(ref, slots[table + j * GROUP + r]) for r in range(GROUP)], axis=0)


def loads_of(own, other, target, sem):
    half = D // 2
    return (
        pltpu.make_async_copy(own, target.at[pl.ds(0, half), :], sem.at[0]),
        pltpu.make_async_copy(other, target.at[pl.ds(half, half), :], sem.at[1]),
    )


def start(copies):
    for copy in copies:
        copy.start()


def wait(copies):
    for copy in copies:
        copy.wait()


Y_FIRST, X_FIRST = 0, NH


def scatter_group(index, base, source, target):
    for u in range(W):
        target[pl.ds(index[base + u], 1), :] = source[pl.ds(u, 1), :]


def gather_group(index, base, source, target):
    for u in range(W):
        target[pl.ds(u, 1), :] = source[pl.ds(index[base + u], 1), :]


def up_body(slots, perm_up, x_ref, left_own, left_other, right_own, right_other, shuffled_hbm, active_hbm, slope_hbm, scale_ref,
             left, right, mixed, even, odd, shuffled, active, slope, sems):
    load_l = loads_of(left_own, left_other, left, sems.at[pl.ds(0, 2)])
    load_r = loads_of(right_own, right_other, right, sems.at[pl.ds(2, 2)])
    start(load_l)
    start(load_r)
    scale = scale_of(x_ref)
    scale_ref[...] = scale
    wait(load_l)
    for j in range(NB):
        normed = (x_ref[:, j * W:(j + 1) * W].astype(F32) * scale).astype(BF)
        mixed[j * W:(j + 1) * W, :] = dot(normed, left_block(left, slots, Y_FIRST, j), (1, 0)).T
    wait(load_r)

    def store(source, target, q, sem):
        n = pl.ds(pl.multiple_of(q * GROUP, GROUP), GROUP)
        return pltpu.make_async_copy(source.at[n], target.at[n], sem)

    def hidden_group(q, source):
        for r in range(GROUP):
            rows = pl.ds(pl.multiple_of(q * W + r * NARROW, NARROW), NARROW)
            k = q * GROUP + r
            piece = source[r * NARROW:(r + 1) * NARROW, :].astype(BF)
            shuffled[rows, :] = piece
            hidden = dot(piece, rows_of(right, slots[X_FIRST + k]), (0, 0))
            squashed = jax.nn.sigmoid(hidden)
            active[k] = (hidden * squashed).astype(BF)
            slope[k] = (squashed * (1.0 + hidden * (1.0 - squashed))).astype(BF)
        store(active, active_hbm, q, sems.at[4]).start()
        store(slope, slope_hbm, q, sems.at[5]).start()

    def pair(p, carry):
        q = 2 * p
        gather_group(perm_up, q * W + W, mixed, odd)
        hidden_group(q, even)
        gather_group(perm_up, jnp.minimum(q + 2, NB - 1) * W, mixed, even)
        hidden_group(q + 1, odd)
        return carry

    gather_group(perm_up, 0, mixed, even)
    lax.fori_loop(0, NB // 2, pair, 0)
    last = pltpu.make_async_copy(shuffled, shuffled_hbm, sems.at[6])
    last.start()
    pltpu.make_async_copy(active, active_hbm, sems.at[4]).wait()
    pltpu.make_async_copy(slope, slope_hbm, sems.at[5]).wait()
    last.wait()


def up_call(slots, perm_up, x, left_up, right_up):
    count = x.shape[0]
    return pl.pallas_call(
        up_body,
        name="up_projection",
        out_shape=(
            jax.ShapeDtypeStruct((D, count), BF),
            jax.ShapeDtypeStruct((NH, count, W), BF),
            jax.ShapeDtypeStruct((NH, count, W), BF),
            jax.ShapeDtypeStruct((count, 1), F32),
        ),
        in_specs=[SMEM, SMEM, VMEM] + [ANY] * 4,
        out_specs=(ANY, ANY, ANY, VMEM),
        scratch_shapes=[
            pltpu.VMEM((D, W), BF),
            pltpu.VMEM((D, W), BF),
            pltpu.VMEM((D, count), F32),
            pltpu.VMEM((W, count), F32),
            pltpu.VMEM((W, count), F32),
            pltpu.VMEM((D, count), BF),
            pltpu.VMEM((NH, count, W), BF),
            pltpu.VMEM((NH, count, W), BF),
            pltpu.SemaphoreType.DMA((7,)),
        ],
        compiler_params=PARAMS,
    )(slots, perm_up, x, *left_up, *right_up)


def place_body(slots, perm_dn, active, right_own, right_other, placed, right, mixed, moved, sems):
    loads = loads_of(right_own, right_other, right, sems)
    start(loads)
    wait(loads)

    def block(q, carry):
        for r in range(8):
            rows = pl.ds(pl.multiple_of((q * 8 + r) * NARROW, NARROW), NARROW)
            mixed[rows, :] = dot(rows_of(right, slots[Y_FIRST + q * 8 + r]), active[q * 8 + r], (1, 1))
        return carry

    lax.fori_loop(0, NH // 8, block, 0)
    gather_rows(perm_dn, mixed, moved)
    for j in range(NB):
        placed[j * W:(j + 1) * W, :] = moved[j * W:(j + 1) * W, :].astype(BF)


def place_call(slots, perm_dn, active, right_dn):
    count = active.shape[1]
    return pl.pallas_call(
        place_body,
        name="placed_rows",
        out_shape=jax.ShapeDtypeStruct((D, count), BF),
        in_specs=[SMEM, SMEM, VMEM, ANY, ANY],
        out_specs=VMEM,
        scratch_shapes=[
            pltpu.VMEM((D, W), BF),
            pltpu.VMEM((D, count), F32),
            pltpu.VMEM((D, count), F32),
            pltpu.SemaphoreType.DMA((2,)),
        ],
        compiler_params=PARAMS,
    )(slots, perm_dn, active, *right_dn)


def back_body(part, parts_per, flag, slots, perm_up, perm_dn, g_hbm, acts_hbm, slope_hbm, lu_own, lu_other, ru_own, ru_other,
              rd_own, rd_other, ld_own, ld_other, *rest):
    (out_hbm, keep_hbm, ghidden_hbm,
     g, x, slope, left_up, right_up, right_dn, left_dn, even, odd, down, up, gdown, ghidden, gup, gnorm, out, sems) = rest[-20:]
    count = g.shape[0]
    tokens = pl.ds(part * count, count)

    @pl.when(flag[0] == 1)
    def work():
        load_g = pltpu.make_async_copy(g_hbm.at[pl.ds((part % parts_per) * count, count), :], g, sems.at[0])
        load_ld = loads_of(ld_own, ld_other, left_dn, sems.at[pl.ds(1, 2)])
        load_rd = loads_of(rd_own, rd_other, right_dn, sems.at[pl.ds(3, 2)])
        load_slope = pltpu.make_async_copy(slope_hbm.at[:, tokens, :], slope, sems.at[9])
        load_ru = loads_of(ru_own, ru_other, right_up, sems.at[pl.ds(5, 2)])
        load_lu = loads_of(lu_own, lu_other, left_up, sems.at[pl.ds(7, 2)])
        load_x = pltpu.make_async_copy(acts_hbm.at[tokens, :], x, sems.at[10])
        load_g.start()
        start(load_ld)
        start(load_rd)
        load_slope.start()
        start(load_ru)
        start(load_lu)
        load_x.start()
        load_g.wait()
        wait(load_ld)

        def placed_block(j, target):
            rows = pl.ds(pl.multiple_of(j * W, W), W)
            target[...] = dot(left_block(left_dn, slots, X_FIRST, j), g[:, rows], (1, 1))

        def left_pair(p, carry):
            j = 2 * p
            placed_block(j + 1, odd)
            scatter_group(perm_dn, j * W, even, down)
            placed_block(jnp.minimum(j + 2, NB - 1), even)
            scatter_group(perm_dn, j * W + W, odd, down)
            return carry

        placed_block(0, even)
        lax.fori_loop(0, NB // 2, left_pair, 0)
        wait(load_rd)
        load_slope.wait()
        wait(load_ru)

        def hidden_group(q, target):
            for r in range(GROUP):
                rows = pl.ds(pl.multiple_of(q * W + r * NARROW, NARROW), NARROW)
                k = q * GROUP + r
                piece = down[rows, :].astype(BF)
                gdown[rows, :] = piece
                gactive = dot(piece, rows_of(right_dn, slots[Y_FIRST + k]), (0, 0)).astype(BF)
                gh = (gactive.astype(F32) * slope[k].astype(F32)).astype(BF)
                ghidden[k] = gh
                target[r * NARROW:(r + 1) * NARROW, :] = dot(rows_of(right_up, slots[X_FIRST + k]), gh, (1, 1))

        def right_pair(p, carry):
            q = 2 * p
            hidden_group(q + 1, odd)
            scatter_group(perm_up, q * W, even, up)
            hidden_group(jnp.minimum(q + 2, NB - 1), even)
            scatter_group(perm_up, q * W + W, odd, up)
            return carry

        hidden_group(0, even)
        lax.fori_loop(0, NB // 2, right_pair, 0)
        store_h = pltpu.make_async_copy(ghidden, ghidden_hbm.at[:, tokens, :], sems.at[11])
        store_g = pltpu.make_async_copy(g, keep_hbm.at[0, tokens, :], sems.at[12])
        store_h.start()
        store_g.start()
        wait(load_lu)
        load_x.wait()
        scale = scale_of(x)
        inner = jnp.zeros((count, W), F32)
        for j in range(NB):
            cols = slice(j * W, (j + 1) * W)
            gu = up[cols, :].T.astype(BF)
            gup[1, :, cols] = gu
            gn = dot(gu, left_block(left_up, slots, Y_FIRST, j), (1, 1))
            gnorm[:, cols] = gn
            inner = inner + gn * (x[:, cols].astype(F32) * scale)
        mean = jnp.sum(inner, axis=1, keepdims=True) * (1.0 / D)
        for j in range(NB):
            cols = slice(j * W, (j + 1) * W)
            normf = x[:, cols].astype(F32) * scale
            out[:, cols] = (g[:, cols].astype(F32) + scale * (gnorm[:, cols] - normf * mean)).astype(BF)
        store_out = pltpu.make_async_copy(out, out_hbm, sems.at[13])
        store_out.start()
        for j in range(NB):
            cols = slice(j * W, (j + 1) * W)
            gup[0, :, cols] = gdown[cols, :].astype(F32).T.astype(BF)
        store_up = pltpu.make_async_copy(gup, keep_hbm.at[pl.ds(1, 2), tokens, :], sems.at[14])
        store_up.start()
        store_h.wait()
        store_g.wait()
        store_out.wait()
        store_up.wait()


def back_call(part, flag, slots, perm_up, perm_dn, g, acts, slope, weights, state, count):
    left_up, right_up, right_dn, left_dn = weights
    total = acts.shape[0]
    out_shape = (
        jax.ShapeDtypeStruct((count, D), BF),
        jax.ShapeDtypeStruct((3, total, D), BF),
        jax.ShapeDtypeStruct((NH, total, W), BF),
    )
    ins = (flag, slots, perm_up, perm_dn, g, acts, slope, *left_up, *right_up, *right_dn, *left_dn)
    kept = [(i, s) for i, s in enumerate(state) if s is not None]
    return pl.pallas_call(
        functools.partial(back_body, part, g.shape[0] // count),
        name="backward_step",
        out_shape=out_shape,
        in_specs=[SMEM] * 4 + [ANY] * (11 + len(kept)),
        out_specs=(ANY,) * 3,
        input_output_aliases={len(ins) + n: i for n, (i, s) in enumerate(kept)},
        scratch_shapes=[
            pltpu.VMEM((count, D), BF),
            pltpu.VMEM((count, D), BF),
            pltpu.VMEM((NH, count, W), BF),
            pltpu.VMEM((D, W), BF),
            pltpu.VMEM((D, W), BF),
            pltpu.VMEM((D, W), BF),
            pltpu.VMEM((D, W), BF),
            pltpu.VMEM((W, count), F32),
            pltpu.VMEM((W, count), F32),
            pltpu.VMEM((D, count), F32),
            pltpu.VMEM((D, count), F32),
            pltpu.VMEM((D, count), BF),
            pltpu.VMEM((NH, count, W), BF),
            pltpu.VMEM((2, count, D), BF),
            pltpu.VMEM((count, D), F32),
            pltpu.VMEM((count, D), BF),
            pltpu.SemaphoreType.DMA((15,)),
        ],
        compiler_params=PARAMS,
    )(*ins, *[s for i, s in kept])


def core_split(core, pieces):
    mine = [jnp.where(core == 0, pieces[2 * y], pieces[2 * y + 1]).astype(BF) for y in range(Y)]
    other = [jnp.where(core == 0, pieces[2 * y + 1], pieces[2 * y]).astype(BF) for y in range(Y)]
    return mine, other


def put(at, y_leads, target, pieces):
    for y in range(Y):
        d = lax.rem(y - at[2] + Y, Y)
        if y_leads:
            target[d, 0, 0] = pieces[y]
        else:
            target[0, d, 0] = pieces[y]


def pieces_of(block):
    return [block[r * NARROW:(r + 1) * NARROW] for r in range(GROUP)]


def left_grads_body(at, x, scale, placed, keep_g, keep_up, up_mine, up_other, dn_mine, dn_other):
    ups, downs = [], []
    for b in range(2):
        cols = slice(b * W, (b + 1) * W)
        normed = (x[:, cols].astype(F32) * scale[...]).astype(BF)
        ups += pieces_of(dot(normed, keep_up[0, :, cols], (0, 0)))
        downs += pieces_of(dot(placed[cols, :], keep_g[0, :, cols], (1, 0)))
    for pieces, leads, mine, other in ((ups, False, up_mine, up_other), (downs, True, dn_mine, dn_other)):
        own, rest = core_split(at[3], pieces)
        put(at, leads, mine, own)
        put(at, leads, other, rest)


def right_grads_body(at, shuffled, active, keep_down, gh, up_mine, up_other, dn_mine, dn_other):
    ups, downs = [], []
    for b in range(2):
        cols = slice(b * W, (b + 1) * W)
        gdown = keep_down[0, :, cols].astype(F32).T.astype(BF)
        for r in range(GROUP):
            rows = slice(b * W + r * NARROW, b * W + (r + 1) * NARROW)
            ups.append(dot(shuffled[rows, :], gh[b * GROUP + r], (1, 0)))
            downs.append(dot(gdown[r * NARROW:(r + 1) * NARROW, :], active[b * GROUP + r], (1, 0)))
    for pieces, leads, mine, other in ((ups, True, up_mine, up_other), (downs, False, dn_mine, dn_other)):
        own, rest = core_split(at[3], pieces)
        put(at, leads, mine, own)
        put(at, leads, other, rest)


def grads_call(body, name, at, ins, specs, y_leads):
    def out_spec(leads):
        if leads:
            return pl.BlockSpec((Y, 1, 1, NARROW, W), lambda i, w: (0, lax.rem(i % X - w[1] + X, X), lax.rem(i // X - w[0] + Z_LO, Z_LO), 0, 0))
        return pl.BlockSpec((1, Y, 1, NARROW, W), lambda i, w: (lax.rem(i % X - w[1] + X, X), 0, lax.rem(i // X - w[0] + Z_LO, Z_LO), 0, 0))

    shape = jax.ShapeDtypeStruct((X, Y, Z_LO, NARROW, W), BF)
    outs = pl.pallas_call(
        body,
        name=name,
        grid_spec=pltpu.PrefetchScalarGridSpec(
            num_scalar_prefetch=1,
            grid=(Z_LO * X,),
            in_specs=specs,
            out_specs=[out_spec(leads) for leads in y_leads for _ in range(2)],
        ),
        out_shape=(shape,) * 4,
        compiler_params=PARAMS,
    )(at, *ins)
    return (outs[0], outs[1]), (outs[2], outs[3])


def left_grads(at, x, scale, placed, keep):
    count = x.shape[0]
    specs = [
        pl.BlockSpec((count, 2 * W), lambda i, w: (0, i)),
        pl.BlockSpec((count, 1), lambda i, w: (0, 0)),
        pl.BlockSpec((2 * W, count), lambda i, w: (i, 0)),
        pl.BlockSpec((1, count, 2 * W), lambda i, w: (0, 0, i)),
        pl.BlockSpec((1, count, 2 * W), lambda i, w: (2, 0, i)),
    ]
    return grads_call(left_grads_body, "left_gradients", at, (x, scale, placed, keep, keep), specs, (False, True))


def right_grads(at, shuffled, active, keep, ghidden):
    count = keep.shape[1]
    cube = pl.BlockSpec((2 * GROUP, count, W), lambda i, w: (i, 0, 0))
    specs = [
        pl.BlockSpec((2 * W, count), lambda i, w: (i, 0)),
        cube,
        pl.BlockSpec((1, count, 2 * W), lambda i, w: (1, 0, i)),
        cube,
    ]
    return grads_call(right_grads_body, "right_gradients", at, (shuffled, active, keep, ghidden), specs, (True, False))


def shards(acts, cotangent, perm_up, perm_dn, left_up, right_up, right_dn, left_dn):
    weights = gather_factors(left_up[0], right_up[0], right_dn[0], left_dn[0])
    slots = slot_tables()
    at = jnp.stack([place(axis) for axis in ("z", "x", "y", "c")]).astype(jnp.int32)
    perm_up, perm_dn = perm_up[0], perm_dn[0]
    section_count = lax.axis_size("section")
    section_index = lax.axis_index("section")
    final_section = section_count - 1
    micro_count, tok_rows = acts.shape[1:3]
    x = acts[0].reshape(micro_count * tok_rows, D)
    parts = x.shape[0] // CHUNK
    shuffled, active, slope, scale = up_call(slots, perm_up, x, weights[0], weights[1])
    incoming = [cotangent.reshape(x.shape)] * parts
    kept = [None, None]
    sent = [None] * parts
    for step in range(section_count):
        own = final_section - step
        flag = (section_index == own).astype(jnp.int32).reshape(1)
        for m in range(parts):
            sent[m], *kept = back_call(
                m, flag, slots, perm_up, perm_dn, incoming[m], x, slope, weights, [sent[m]] + kept, CHUNK
            )
            if own:
                incoming[m] = lax.ppermute(sent[m], "section", [(own, own - 1)])
        if step == 0:
            late, kept[0] = lax.optimization_barrier((active, kept[0]))
            placed = place_call(slots, perm_dn, late, weights[2])
    lefts = left_grads(at, x, scale, placed, kept[0])
    rights = right_grads(at, shuffled, active, kept[0], kept[1])
    left_owned = scatter_pair(lefts, (("x", "y"), ("y", "x")))
    right_owned = scatter_pair(rights, (("y", "x"), ("x", "y")))
    results = jnp.concatenate(sent).reshape(acts.shape)
    return (results, left_owned[0][None], right_owned[0][None], right_owned[1][None], left_owned[1][None])


def solution(mesh):
    rows = P("section", "dp", None)
    return jax.shard_map(
        shards,
        mesh=mesh,
        in_specs=(
            P("section", None, "dp", None),
            P(None, "dp", None),
            P("section", None),
            P("section", None),
            rows,
            rows,
            rows,
            rows,
        ),
        out_specs=(P("section", None, "dp", None), rows, rows, rows, rows),
        check_vma=False,
    )
```

```python
import functools
import jax
import jax.numpy as jnp
from jax import lax
from jax.experimental import pallas as pl
from jax.experimental.pallas import tpu as pltpu
from jax.sharding import PartitionSpec as P

D = 4096
W = 256
NARROW = 64
NB = 16
NH = 64
GROUP = W // NARROW
CHUNK = 64
epsilon = 1e-06
BF = jnp.bfloat16
F32 = jnp.float32
ANY = pl.BlockSpec(memory_space=pl.ANY)
SMEM = pl.BlockSpec(memory_space=pltpu.SMEM)
VMEM = pl.BlockSpec(memory_space=pltpu.VMEM)
ROWS_PER_STEP = 8
PARAMS = pltpu.CompilerParams(vmem_limit_bytes=56 * 2**20)


def cost(microseconds):
    return pl.CostEstimate(flops=0, transcendentals=0, bytes_accessed=int(microseconds * 3.3e6))


Z_LO, X, Y, CORE = 2, 4, 4, 2
EXTENT = {"z": Z_LO, "x": X, "y": Y, "c": CORE}
STRIDE = {"z": X * Y * CORE, "x": Y * CORE, "y": CORE, "c": 1}


def place(axis):
    return lax.rem(lax.axis_index("dp") // STRIDE[axis], EXTENT[axis])


def shifted(block, axis, distance):
    stride, extent = STRIDE[axis], EXTENT[axis]
    route = []
    for device in range(Z_LO * X * Y * CORE):
        at = device // stride % extent
        route.append((device, device + ((at + distance) % extent - at) * stride))
    return lax.ppermute(block, "dp", route)


def gather_ring(block, axis):
    return jnp.stack([block] + [shifted(block, axis, -d) for d in range(1, EXTENT[axis])])


def slot_tables():
    k = jnp.arange(Z_LO * X * Y * CORE, dtype=jnp.int32)
    dz = (k // STRIDE["z"] - place("z")) % Z_LO
    dx = (k // STRIDE["x"] - place("x")) % X
    dy = (k // STRIDE["y"] - place("y")) % Y
    dc = (k - place("c")) % CORE
    return jnp.concatenate(
        [(((dc * X + dx) * Y + dy) * Z_LO + dz) * NARROW, (((dc * Y + dy) * X + dx) * Z_LO + dz) * NARROW]
    ).astype(jnp.int32)


def gather_factors(left_up, right_up, right_dn, left_dn):
    packed = jnp.concatenate([left_up, right_dn, right_up, left_dn]).reshape(4, NARROW, W)
    packed = gather_ring(packed, "z")
    along_y = gather_ring(packed[:, :2], "y")
    along_x = gather_ring(packed[:, 2:], "x")
    left_up, right_dn = along_y[:, :, 0], along_y[:, :, 1]
    right_up, left_dn = along_x[:, :, 0], along_x[:, :, 1]
    left_up = gather_ring(left_up, "x")
    right_up = gather_ring(right_up, "y")
    left_up, right_up, right_dn, left_dn = lax.optimization_barrier((left_up, right_up, right_dn, left_dn))
    right_dn = gather_ring(right_dn, "x")
    left_dn = gather_ring(left_dn, "y")
    both = []
    for factor in (left_up, right_up, right_dn, left_dn):
        own = factor.reshape(-1, W)
        both.append((own, shifted(own, "c", 1)))
    return both


def total_of(pieces):
    total = pieces[0].astype(F32)
    for piece in pieces[1:]:
        total = total + piece.astype(F32)
    return total


def reduce_ring(pieces, axis):
    return [pieces[0]] + [shifted(pieces[d], axis, d) for d in range(1, EXTENT[axis])]


def scatter_factors(groups, orders):
    arrived = [shifted(other, "c", 1) for mine, other in groups]
    rings = []
    for (mine, other), got, axes in zip(groups, arrived, orders):
        pieces = [total_of([mine[d], got[d]]).astype(BF) for d in range(EXTENT[axes[0]])]
        rings.append(reduce_ring(pieces, axes[0]))
    ends = []
    for ring, axes in zip(rings, orders):
        pieces = [total_of([r[:, d] for r in ring]).astype(BF) for d in range(EXTENT[axes[1]])]
        ends.append(reduce_ring(pieces, axes[1]))
    sums = jnp.concatenate([total_of(ring) for ring in ends])
    far = shifted(sums[:, 1].astype(BF), "z", 1)
    return sums[:, 0] + far.astype(F32)


def dot(a, b, contract):
    return lax.dot_general(a, b, ((contract[:1], contract[1:]), ((), ())), preferred_element_type=F32)


def gather_rows(index, source, target):
    def body(step, carry):
        base = step * ROWS_PER_STEP
        for u in range(ROWS_PER_STEP):
            target[pl.ds(base + u, 1), :] = source[pl.ds(index[base + u], 1), :]
        return carry

    lax.fori_loop(0, D // ROWS_PER_STEP, body, 0)


def scale_of(x_ref):
    total = jnp.zeros((x_ref.shape[0], W), F32)
    for j in range(NB):
        x = x_ref[:, j * W:(j + 1) * W].astype(F32)
        total = total + x * x
    return lax.rsqrt(jnp.sum(total, axis=1, keepdims=True) * (1.0 / D) + epsilon)


def rows_of(ref, start):
    return ref[pl.ds(pl.multiple_of(start, NARROW), NARROW), :]


def left_block(ref, slots, table, j):
    return jnp.concatenate([rows_of(ref, slots[table + j * GROUP + r]) for r in range(GROUP)], axis=0)


def loads_of(own, other, target, sem):
    half = D // 2
    return (
        pltpu.make_async_copy(own, target.at[pl.ds(0, half), :], sem.at[0]),
        pltpu.make_async_copy(other, target.at[pl.ds(half, half), :], sem.at[1]),
    )


def start(copies):
    for copy in copies:
        copy.start()


def wait(copies):
    for copy in copies:
        copy.wait()


Y_FIRST, X_FIRST = 0, NH


def scatter_group(index, base, source, target):
    for u in range(W):
        target[pl.ds(index[base + u], 1), :] = source[pl.ds(u, 1), :]


def gather_group(index, base, source, target):
    for u in range(W):
        target[pl.ds(u, 1), :] = source[pl.ds(index[base + u], 1), :]


def up_body(slots, perm_up, x_ref, left_own, left_other, right_own, right_other, shuffled_hbm, active_hbm, slope_hbm, scale_ref,
             left, right, mixed, even, odd, shuffled, active, slope, sems):
    load_l = loads_of(left_own, left_other, left, sems.at[pl.ds(0, 2)])
    load_r = loads_of(right_own, right_other, right, sems.at[pl.ds(2, 2)])
    start(load_l)
    start(load_r)
    scale = scale_of(x_ref)
    scale_ref[...] = scale
    wait(load_l)
    for j in range(NB):
        normed = (x_ref[:, j * W:(j + 1) * W].astype(F32) * scale).astype(BF)
        mixed[j * W:(j + 1) * W, :] = dot(normed, left_block(left, slots, Y_FIRST, j), (1, 0)).T
    wait(load_r)

    def store(source, target, q, sem):
        n = pl.ds(pl.multiple_of(q * GROUP, GROUP), GROUP)
        return pltpu.make_async_copy(source.at[n], target.at[n], sem)

    def hidden_group(q, source):
        for r in range(GROUP):
            rows = pl.ds(pl.multiple_of(q * W + r * NARROW, NARROW), NARROW)
            k = q * GROUP + r
            piece = source[r * NARROW:(r + 1) * NARROW, :].astype(BF)
            shuffled[rows, :] = piece
            hidden = dot(piece, rows_of(right, slots[X_FIRST + k]), (0, 0))
            squashed = jax.nn.sigmoid(hidden)
            active[k] = (hidden * squashed).astype(BF)
            slope[k] = (squashed * (1.0 + hidden * (1.0 - squashed))).astype(BF)
        store(active, active_hbm, q, sems.at[4]).start()
        store(slope, slope_hbm, q, sems.at[5]).start()

    def pair(p, carry):
        q = 2 * p
        gather_group(perm_up, q * W + W, mixed, odd)
        hidden_group(q, even)
        gather_group(perm_up, jnp.minimum(q + 2, NB - 1) * W, mixed, even)
        hidden_group(q + 1, odd)
        return carry

    gather_group(perm_up, 0, mixed, even)
    lax.fori_loop(0, NB // 2, pair, 0)
    last = pltpu.make_async_copy(shuffled, shuffled_hbm, sems.at[6])
    last.start()
    pltpu.make_async_copy(active, active_hbm, sems.at[4]).wait()
    pltpu.make_async_copy(slope, slope_hbm, sems.at[5]).wait()
    last.wait()


def up_call(slots, perm_up, x, left_up, right_up):
    count = x.shape[0]
    return pl.pallas_call(
        up_body,
        name="up_projection",
        cost_estimate=cost(12),
        out_shape=(
            jax.ShapeDtypeStruct((D, count), BF),
            jax.ShapeDtypeStruct((NH, count, W), BF),
            jax.ShapeDtypeStruct((NH, count, W), BF),
            jax.ShapeDtypeStruct((count, 1), F32),
        ),
        in_specs=[SMEM, SMEM, VMEM] + [ANY] * 4,
        out_specs=(ANY, ANY, ANY, VMEM),
        scratch_shapes=[
            pltpu.VMEM((D, W), BF),
            pltpu.VMEM((D, W), BF),
            pltpu.VMEM((D, count), F32),
            pltpu.VMEM((W, count), F32),
            pltpu.VMEM((W, count), F32),
            pltpu.VMEM((D, count), BF),
            pltpu.VMEM((NH, count, W), BF),
            pltpu.VMEM((NH, count, W), BF),
            pltpu.SemaphoreType.DMA((7,)),
        ],
        compiler_params=PARAMS,
    )(slots, perm_up, x, *left_up, *right_up)


def place_body(flag, slots, perm_dn, active_hbm, right_own, right_other, *rest):
    placed_hbm, active, right, mixed, moved, placed, sems = rest[-7:]

    @pl.when(flag[0] == 1)
    def work():
        loads = loads_of(right_own, right_other, right, sems.at[pl.ds(0, 2)])
        loads += (pltpu.make_async_copy(active_hbm, active, sems.at[2]),)
        start(loads)
        wait(loads)

        def block(q, carry):
            for r in range(8):
                k = q * 8 + r
                rows = pl.ds(pl.multiple_of(k * NARROW, NARROW), NARROW)
                mixed[rows, :] = dot(rows_of(right, slots[Y_FIRST + k]), active[k], (1, 1))
            return carry

        lax.fori_loop(0, NH // 8, block, 0)
        gather_rows(perm_dn, mixed, moved)
        for j in range(NB):
            placed[j * W:(j + 1) * W, :] = moved[j * W:(j + 1) * W, :].astype(BF)
        store = pltpu.make_async_copy(placed, placed_hbm, sems.at[0])
        store.start()
        store.wait()


def place_call(flag, slots, perm_dn, active, right_dn, after, before):
    count = active.shape[1]
    ins = (flag, slots, perm_dn, active, *right_dn, *after)
    return pl.pallas_call(
        place_body,
        name="placed_rows",
        cost_estimate=cost(12),
        out_shape=jax.ShapeDtypeStruct((D, count), BF),
        in_specs=[SMEM] * 3 + [ANY] * (len(ins) - 3 + len(before)),
        out_specs=ANY,
        input_output_aliases={len(ins): 0} if before else {},
        scratch_shapes=[
            pltpu.VMEM((NH, count, W), BF),
            pltpu.VMEM((D, W), BF),
            pltpu.VMEM((D, count), F32),
            pltpu.VMEM((D, count), F32),
            pltpu.VMEM((D, count), BF),
            pltpu.SemaphoreType.DMA((3,)),
        ],
        compiler_params=PARAMS,
    )(*ins, *before)


def back_body(part, parts_per, flag, slots, perm_up, perm_dn, g_hbm, acts_hbm, slope_hbm, lu_own, lu_other, ru_own, ru_other,
              rd_own, rd_other, ld_own, ld_other, *rest):
    (out_hbm, keep_hbm, gdown_hbm, ghidden_hbm,
     g, x, slope, left_up, right_up, right_dn, left_dn, even, odd, down, up, gdown, ghidden, gup, gnorm, out, sems) = rest[-21:]
    count = g.shape[0]
    tokens = pl.ds(part * count, count)

    @pl.when(flag[0] == 1)
    def work():
        load_g = pltpu.make_async_copy(g_hbm.at[pl.ds((part % parts_per) * count, count), :], g, sems.at[0])
        load_ld = loads_of(ld_own, ld_other, left_dn, sems.at[pl.ds(1, 2)])
        load_rd = loads_of(rd_own, rd_other, right_dn, sems.at[pl.ds(3, 2)])
        load_slope = pltpu.make_async_copy(slope_hbm.at[:, tokens, :], slope, sems.at[9])
        load_ru = loads_of(ru_own, ru_other, right_up, sems.at[pl.ds(5, 2)])
        load_lu = loads_of(lu_own, lu_other, left_up, sems.at[pl.ds(7, 2)])
        load_x = pltpu.make_async_copy(acts_hbm.at[tokens, :], x, sems.at[10])
        load_g.start()
        start(load_ld)
        start(load_rd)
        load_slope.start()
        start(load_ru)
        start(load_lu)
        load_x.start()
        load_g.wait()
        wait(load_ld)

        def placed_block(j, target):
            rows = pl.ds(pl.multiple_of(j * W, W), W)
            target[...] = dot(left_block(left_dn, slots, X_FIRST, j), g[:, rows], (1, 1))

        def left_pair(p, carry):
            j = 2 * p
            placed_block(j + 1, odd)
            scatter_group(perm_dn, j * W, even, down)
            placed_block(jnp.minimum(j + 2, NB - 1), even)
            scatter_group(perm_dn, j * W + W, odd, down)
            return carry

        placed_block(0, even)
        lax.fori_loop(0, NB // 2, left_pair, 0)
        wait(load_rd)
        load_slope.wait()
        wait(load_ru)

        def hidden_group(q, target):
            for r in range(GROUP):
                rows = pl.ds(pl.multiple_of(q * W + r * NARROW, NARROW), NARROW)
                k = q * GROUP + r
                piece = down[rows, :].astype(BF)
                gdown[rows, :] = piece
                gactive = dot(piece, rows_of(right_dn, slots[Y_FIRST + k]), (0, 0)).astype(BF)
                gh = (gactive.astype(F32) * slope[k].astype(F32)).astype(BF)
                ghidden[k] = gh
                target[r * NARROW:(r + 1) * NARROW, :] = dot(rows_of(right_up, slots[X_FIRST + k]), gh, (1, 1))

        def right_pair(p, carry):
            q = 2 * p
            hidden_group(q + 1, odd)
            scatter_group(perm_up, q * W, even, up)
            hidden_group(jnp.minimum(q + 2, NB - 1), even)
            scatter_group(perm_up, q * W + W, odd, up)
            return carry

        hidden_group(0, even)
        lax.fori_loop(0, NB // 2, right_pair, 0)
        store_h = pltpu.make_async_copy(ghidden, ghidden_hbm.at[:, tokens, :], sems.at[11])
        store_g = pltpu.make_async_copy(g, keep_hbm.at[0, tokens, :], sems.at[12])
        store_d = pltpu.make_async_copy(gdown, gdown_hbm.at[part], sems.at[0])
        store_h.start()
        store_d.start()
        store_g.start()
        wait(load_lu)
        load_x.wait()
        scale = scale_of(x)
        inner = jnp.zeros((count, W), F32)
        for j in range(NB):
            cols = slice(j * W, (j + 1) * W)
            gu = up[cols, :].T.astype(BF)
            gup[:, cols] = gu
            gn = dot(gu, left_block(left_up, slots, Y_FIRST, j), (1, 1))
            gnorm[:, cols] = gn
            inner = inner + gn * (x[:, cols].astype(F32) * scale)
        mean = jnp.sum(inner, axis=1, keepdims=True) * (1.0 / D)
        for j in range(NB):
            cols = slice(j * W, (j + 1) * W)
            normf = x[:, cols].astype(F32) * scale
            out[:, cols] = (g[:, cols].astype(F32) + scale * (gnorm[:, cols] - normf * mean)).astype(BF)
        store_out = pltpu.make_async_copy(out, out_hbm, sems.at[13])
        store_out.start()
        store_up = pltpu.make_async_copy(gup, keep_hbm.at[1, tokens, :], sems.at[14])
        store_up.start()
        store_h.wait()
        store_d.wait()
        store_g.wait()
        store_out.wait()
        store_up.wait()


def back_call(part, flag, slots, perm_up, perm_dn, g, acts, slope, weights, after, state, count):
    left_up, right_up, right_dn, left_dn = weights
    total = acts.shape[0]
    out_shape = (
        jax.ShapeDtypeStruct((count, D), BF),
        jax.ShapeDtypeStruct((2, total, D), BF),
        jax.ShapeDtypeStruct((total // count, D, count), BF),
        jax.ShapeDtypeStruct((NH, total, W), BF),
    )
    ins = (flag, slots, perm_up, perm_dn, g, acts, slope, *left_up, *right_up, *right_dn, *left_dn, *after)
    kept = [(i, s) for i, s in enumerate(state) if s is not None]
    return pl.pallas_call(
        functools.partial(back_body, part, g.shape[0] // count),
        name="backward_step",
        cost_estimate=cost(14),
        out_shape=out_shape,
        in_specs=[SMEM] * 4 + [ANY] * (len(ins) - 4 + len(kept)),
        out_specs=(ANY,) * 4,
        input_output_aliases={len(ins) + n: i for n, (i, s) in enumerate(kept)},
        scratch_shapes=[
            pltpu.VMEM((count, D), BF),
            pltpu.VMEM((count, D), BF),
            pltpu.VMEM((NH, count, W), BF),
            pltpu.VMEM((D, W), BF),
            pltpu.VMEM((D, W), BF),
            pltpu.VMEM((D, W), BF),
            pltpu.VMEM((D, W), BF),
            pltpu.VMEM((W, count), F32),
            pltpu.VMEM((W, count), F32),
            pltpu.VMEM((D, count), F32),
            pltpu.VMEM((D, count), F32),
            pltpu.VMEM((D, count), BF),
            pltpu.VMEM((NH, count, W), BF),
            pltpu.VMEM((count, D), BF),
            pltpu.VMEM((count, D), F32),
            pltpu.VMEM((count, D), BF),
            pltpu.SemaphoreType.DMA((15,)),
        ],
        compiler_params=PARAMS,
    )(*ins, *[s for i, s in kept])


def core_split(core, pieces):
    mine = [jnp.where(core == 0, pieces[2 * y], pieces[2 * y + 1]).astype(BF) for y in range(Y)]
    other = [jnp.where(core == 0, pieces[2 * y + 1], pieces[2 * y]).astype(BF) for y in range(Y)]
    return mine, other


def put(at, factor, target, other, pieces, y_leads):
    own, rest = core_split(at[3], pieces)
    for y in range(Y):
        d = lax.rem(y - at[2] + Y, Y)
        if y_leads:
            target[d, factor, 0, 0] = own[y]
            other[d, factor, 0, 0] = rest[y]
        else:
            target[0, factor, d, 0] = own[y]
            other[0, factor, d, 0] = rest[y]


def pieces_of(block):
    return [block[r * NARROW:(r + 1) * NARROW] for r in range(GROUP)]


def grads_body(at, x, scale, shuffled, active, placed, keep, keep_down, gh, x_mine, x_other, y_mine, y_other):
    left_up, left_dn, right_up, right_dn = [], [], [], []
    for b in range(2):
        cols = slice(b * W, (b + 1) * W)
        normed = (x[:, cols].astype(F32) * scale[...]).astype(BF)
        left_up += pieces_of(dot(normed, keep[1, :, cols], (0, 0)))
        left_dn += pieces_of(dot(placed[cols, :], keep[0, :, cols], (1, 0)))
        gdown = jnp.concatenate([keep_down[p, cols, :] for p in range(keep_down.shape[0])], axis=1)
        for r in range(GROUP):
            rows = slice(r * NARROW, (r + 1) * NARROW)
            right_up.append(dot(shuffled[cols, :][rows], gh[b * GROUP + r], (1, 0)))
            right_dn.append(dot(gdown[rows], active[b * GROUP + r], (1, 0)))
    put(at, 0, x_mine, x_other, left_up, False)
    put(at, 1, x_mine, x_other, right_dn, False)
    put(at, 0, y_mine, y_other, right_up, True)
    put(at, 1, y_mine, y_other, left_dn, True)


def grads_call(at, x, scale, shuffled, active, placed, keep, keep_down, ghidden):
    count = x.shape[0]
    parts, _, part = keep_down.shape
    rows = pl.BlockSpec((2 * W, count), lambda i, w: (i, 0))
    cube = pl.BlockSpec((2 * GROUP, count, W), lambda i, w: (i, 0, 0))

    def distances(i, w):
        return lax.rem(i % X - w[1] + X, X), lax.rem(i // X - w[0] + Z_LO, Z_LO)

    def x_leads(i, w):
        dx, dz = distances(i, w)
        return dx, 0, 0, dz, 0, 0

    def y_leads(i, w):
        dx, dz = distances(i, w)
        return 0, 0, dx, dz, 0, 0

    x_block = pl.BlockSpec((1, 2, Y, 1, NARROW, W), x_leads)
    y_block = pl.BlockSpec((Y, 2, 1, 1, NARROW, W), y_leads)
    shape = jax.ShapeDtypeStruct((X, 2, Y, Z_LO, NARROW, W), BF)
    outs = pl.pallas_call(
        grads_body,
        name="factor_gradients",
        cost_estimate=cost(12),
        grid_spec=pltpu.PrefetchScalarGridSpec(
            num_scalar_prefetch=1,
            grid=(Z_LO * X,),
            in_specs=[
                pl.BlockSpec((count, 2 * W), lambda i, w: (0, i)),
                pl.BlockSpec((count, 1), lambda i, w: (0, 0)),
                rows, cube, rows,
                pl.BlockSpec((2, count, 2 * W), lambda i, w: (0, 0, i)),
                pl.BlockSpec((parts, 2 * W, part), lambda i, w: (0, i, 0)),
                cube,
            ],
            out_specs=[x_block, x_block, y_block, y_block],
        ),
        out_shape=(shape,) * 4,
        compiler_params=PARAMS,
    )(at, x, scale, shuffled, active, placed, keep, keep_down, ghidden)
    return outs[:2], outs[2:]


def shards(acts, cotangent, perm_up, perm_dn, left_up, right_up, right_dn, left_dn):
    weights = gather_factors(left_up[0], right_up[0], right_dn[0], left_dn[0])
    slots = slot_tables()
    at = jnp.stack([place(axis) for axis in ("z", "x", "y", "c")]).astype(jnp.int32)
    perm_up, perm_dn = perm_up[0], perm_dn[0]
    section_count = lax.axis_size("section")
    section_index = lax.axis_index("section")
    final_section = section_count - 1
    micro_count, tok_rows = acts.shape[1:3]
    x = acts[0].reshape(micro_count * tok_rows, D)
    parts = x.shape[0] // CHUNK
    shuffled, active, slope, scale = up_call(slots, perm_up, x, weights[0], weights[1])
    incoming = [cotangent.reshape(x.shape)] * parts
    kept = [None] * 3
    sent = [None] * parts
    early = (at[:1] == 1).astype(jnp.int32)
    placed = place_call(early, slots, perm_dn, active, weights[2], (), ())
    for step in range(section_count):
        own = final_section - step
        flag = (section_index == own).astype(jnp.int32).reshape(1)
        for m in range(parts):
            after = (placed,) if m == 0 else ()
            sent[m], *kept = back_call(
                m, flag, slots, perm_up, perm_dn, incoming[m], x, slope, weights, after, [sent[m]] + kept, CHUNK
            )
            if own:
                incoming[m] = lax.ppermute(sent[m], "section", [(own, own - 1)])
        if step == 0:
            placed = place_call(1 - early, slots, perm_dn, active, weights[2], (kept[2],), (placed,))
    groups = grads_call(at, x, scale, shuffled, active, placed, *kept)
    owned = scatter_factors(groups, (("x", "y"), ("y", "x")))
    results = jnp.concatenate(sent).reshape(acts.shape)
    left_up, right_dn, right_up, left_dn = [owned[i][None] for i in range(4)]
    return (results, left_up, right_up, right_dn, left_dn)


def solution(mesh):
    rows = P("section", "dp", None)
    return jax.shard_map(
        shards,
        mesh=mesh,
        in_specs=(
            P("section", None, "dp", None),
            P(None, "dp", None),
            P("section", None),
            P("section", None),
            rows,
            rows,
            rows,
            rows,
        ),
        out_specs=(P("section", None, "dp", None), rows, rows, rows, rows),
        check_vma=False,
    )
```

```python
import functools
import jax
import jax.numpy as jnp
from jax import lax
from jax.experimental import pallas as pl
from jax.experimental.pallas import tpu as pltpu
from jax.sharding import PartitionSpec as P

D = 4096
W = 256
NARROW = 64
NB = 16
NH = 64
GROUP = W // NARROW
CHUNK = 64
epsilon = 1e-06
BF = jnp.bfloat16
F32 = jnp.float32
ANY = pl.BlockSpec(memory_space=pl.ANY)
SMEM = pl.BlockSpec(memory_space=pltpu.SMEM)
VMEM = pl.BlockSpec(memory_space=pltpu.VMEM)
ROWS_PER_STEP = 8


def room(mebibytes):
    return pltpu.CompilerParams(vmem_limit_bytes=mebibytes * 2**20)


def cost(microseconds):
    return pl.CostEstimate(flops=0, transcendentals=0, bytes_accessed=int(microseconds * 3.3e6))


Z_LO, X, Y, CORE = 2, 4, 4, 2
EXTENT = {"z": Z_LO, "x": X, "y": Y, "c": CORE}
STRIDE = {"z": X * Y * CORE, "x": Y * CORE, "y": CORE, "c": 1}


def place(axis):
    return lax.rem(lax.axis_index("dp") // STRIDE[axis], EXTENT[axis])


def shifted(block, axis, distance):
    stride, extent = STRIDE[axis], EXTENT[axis]
    route = []
    for device in range(Z_LO * X * Y * CORE):
        at = device // stride % extent
        route.append((device, device + ((at + distance) % extent - at) * stride))
    return lax.ppermute(block, "dp", route)


def gather_ring(block, axis):
    return jnp.stack([block] + [shifted(block, axis, -d) for d in range(1, EXTENT[axis])])


def slot_tables():
    k = jnp.arange(Z_LO * X * Y * CORE, dtype=jnp.int32)
    dz = (k // STRIDE["z"] - place("z")) % Z_LO
    dx = (k // STRIDE["x"] - place("x")) % X
    dy = (k // STRIDE["y"] - place("y")) % Y
    dc = (k - place("c")) % CORE
    return jnp.concatenate(
        [(((dc * X + dx) * Y + dy) * Z_LO + dz) * NARROW, (((dc * Y + dy) * X + dx) * Z_LO + dz) * NARROW]
    ).astype(jnp.int32)


def gather_rest(block, axis):
    return [block] + [shifted(block, axis, -d) for d in range(1, EXTENT[axis])]


def both_cores(own):
    return own, shifted(own, "c", 1)


def gather_factors(left_up, right_up, right_dn, left_dn):
    packed = jnp.concatenate([left_up, right_dn, right_up, left_dn]).reshape(4, NARROW, W)
    packed = gather_ring(packed, "z")
    along_y = gather_ring(packed[:, :2], "y")
    along_x = gather_ring(packed[:, 2:], "x")
    left_up, right_dn = along_y[:, :, 0], along_y[:, :, 1]
    right_up, left_dn = along_x[:, :, 0], along_x[:, :, 1]
    left_up = gather_ring(left_up, "x")
    right_up = gather_ring(right_up, "y")
    left_up, right_up, right_dn, left_dn = lax.optimization_barrier((left_up, right_up, right_dn, left_dn))
    up = [both_cores(factor.reshape(-1, W)) for factor in (left_up, right_up)]
    return up, gather_rest(right_dn, "x"), gather_rest(left_dn, "y")


def total_of(pieces):
    total = pieces[0].astype(F32)
    for piece in pieces[1:]:
        total = total + piece.astype(F32)
    return total


def reduce_ring(pieces, axis):
    return [pieces[0]] + [shifted(pieces[d], axis, d) for d in range(1, EXTENT[axis])]


def scatter_factors(groups, orders):
    arrived = [shifted(other, "c", 1) for mine, other in groups]
    rings = []
    for (mine, other), got, axes in zip(groups, arrived, orders):
        pieces = [total_of([mine[d], got[d]]).astype(BF) for d in range(EXTENT[axes[0]])]
        rings.append(reduce_ring(pieces, axes[0]))
    ends = []
    for ring, axes in zip(rings, orders):
        pieces = [total_of([r[d] for r in ring]).astype(BF) for d in range(EXTENT[axes[1]])]
        ends.append(reduce_ring(pieces, axes[1]))
    sums = jnp.concatenate([total_of(ring) for ring in ends])
    far = shifted(sums[:, 1].astype(BF), "z", 1)
    return sums[:, 0] + far.astype(F32)


def dot(a, b, contract):
    return lax.dot_general(a, b, ((contract[:1], contract[1:]), ((), ())), preferred_element_type=F32)


def gather_rows(index, source, target):
    def body(step, carry):
        base = step * ROWS_PER_STEP
        for u in range(ROWS_PER_STEP):
            target[pl.ds(base + u, 1), :] = source[pl.ds(index[base + u], 1), :]
        return carry

    lax.fori_loop(0, D // ROWS_PER_STEP, body, 0)


def scale_of(x_ref):
    total = jnp.zeros((x_ref.shape[0], W), F32)
    for j in range(NB):
        x = x_ref[:, j * W:(j + 1) * W].astype(F32)
        total = total + x * x
    return lax.rsqrt(jnp.sum(total, axis=1, keepdims=True) * (1.0 / D) + epsilon)


def rows_of(ref, start):
    return ref[pl.ds(pl.multiple_of(start, NARROW), NARROW), :]


def left_block(ref, slots, table, j):
    return jnp.concatenate([rows_of(ref, slots[table + j * GROUP + r]) for r in range(GROUP)], axis=0)


def loads_of(own, other, target, sem):
    half = D // 2
    return (
        pltpu.make_async_copy(own, target.at[pl.ds(0, half), :], sem.at[0]),
        pltpu.make_async_copy(other, target.at[pl.ds(half, half), :], sem.at[1]),
    )


def start(copies):
    for copy in copies:
        copy.start()


def wait(copies):
    for copy in copies:
        copy.wait()


Y_FIRST, X_FIRST = 0, NH


def scatter_group(index, base, source, target):
    for u in range(W):
        target[pl.ds(index[base + u], 1), :] = source[pl.ds(u, 1), :]


def gather_group(index, base, source, target):
    for u in range(W):
        target[pl.ds(u, 1), :] = source[pl.ds(index[base + u], 1), :]


def join_body(*refs):
    pieces, whole = refs[:X], refs[-1]
    rows = whole.shape[0] // X
    for d in range(X):
        whole[d * rows:(d + 1) * rows, :] = pieces[d][...]


def join_call(pieces, after):
    pieces = [piece.reshape(-1, W) for piece in pieces]
    return pl.pallas_call(
        join_body,
        name="joined_pieces",
        cost_estimate=cost(1),
        out_shape=jax.ShapeDtypeStruct((X * pieces[0].shape[0], W), BF),
        in_specs=[VMEM] * X + [ANY],
        out_specs=VMEM,
        compiler_params=room(8),
    )(*pieces, after)


def up_body(slots, perm_up, x_ref, left_own, left_other, right_own, right_other, shuffled_hbm, active_hbm, slope_hbm, scale_ref,
             left, right, mixed, even, odd, shuffled, active, slope, sems):
    load_l = loads_of(left_own, left_other, left, sems.at[pl.ds(0, 2)])
    load_r = loads_of(right_own, right_other, right, sems.at[pl.ds(2, 2)])
    start(load_l)
    start(load_r)
    scale = scale_of(x_ref)
    scale_ref[...] = scale
    wait(load_l)
    for j in range(NB):
        normed = (x_ref[:, j * W:(j + 1) * W].astype(F32) * scale).astype(BF)
        mixed[j * W:(j + 1) * W, :] = dot(normed, left_block(left, slots, Y_FIRST, j), (1, 0)).T
    wait(load_r)

    def store(source, target, q, sem):
        n = pl.ds(pl.multiple_of(q * GROUP, GROUP), GROUP)
        return pltpu.make_async_copy(source.at[n], target.at[n], sem)

    def hidden_group(q, source):
        for r in range(GROUP):
            rows = pl.ds(pl.multiple_of(q * W + r * NARROW, NARROW), NARROW)
            k = q * GROUP + r
            piece = source[r * NARROW:(r + 1) * NARROW, :].astype(BF)
            shuffled[rows, :] = piece
            hidden = dot(piece, rows_of(right, slots[X_FIRST + k]), (0, 0))
            squashed = jax.nn.sigmoid(hidden)
            active[k] = (hidden * squashed).astype(BF)
            slope[k] = (squashed * (1.0 + hidden * (1.0 - squashed))).astype(BF)
        store(active, active_hbm, q, sems.at[4]).start()
        store(slope, slope_hbm, q, sems.at[5]).start()

    def pair(p, carry):
        q = 2 * p
        gather_group(perm_up, q * W + W, mixed, odd)
        hidden_group(q, even)
        gather_group(perm_up, jnp.minimum(q + 2, NB - 1) * W, mixed, even)
        hidden_group(q + 1, odd)
        return carry

    gather_group(perm_up, 0, mixed, even)
    lax.fori_loop(0, NB // 2, pair, 0)
    last = pltpu.make_async_copy(shuffled, shuffled_hbm, sems.at[6])
    last.start()
    pltpu.make_async_copy(active, active_hbm, sems.at[4]).wait()
    pltpu.make_async_copy(slope, slope_hbm, sems.at[5]).wait()
    last.wait()


def up_call(slots, perm_up, x, left_up, right_up):
    count = x.shape[0]
    return pl.pallas_call(
        up_body,
        name="up_projection",
        cost_estimate=cost(12),
        out_shape=(
            jax.ShapeDtypeStruct((D, count), BF),
            jax.ShapeDtypeStruct((NH, count, W), BF),
            jax.ShapeDtypeStruct((NH, count, W), BF),
            jax.ShapeDtypeStruct((count, 1), F32),
        ),
        in_specs=[SMEM, SMEM, VMEM] + [ANY] * 4,
        out_specs=(ANY, ANY, ANY, VMEM),
        scratch_shapes=[
            pltpu.VMEM((D, W), BF),
            pltpu.VMEM((D, W), BF),
            pltpu.VMEM((D, count), F32),
            pltpu.VMEM((W, count), F32),
            pltpu.VMEM((W, count), F32),
            pltpu.VMEM((D, count), BF),
            pltpu.VMEM((NH, count, W), BF),
            pltpu.VMEM((NH, count, W), BF),
            pltpu.SemaphoreType.DMA((7,)),
        ],
        compiler_params=room(24),
    )(slots, perm_up, x, *left_up, *right_up)


def place_body(flag, slots, perm_dn, active_hbm, right_own, right_other, *rest):
    placed_hbm, active, right, mixed, moved, placed, sems = rest[-7:]

    @pl.when(flag[0] == 1)
    def work():
        loads = loads_of(right_own, right_other, right, sems.at[pl.ds(0, 2)])
        loads += (pltpu.make_async_copy(active_hbm, active, sems.at[2]),)
        start(loads)
        wait(loads)

        def block(q, carry):
            for r in range(8):
                k = q * 8 + r
                rows = pl.ds(pl.multiple_of(k * NARROW, NARROW), NARROW)
                mixed[rows, :] = dot(rows_of(right, slots[Y_FIRST + k]), active[k], (1, 1))
            return carry

        lax.fori_loop(0, NH // 8, block, 0)
        gather_rows(perm_dn, mixed, moved)
        for j in range(NB):
            placed[j * W:(j + 1) * W, :] = moved[j * W:(j + 1) * W, :].astype(BF)
        store = pltpu.make_async_copy(placed, placed_hbm, sems.at[0])
        store.start()
        store.wait()


def place_call(flag, slots, perm_dn, active, right_dn, after, before):
    count = active.shape[1]
    ins = (flag, slots, perm_dn, active, *right_dn, *after)
    return pl.pallas_call(
        place_body,
        name="placed_rows",
        cost_estimate=cost(12),
        out_shape=jax.ShapeDtypeStruct((D, count), BF),
        in_specs=[SMEM] * 3 + [ANY] * (len(ins) - 3 + len(before)),
        out_specs=ANY,
        input_output_aliases={len(ins): 0} if before else {},
        scratch_shapes=[
            pltpu.VMEM((NH, count, W), BF),
            pltpu.VMEM((D, W), BF),
            pltpu.VMEM((D, count), F32),
            pltpu.VMEM((D, count), F32),
            pltpu.VMEM((D, count), BF),
            pltpu.SemaphoreType.DMA((3,)),
        ],
        compiler_params=room(18),
    )(*ins, *before)


def back_body(part, parts_per, flag, slots, perm_up, perm_dn, g_hbm, acts_hbm, slope_hbm, lu_own, lu_other, ru_own, ru_other,
              rd_own, rd_other, ld_own, ld_other, *rest):
    (out_hbm, keep_hbm, gdown_hbm, ghidden_hbm,
     g, x, slope, left_up, right_up, right_dn, left_dn, even, odd, down, up, gdown, ghidden, gup, gnorm, out, sems) = rest[-21:]
    count = g.shape[0]
    tokens = pl.ds(part * count, count)

    @pl.when(flag[0] == 1)
    def work():
        load_g = pltpu.make_async_copy(g_hbm.at[pl.ds((part % parts_per) * count, count), :], g, sems.at[0])
        load_ld = loads_of(ld_own, ld_other, left_dn, sems.at[pl.ds(1, 2)])
        load_rd = loads_of(rd_own, rd_other, right_dn, sems.at[pl.ds(3, 2)])
        load_slope = pltpu.make_async_copy(slope_hbm.at[:, tokens, :], slope, sems.at[9])
        load_ru = loads_of(ru_own, ru_other, right_up, sems.at[pl.ds(5, 2)])
        load_lu = loads_of(lu_own, lu_other, left_up, sems.at[pl.ds(7, 2)])
        load_x = pltpu.make_async_copy(acts_hbm.at[tokens, :], x, sems.at[10])
        load_g.start()
        start(load_ld)
        start(load_rd)
        load_slope.start()
        start(load_ru)
        start(load_lu)
        load_x.start()
        load_g.wait()
        wait(load_ld)

        def placed_block(j, target):
            rows = pl.ds(pl.multiple_of(j * W, W), W)
            target[...] = dot(left_block(left_dn, slots, X_FIRST, j), g[:, rows], (1, 1))

        def left_pair(p, carry):
            j = 2 * p
            placed_block(j + 1, odd)
            scatter_group(perm_dn, j * W, even, down)
            placed_block(jnp.minimum(j + 2, NB - 1), even)
            scatter_group(perm_dn, j * W + W, odd, down)
            return carry

        placed_block(0, even)
        lax.fori_loop(0, NB // 2, left_pair, 0)
        wait(load_rd)
        load_slope.wait()
        wait(load_ru)

        def hidden_group(q, target):
            for r in range(GROUP):
                rows = pl.ds(pl.multiple_of(q * W + r * NARROW, NARROW), NARROW)
                k = q * GROUP + r
                piece = down[rows, :].astype(BF)
                gdown[rows, :] = piece
                gactive = dot(piece, rows_of(right_dn, slots[Y_FIRST + k]), (0, 0)).astype(BF)
                gh = (gactive.astype(F32) * slope[k].astype(F32)).astype(BF)
                ghidden[k] = gh
                target[r * NARROW:(r + 1) * NARROW, :] = dot(rows_of(right_up, slots[X_FIRST + k]), gh, (1, 1))

        def right_pair(p, carry):
            q = 2 * p
            hidden_group(q + 1, odd)
            scatter_group(perm_up, q * W, even, up)
            hidden_group(jnp.minimum(q + 2, NB - 1), even)
            scatter_group(perm_up, q * W + W, odd, up)
            return carry

        hidden_group(0, even)
        lax.fori_loop(0, NB // 2, right_pair, 0)
        store_h = pltpu.make_async_copy(ghidden, ghidden_hbm.at[:, tokens, :], sems.at[11])
        store_g = pltpu.make_async_copy(g, keep_hbm.at[0, tokens, :], sems.at[12])
        store_d = pltpu.make_async_copy(gdown, gdown_hbm.at[part], sems.at[0])
        store_h.start()
        store_d.start()
        store_g.start()
        wait(load_lu)
        load_x.wait()
        scale = scale_of(x)
        inner = jnp.zeros((count, W), F32)
        for j in range(NB):
            cols = slice(j * W, (j + 1) * W)
            gu = up[cols, :].T.astype(BF)
            gup[:, cols] = gu
            gn = dot(gu, left_block(left_up, slots, Y_FIRST, j), (1, 1))
            gnorm[:, cols] = gn
            inner = inner + gn * (x[:, cols].astype(F32) * scale)
        mean = jnp.sum(inner, axis=1, keepdims=True) * (1.0 / D)
        for j in range(NB):
            cols = slice(j * W, (j + 1) * W)
            normf = x[:, cols].astype(F32) * scale
            out[:, cols] = (g[:, cols].astype(F32) + scale * (gnorm[:, cols] - normf * mean)).astype(BF)
        store_out = pltpu.make_async_copy(out, out_hbm, sems.at[13])
        store_out.start()
        store_up = pltpu.make_async_copy(gup, keep_hbm.at[1, tokens, :], sems.at[14])
        store_up.start()
        store_h.wait()
        store_d.wait()
        store_g.wait()
        store_out.wait()
        store_up.wait()


def back_call(part, flag, slots, perm_up, perm_dn, g, acts, slope, weights, after, state, count):
    left_up, right_up, right_dn, left_dn = weights
    total = acts.shape[0]
    out_shape = (
        jax.ShapeDtypeStruct((count, D), BF),
        jax.ShapeDtypeStruct((2, total, D), BF),
        jax.ShapeDtypeStruct((total // count, D, count), BF),
        jax.ShapeDtypeStruct((NH, total, W), BF),
    )
    ins = (flag, slots, perm_up, perm_dn, g, acts, slope, *left_up, *right_up, *right_dn, *left_dn, *after)
    kept = [(i, s) for i, s in enumerate(state) if s is not None]
    return pl.pallas_call(
        functools.partial(back_body, part, g.shape[0] // count),
        name="backward_step",
        cost_estimate=cost(14),
        out_shape=out_shape,
        in_specs=[SMEM] * 4 + [ANY] * (len(ins) - 4 + len(kept)),
        out_specs=(ANY,) * 4,
        input_output_aliases={len(ins) + n: i for n, (i, s) in enumerate(kept)},
        scratch_shapes=[
            pltpu.VMEM((count, D), BF),
            pltpu.VMEM((count, D), BF),
            pltpu.VMEM((NH, count, W), BF),
            pltpu.VMEM((D, W), BF),
            pltpu.VMEM((D, W), BF),
            pltpu.VMEM((D, W), BF),
            pltpu.VMEM((D, W), BF),
            pltpu.VMEM((W, count), F32),
            pltpu.VMEM((W, count), F32),
            pltpu.VMEM((D, count), F32),
            pltpu.VMEM((D, count), F32),
            pltpu.VMEM((D, count), BF),
            pltpu.VMEM((NH, count, W), BF),
            pltpu.VMEM((count, D), BF),
            pltpu.VMEM((count, D), F32),
            pltpu.VMEM((count, D), BF),
            pltpu.SemaphoreType.DMA((15,)),
        ],
        compiler_params=room(28),
    )(*ins, *[s for i, s in kept])


def core_split(core, pieces):
    mine = [jnp.where(core == 0, pieces[2 * y], pieces[2 * y + 1]).astype(BF) for y in range(Y)]
    other = [jnp.where(core == 0, pieces[2 * y + 1], pieces[2 * y]).astype(BF) for y in range(Y)]
    return mine, other


def put(at, factor, target, other, pieces, y_leads):
    own, rest = core_split(at[3], pieces)
    for y in range(Y):
        d = lax.rem(y - at[2] + Y, Y)
        if y_leads:
            target[d, 0, factor, 0] = own[y]
            other[d, 0, factor, 0] = rest[y]
        else:
            target[0, d, factor, 0] = own[y]
            other[0, d, factor, 0] = rest[y]


def pieces_of(block):
    return [block[r * NARROW:(r + 1) * NARROW] for r in range(GROUP)]


def grads_body(at, x, scale, shuffled, active, placed, keep, keep_down, gh, x_mine, x_other, y_mine, y_other):
    left_up, left_dn, right_up, right_dn = [], [], [], []
    for b in range(2):
        cols = slice(b * W, (b + 1) * W)
        normed = (x[:, cols].astype(F32) * scale[...]).astype(BF)
        left_up += pieces_of(dot(normed, keep[1, :, cols], (0, 0)))
        left_dn += pieces_of(dot(placed[cols, :], keep[0, :, cols], (1, 0)))
        gdown = jnp.concatenate([keep_down[p, cols, :] for p in range(keep_down.shape[0])], axis=1)
        for r in range(GROUP):
            rows = slice(r * NARROW, (r + 1) * NARROW)
            right_up.append(dot(shuffled[cols, :][rows], gh[b * GROUP + r], (1, 0)))
            right_dn.append(dot(gdown[rows], active[b * GROUP + r], (1, 0)))
    put(at, 0, x_mine, x_other, left_up, False)
    put(at, 1, x_mine, x_other, right_dn, False)
    put(at, 0, y_mine, y_other, right_up, True)
    put(at, 1, y_mine, y_other, left_dn, True)


def grads_call(at, x, scale, shuffled, active, placed, keep, keep_down, ghidden):
    count = x.shape[0]
    parts, _, part = keep_down.shape
    rows = pl.BlockSpec((2 * W, count), lambda i, w: (i, 0))
    cube = pl.BlockSpec((2 * GROUP, count, W), lambda i, w: (i, 0, 0))

    def distances(i, w):
        return lax.rem(i % X - w[1] + X, X), lax.rem(i // X - w[0] + Z_LO, Z_LO)

    def x_leads(i, w):
        dx, dz = distances(i, w)
        return dx, 0, 0, dz, 0, 0

    def y_leads(i, w):
        dx, dz = distances(i, w)
        return 0, dx, 0, dz, 0, 0

    x_block = pl.BlockSpec((1, Y, 2, 1, NARROW, W), x_leads)
    y_block = pl.BlockSpec((Y, 1, 2, 1, NARROW, W), y_leads)
    shape = jax.ShapeDtypeStruct((X, Y, 2, Z_LO, NARROW, W), BF)
    outs = pl.pallas_call(
        grads_body,
        name="factor_gradients",
        cost_estimate=cost(12),
        grid_spec=pltpu.PrefetchScalarGridSpec(
            num_scalar_prefetch=1,
            grid=(Z_LO * X,),
            in_specs=[
                pl.BlockSpec((count, 2 * W), lambda i, w: (0, i)),
                pl.BlockSpec((count, 1), lambda i, w: (0, 0)),
                rows, cube, rows,
                pl.BlockSpec((2, count, 2 * W), lambda i, w: (0, 0, i)),
                pl.BlockSpec((parts, 2 * W, part), lambda i, w: (0, i, 0)),
                cube,
            ],
            out_specs=[x_block, x_block, y_block, y_block],
        ),
        out_shape=(shape,) * 4,
        compiler_params=room(24),
    )(at, x, scale, shuffled, active, placed, keep, keep_down, ghidden)
    return outs[:2], outs[2:]


def shards(acts, cotangent, perm_up, perm_dn, left_up, right_up, right_dn, left_dn):
    up_factors, right_pieces, left_pieces = gather_factors(left_up[0], right_up[0], right_dn[0], left_dn[0])
    slots = slot_tables()
    at = jnp.stack([place(axis) for axis in ("z", "x", "y", "c")]).astype(jnp.int32)
    perm_up, perm_dn = perm_up[0], perm_dn[0]
    section_count = lax.axis_size("section")
    section_index = lax.axis_index("section")
    final_section = section_count - 1
    micro_count, tok_rows = acts.shape[1:3]
    x = acts[0].reshape(micro_count * tok_rows, D)
    parts = x.shape[0] // CHUNK
    shuffled, active, slope, scale = up_call(slots, perm_up, x, *up_factors)
    right_dn = both_cores(join_call(right_pieces, scale))
    left_dn = both_cores(join_call(left_pieces, scale))
    weights = (*up_factors, right_dn, left_dn)
    incoming = [cotangent.reshape(x.shape)] * parts
    kept = [None] * 3
    sent = [None] * parts
    early = (at[:1] == 1).astype(jnp.int32)
    placed = place_call(early, slots, perm_dn, active, weights[2], (), ())
    for step in range(section_count):
        own = final_section - step
        flag = (section_index == own).astype(jnp.int32).reshape(1)
        for m in range(parts):
            after = (placed,) if m == 0 else ()
            sent[m], *kept = back_call(
                m, flag, slots, perm_up, perm_dn, incoming[m], x, slope, weights, after, [sent[m]] + kept, CHUNK
            )
            if own:
                incoming[m] = lax.ppermute(sent[m], "section", [(own, own - 1)])
        if step == 0:
            placed = place_call(1 - early, slots, perm_dn, active, weights[2], (kept[2],), (placed,))
    groups = grads_call(at, x, scale, shuffled, active, placed, *kept)
    owned = scatter_factors(groups, (("x", "y"), ("y", "x")))
    results = jnp.concatenate(sent).reshape(acts.shape)
    left_up, right_dn, right_up, left_dn = [owned[i][None] for i in range(4)]
    return (results, left_up, right_up, right_dn, left_dn)


def solution(mesh):
    rows = P("section", "dp", None)
    return jax.shard_map(
        shards,
        mesh=mesh,
        in_specs=(
            P("section", None, "dp", None),
            P(None, "dp", None),
            P("section", None),
            P("section", None),
            rows,
            rows,
            rows,
            rows,
        ),
        out_specs=(P("section", None, "dp", None), rows, rows, rows, rows),
        check_vma=False,
    )
```

```python
import functools
import jax
import jax.numpy as jnp
from jax import lax
from jax.experimental import pallas as pl
from jax.experimental.pallas import tpu as pltpu
from jax.sharding import PartitionSpec as P

D = 4096
W = 256
NARROW = 64
NB = 16
NH = 64
GROUP = W // NARROW
CHUNK = 64
epsilon = 1e-06
BF = jnp.bfloat16
F32 = jnp.float32
ANY = pl.BlockSpec(memory_space=pl.ANY)
SMEM = pl.BlockSpec(memory_space=pltpu.SMEM)
VMEM = pl.BlockSpec(memory_space=pltpu.VMEM)
ROWS_PER_STEP = 8


def in_hbm(*arrays):
    return [pltpu.with_memory_space_constraint(a, pltpu.HBM) for a in arrays]


def room(mebibytes):
    return pltpu.CompilerParams(vmem_limit_bytes=mebibytes * 2**20)


def cost(microseconds):
    return pl.CostEstimate(flops=0, transcendentals=0, bytes_accessed=int(microseconds * 3.3e6))


Z_LO, X, Y, CORE = 2, 4, 4, 2
EXTENT = {"z": Z_LO, "x": X, "y": Y, "c": CORE}
STRIDE = {"z": X * Y * CORE, "x": Y * CORE, "y": CORE, "c": 1}


def place(axis):
    return lax.rem(lax.axis_index("dp") // STRIDE[axis], EXTENT[axis])


def shifted(block, axis, distance):
    stride, extent = STRIDE[axis], EXTENT[axis]
    route = []
    for device in range(Z_LO * X * Y * CORE):
        at = device // stride % extent
        route.append((device, device + ((at + distance) % extent - at) * stride))
    return lax.ppermute(block, "dp", route)


def gather_ring(block, axis):
    return jnp.stack([block] + [shifted(block, axis, -d) for d in range(1, EXTENT[axis])])


def slot_tables():
    k = jnp.arange(Z_LO * X * Y * CORE, dtype=jnp.int32)
    dz = (k // STRIDE["z"] - place("z")) % Z_LO
    dx = (k // STRIDE["x"] - place("x")) % X
    dy = (k // STRIDE["y"] - place("y")) % Y
    dc = (k - place("c")) % CORE
    return jnp.concatenate(
        [(((dc * X + dx) * Y + dy) * Z_LO + dz) * NARROW, (((dc * Y + dy) * X + dx) * Z_LO + dz) * NARROW]
    ).astype(jnp.int32)


def gather_rest(block, axis):
    return [block] + [shifted(block, axis, -d) for d in range(1, EXTENT[axis])]


def both_cores(own):
    return own, shifted(own, "c", 1)


def gather_factors(left_up, right_up, right_dn, left_dn):
    packed = jnp.concatenate([left_up, right_dn, right_up, left_dn]).reshape(4, NARROW, W)
    packed = gather_ring(packed, "z")
    along_y = gather_ring(packed[:, :2], "y")
    along_x = gather_ring(packed[:, 2:], "x")
    left_up, right_dn = along_y[:, :, 0], along_y[:, :, 1]
    right_up, left_dn = along_x[:, :, 0], along_x[:, :, 1]
    left_up = gather_ring(left_up, "x")
    right_up = gather_ring(right_up, "y")
    left_up, right_up, right_dn, left_dn = lax.optimization_barrier((left_up, right_up, right_dn, left_dn))
    up = [both_cores(factor.reshape(-1, W)) for factor in (left_up, right_up)]
    return up, gather_rest(right_dn, "x"), gather_rest(left_dn, "y")


def total_of(pieces):
    total = pieces[0].astype(F32)
    for piece in pieces[1:]:
        total = total + piece.astype(F32)
    return total


def reduce_ring(pieces, axis):
    return [pieces[0]] + [shifted(pieces[d], axis, d) for d in range(1, EXTENT[axis])]


def scatter_factors(groups, orders):
    arrived = [shifted(other, "c", 1) for mine, other in groups]
    rings = []
    for (mine, other), got, axes in zip(groups, arrived, orders):
        pieces = [total_of([mine[d], got[d]]).astype(BF) for d in range(EXTENT[axes[0]])]
        rings.append(reduce_ring(pieces, axes[0]))
    ends = []
    for ring, axes in zip(rings, orders):
        pieces = [total_of([r[d] for r in ring]).astype(BF) for d in range(EXTENT[axes[1]])]
        ends.append(reduce_ring(pieces, axes[1]))
    sums = jnp.concatenate([total_of(ring) for ring in ends])
    far = shifted(sums[:, 1].astype(BF), "z", 1)
    return sums[:, 0] + far.astype(F32)


def dot(a, b, contract):
    return lax.dot_general(a, b, ((contract[:1], contract[1:]), ((), ())), preferred_element_type=F32)


def gather_rows(index, source, target):
    def body(step, carry):
        base = step * ROWS_PER_STEP
        for u in range(ROWS_PER_STEP):
            target[pl.ds(base + u, 1), :] = source[pl.ds(index[base + u], 1), :]
        return carry

    lax.fori_loop(0, D // ROWS_PER_STEP, body, 0)


def scale_of(x_ref):
    total = jnp.zeros((x_ref.shape[0], W), F32)
    for j in range(NB):
        x = x_ref[:, j * W:(j + 1) * W].astype(F32)
        total = total + x * x
    return lax.rsqrt(jnp.sum(total, axis=1, keepdims=True) * (1.0 / D) + epsilon)


def rows_of(ref, start):
    return ref[pl.ds(pl.multiple_of(start, NARROW), NARROW), :]


def left_block(ref, slots, table, j):
    return jnp.concatenate([rows_of(ref, slots[table + j * GROUP + r]) for r in range(GROUP)], axis=0)


def loads_of(own, other, target, sem):
    half = D // 2
    return (
        pltpu.make_async_copy(own, target.at[pl.ds(0, half), :], sem.at[0]),
        pltpu.make_async_copy(other, target.at[pl.ds(half, half), :], sem.at[1]),
    )


def start(copies):
    for copy in copies:
        copy.start()


def wait(copies):
    for copy in copies:
        copy.wait()


Y_FIRST, X_FIRST = 0, NH


def scatter_group(index, base, source, target):
    for u in range(W):
        target[pl.ds(index[base + u], 1), :] = source[pl.ds(u, 1), :]


def gather_group(index, base, source, target):
    for u in range(W):
        target[pl.ds(u, 1), :] = source[pl.ds(index[base + u], 1), :]


def join_body(*refs):
    pieces, whole = refs[:X], refs[-1]
    rows = whole.shape[0] // X
    for d in range(X):
        whole[d * rows:(d + 1) * rows, :] = pieces[d][...]


def join_call(pieces, after):
    pieces = [piece.reshape(-1, W) for piece in pieces]
    return pl.pallas_call(
        join_body,
        name="joined_pieces",
        cost_estimate=cost(1),
        out_shape=pltpu.HBM((X * pieces[0].shape[0], W), BF),
        in_specs=[VMEM] * X + [ANY],
        out_specs=VMEM,
        compiler_params=room(8),
    )(*pieces, after)


def up_body(slots, perm_up, x_ref, left_own, left_other, right_own, right_other, shuffled_hbm, active_hbm, slope_hbm, scale_ref,
             left, right, mixed, even, odd, shuffled, active, slope, sems):
    load_l = loads_of(left_own, left_other, left, sems.at[pl.ds(0, 2)])
    load_r = loads_of(right_own, right_other, right, sems.at[pl.ds(2, 2)])
    start(load_l)
    start(load_r)
    scale = scale_of(x_ref)
    scale_ref[...] = scale
    wait(load_l)
    for j in range(NB):
        normed = (x_ref[:, j * W:(j + 1) * W].astype(F32) * scale).astype(BF)
        mixed[j * W:(j + 1) * W, :] = dot(normed, left_block(left, slots, Y_FIRST, j), (1, 0)).T
    wait(load_r)

    def store(source, target, q, sem):
        n = pl.ds(pl.multiple_of(q * GROUP, GROUP), GROUP)
        return pltpu.make_async_copy(source.at[n], target.at[n], sem)

    def hidden_group(q, source):
        for r in range(GROUP):
            rows = pl.ds(pl.multiple_of(q * W + r * NARROW, NARROW), NARROW)
            k = q * GROUP + r
            piece = source[r * NARROW:(r + 1) * NARROW, :].astype(BF)
            shuffled[rows, :] = piece
            hidden = dot(piece, rows_of(right, slots[X_FIRST + k]), (0, 0))
            squashed = jax.nn.sigmoid(hidden)
            active[k] = (hidden * squashed).astype(BF)
            slope[k] = (squashed * (1.0 + hidden * (1.0 - squashed))).astype(BF)
        store(active, active_hbm, q, sems.at[4]).start()
        store(slope, slope_hbm, q, sems.at[5]).start()

    def pair(p, carry):
        q = 2 * p
        gather_group(perm_up, q * W + W, mixed, odd)
        hidden_group(q, even)
        gather_group(perm_up, jnp.minimum(q + 2, NB - 1) * W, mixed, even)
        hidden_group(q + 1, odd)
        return carry

    gather_group(perm_up, 0, mixed, even)
    lax.fori_loop(0, NB // 2, pair, 0)
    last = pltpu.make_async_copy(shuffled, shuffled_hbm, sems.at[6])
    last.start()
    pltpu.make_async_copy(active, active_hbm, sems.at[4]).wait()
    pltpu.make_async_copy(slope, slope_hbm, sems.at[5]).wait()
    last.wait()


def up_call(slots, perm_up, x, left_up, right_up):
    count = x.shape[0]
    return pl.pallas_call(
        up_body,
        name="up_projection",
        cost_estimate=cost(12),
        out_shape=(
            pltpu.HBM((D, count), BF),
            pltpu.HBM((NH, count, W), BF),
            pltpu.HBM((NH, count, W), BF),
            jax.ShapeDtypeStruct((count, 1), F32),
        ),
        in_specs=[SMEM, SMEM, VMEM] + [ANY] * 4,
        out_specs=(ANY, ANY, ANY, VMEM),
        scratch_shapes=[
            pltpu.VMEM((D, W), BF),
            pltpu.VMEM((D, W), BF),
            pltpu.VMEM((D, count), F32),
            pltpu.VMEM((W, count), F32),
            pltpu.VMEM((W, count), F32),
            pltpu.VMEM((D, count), BF),
            pltpu.VMEM((NH, count, W), BF),
            pltpu.VMEM((NH, count, W), BF),
            pltpu.SemaphoreType.DMA((7,)),
        ],
        compiler_params=room(24),
    )(slots, perm_up, x, *left_up, *right_up)


def place_body(flag, slots, perm_dn, active_hbm, right_own, right_other, *rest):
    placed_hbm, active, right, mixed, moved, placed, sems = rest[-7:]

    @pl.when(flag[0] == 1)
    def work():
        loads = loads_of(right_own, right_other, right, sems.at[pl.ds(0, 2)])
        loads += (pltpu.make_async_copy(active_hbm, active, sems.at[2]),)
        start(loads)
        wait(loads)

        def block(q, carry):
            for r in range(8):
                k = q * 8 + r
                rows = pl.ds(pl.multiple_of(k * NARROW, NARROW), NARROW)
                mixed[rows, :] = dot(rows_of(right, slots[Y_FIRST + k]), active[k], (1, 1))
            return carry

        lax.fori_loop(0, NH // 8, block, 0)
        gather_rows(perm_dn, mixed, moved)
        for j in range(NB):
            placed[j * W:(j + 1) * W, :] = moved[j * W:(j + 1) * W, :].astype(BF)
        store = pltpu.make_async_copy(placed, placed_hbm, sems.at[0])
        store.start()
        store.wait()


def place_call(flag, slots, perm_dn, active, right_dn, after, before):
    count = active.shape[1]
    ins = (flag, slots, perm_dn, *in_hbm(active), *right_dn, *in_hbm(*after))
    return pl.pallas_call(
        place_body,
        name="placed_rows",
        cost_estimate=cost(12),
        out_shape=pltpu.HBM((D, count), BF),
        in_specs=[SMEM] * 3 + [ANY] * (len(ins) - 3 + len(before)),
        out_specs=ANY,
        input_output_aliases={len(ins): 0} if before else {},
        scratch_shapes=[
            pltpu.VMEM((NH, count, W), BF),
            pltpu.VMEM((D, W), BF),
            pltpu.VMEM((D, count), F32),
            pltpu.VMEM((D, count), F32),
            pltpu.VMEM((D, count), BF),
            pltpu.SemaphoreType.DMA((3,)),
        ],
        compiler_params=room(18),
    )(*ins, *in_hbm(*before))


def back_body(part, parts_per, flag, slots, perm_up, perm_dn, g_hbm, acts_hbm, slope_hbm, lu_own, lu_other, ru_own, ru_other,
              rd_own, rd_other, ld_own, ld_other, *rest):
    (out_hbm, keep_hbm, gdown_hbm, ghidden_hbm,
     g, x, slope, left_up, right_up, right_dn, left_dn, even, odd, down, up, gdown, ghidden, gup, gnorm, out, sems) = rest[-21:]
    count = g.shape[0]
    tokens = pl.ds(part * count, count)

    @pl.when(flag[0] == 1)
    def work():
        load_g = pltpu.make_async_copy(g_hbm.at[pl.ds((part % parts_per) * count, count), :], g, sems.at[0])
        load_ld = loads_of(ld_own, ld_other, left_dn, sems.at[pl.ds(1, 2)])
        load_rd = loads_of(rd_own, rd_other, right_dn, sems.at[pl.ds(3, 2)])
        load_slope = pltpu.make_async_copy(slope_hbm.at[:, tokens, :], slope, sems.at[9])
        load_ru = loads_of(ru_own, ru_other, right_up, sems.at[pl.ds(5, 2)])
        load_lu = loads_of(lu_own, lu_other, left_up, sems.at[pl.ds(7, 2)])
        load_x = pltpu.make_async_copy(acts_hbm.at[tokens, :], x, sems.at[10])
        load_g.start()
        start(load_ld)
        start(load_rd)
        load_slope.start()
        start(load_ru)
        start(load_lu)
        load_x.start()
        load_g.wait()
        wait(load_ld)

        def placed_block(j, target):
            rows = pl.ds(pl.multiple_of(j * W, W), W)
            target[...] = dot(left_block(left_dn, slots, X_FIRST, j), g[:, rows], (1, 1))

        def left_pair(p, carry):
            j = 2 * p
            placed_block(j + 1, odd)
            scatter_group(perm_dn, j * W, even, down)
            placed_block(jnp.minimum(j + 2, NB - 1), even)
            scatter_group(perm_dn, j * W + W, odd, down)
            return carry

        placed_block(0, even)
        lax.fori_loop(0, NB // 2, left_pair, 0)
        wait(load_rd)
        load_slope.wait()
        wait(load_ru)

        def hidden_group(q, target):
            for r in range(GROUP):
                rows = pl.ds(pl.multiple_of(q * W + r * NARROW, NARROW), NARROW)
                k = q * GROUP + r
                piece = down[rows, :].astype(BF)
                gdown[rows, :] = piece
                gactive = dot(piece, rows_of(right_dn, slots[Y_FIRST + k]), (0, 0)).astype(BF)
                gh = (gactive.astype(F32) * slope[k].astype(F32)).astype(BF)
                ghidden[k] = gh
                target[r * NARROW:(r + 1) * NARROW, :] = dot(rows_of(right_up, slots[X_FIRST + k]), gh, (1, 1))

        def right_pair(p, carry):
            q = 2 * p
            hidden_group(q + 1, odd)
            scatter_group(perm_up, q * W, even, up)
            hidden_group(jnp.minimum(q + 2, NB - 1), even)
            scatter_group(perm_up, q * W + W, odd, up)
            return carry

        hidden_group(0, even)
        lax.fori_loop(0, NB // 2, right_pair, 0)
        store_h = pltpu.make_async_copy(ghidden, ghidden_hbm.at[:, tokens, :], sems.at[11])
        store_g = pltpu.make_async_copy(g, keep_hbm.at[0, tokens, :], sems.at[12])
        store_d = pltpu.make_async_copy(gdown, gdown_hbm.at[part], sems.at[0])
        store_h.start()
        store_d.start()
        store_g.start()
        wait(load_lu)
        load_x.wait()
        scale = scale_of(x)
        inner = jnp.zeros((count, W), F32)
        for j in range(NB):
            cols = slice(j * W, (j + 1) * W)
            gu = up[cols, :].T.astype(BF)
            gup[:, cols] = gu
            gn = dot(gu, left_block(left_up, slots, Y_FIRST, j), (1, 1))
            gnorm[:, cols] = gn
            inner = inner + gn * (x[:, cols].astype(F32) * scale)
        mean = jnp.sum(inner, axis=1, keepdims=True) * (1.0 / D)
        for j in range(NB):
            cols = slice(j * W, (j + 1) * W)
            normf = x[:, cols].astype(F32) * scale
            out[:, cols] = (g[:, cols].astype(F32) + scale * (gnorm[:, cols] - normf * mean)).astype(BF)
        store_out = pltpu.make_async_copy(out, out_hbm, sems.at[13])
        store_out.start()
        store_up = pltpu.make_async_copy(gup, keep_hbm.at[1, tokens, :], sems.at[14])
        store_up.start()
        store_h.wait()
        store_d.wait()
        store_g.wait()
        store_out.wait()
        store_up.wait()


def back_call(part, flag, slots, perm_up, perm_dn, g, acts, slope, weights, after, state, count):
    left_up, right_up, right_dn, left_dn = weights
    total = acts.shape[0]
    out_shape = (
        pltpu.HBM((count, D), BF),
        pltpu.HBM((2, total, D), BF),
        pltpu.HBM((total // count, D, count), BF),
        pltpu.HBM((NH, total, W), BF),
    )
    g = pltpu.with_memory_space_constraint(g, pltpu.VMEM)
    hbm = in_hbm(acts, slope, *left_up, *right_up, *right_dn, *left_dn, *after)
    ins = (flag, slots, perm_up, perm_dn, g, *hbm)
    kept = [(i, s) for i, s in enumerate(state) if s is not None]
    return pl.pallas_call(
        functools.partial(back_body, part, g.shape[0] // count),
        name="backward_step",
        cost_estimate=cost(14),
        out_shape=out_shape,
        in_specs=[SMEM] * 4 + [ANY] * (len(ins) - 4 + len(kept)),
        out_specs=(ANY,) * 4,
        input_output_aliases={len(ins) + n: i for n, (i, s) in enumerate(kept)},
        scratch_shapes=[
            pltpu.VMEM((count, D), BF),
            pltpu.VMEM((count, D), BF),
            pltpu.VMEM((NH, count, W), BF),
            pltpu.VMEM((D, W), BF),
            pltpu.VMEM((D, W), BF),
            pltpu.VMEM((D, W), BF),
            pltpu.VMEM((D, W), BF),
            pltpu.VMEM((W, count), F32),
            pltpu.VMEM((W, count), F32),
            pltpu.VMEM((D, count), F32),
            pltpu.VMEM((D, count), F32),
            pltpu.VMEM((D, count), BF),
            pltpu.VMEM((NH, count, W), BF),
            pltpu.VMEM((count, D), BF),
            pltpu.VMEM((count, D), F32),
            pltpu.VMEM((count, D), BF),
            pltpu.SemaphoreType.DMA((15,)),
        ],
        compiler_params=room(48),
    )(*ins, *in_hbm(*[s for i, s in kept]))


def core_split(core, pieces):
    mine = [jnp.where(core == 0, pieces[2 * y], pieces[2 * y + 1]).astype(BF) for y in range(Y)]
    other = [jnp.where(core == 0, pieces[2 * y + 1], pieces[2 * y]).astype(BF) for y in range(Y)]
    return mine, other


def put(at, factor, target, other, pieces, y_leads):
    own, rest = core_split(at[3], pieces)
    for y in range(Y):
        d = lax.rem(y - at[2] + Y, Y)
        if y_leads:
            target[d, 0, factor, 0] = own[y]
            other[d, 0, factor, 0] = rest[y]
        else:
            target[0, d, factor, 0] = own[y]
            other[0, d, factor, 0] = rest[y]


def pieces_of(block):
    return [block[r * NARROW:(r + 1) * NARROW] for r in range(GROUP)]


def grads_body(at, x, scale, shuffled, active, placed, keep, keep_down, gh, x_mine, x_other, y_mine, y_other):
    left_up, left_dn, right_up, right_dn = [], [], [], []
    for b in range(2):
        cols = slice(b * W, (b + 1) * W)
        normed = (x[:, cols].astype(F32) * scale[...]).astype(BF)
        left_up += pieces_of(dot(normed, keep[1, :, cols], (0, 0)))
        left_dn += pieces_of(dot(placed[cols, :], keep[0, :, cols], (1, 0)))
        gdown = jnp.concatenate([keep_down[p, cols, :] for p in range(keep_down.shape[0])], axis=1)
        for r in range(GROUP):
            rows = slice(r * NARROW, (r + 1) * NARROW)
            right_up.append(dot(shuffled[cols, :][rows], gh[b * GROUP + r], (1, 0)))
            right_dn.append(dot(gdown[rows], active[b * GROUP + r], (1, 0)))
    put(at, 0, x_mine, x_other, left_up, False)
    put(at, 1, x_mine, x_other, right_dn, False)
    put(at, 0, y_mine, y_other, right_up, True)
    put(at, 1, y_mine, y_other, left_dn, True)


def grads_call(at, x, scale, shuffled, active, placed, keep, keep_down, ghidden):
    count = x.shape[0]
    parts, _, part = keep_down.shape
    rows = pl.BlockSpec((2 * W, count), lambda i, w: (i, 0))
    cube = pl.BlockSpec((2 * GROUP, count, W), lambda i, w: (i, 0, 0))

    def distances(i, w):
        return lax.rem(i % X - w[1] + X, X), lax.rem(i // X - w[0] + Z_LO, Z_LO)

    def x_leads(i, w):
        dx, dz = distances(i, w)
        return dx, 0, 0, dz, 0, 0

    def y_leads(i, w):
        dx, dz = distances(i, w)
        return 0, dx, 0, dz, 0, 0

    x_block = pl.BlockSpec((1, Y, 2, 1, NARROW, W), x_leads)
    y_block = pl.BlockSpec((Y, 1, 2, 1, NARROW, W), y_leads)
    shape = jax.ShapeDtypeStruct((X, Y, 2, Z_LO, NARROW, W), BF)
    outs = pl.pallas_call(
        grads_body,
        name="factor_gradients",
        cost_estimate=cost(12),
        grid_spec=pltpu.PrefetchScalarGridSpec(
            num_scalar_prefetch=1,
            grid=(Z_LO * X,),
            in_specs=[
                pl.BlockSpec((count, 2 * W), lambda i, w: (0, i)),
                pl.BlockSpec((count, 1), lambda i, w: (0, 0)),
                rows, cube, rows,
                pl.BlockSpec((2, count, 2 * W), lambda i, w: (0, 0, i)),
                pl.BlockSpec((parts, 2 * W, part), lambda i, w: (0, i, 0)),
                cube,
            ],
            out_specs=[x_block, x_block, y_block, y_block],
        ),
        out_shape=(shape,) * 4,
        compiler_params=room(24),
    )(at, *in_hbm(x, scale, shuffled, active, placed, keep, keep_down, ghidden))
    return outs[:2], outs[2:]


def shards(acts, cotangent, perm_up, perm_dn, left_up, right_up, right_dn, left_dn):
    up_factors, right_pieces, left_pieces = gather_factors(left_up[0], right_up[0], right_dn[0], left_dn[0])
    slots = slot_tables()
    at = jnp.stack([place(axis) for axis in ("z", "x", "y", "c")]).astype(jnp.int32)
    perm_up, perm_dn = perm_up[0], perm_dn[0]
    section_count = lax.axis_size("section")
    section_index = lax.axis_index("section")
    final_section = section_count - 1
    micro_count, tok_rows = acts.shape[1:3]
    x = acts[0].reshape(micro_count * tok_rows, D)
    parts = x.shape[0] // CHUNK
    shuffled, active, slope, scale = up_call(slots, perm_up, x, *up_factors)
    right_dn = both_cores(join_call(right_pieces, scale))
    left_dn = both_cores(join_call(left_pieces, scale))
    weights = (*up_factors, right_dn, left_dn)
    incoming = [cotangent.reshape(x.shape)] * parts
    kept = [None] * 3
    sent = [None] * parts
    early = (at[:1] == 1).astype(jnp.int32)
    placed = place_call(early, slots, perm_dn, active, weights[2], (), ())
    for step in range(section_count):
        own = final_section - step
        flag = (section_index == own).astype(jnp.int32).reshape(1)
        for m in range(parts):
            after = (placed,) if m == 0 else ()
            sent[m], *kept = back_call(
                m, flag, slots, perm_up, perm_dn, incoming[m], x, slope, weights, after, [sent[m]] + kept, CHUNK
            )
            if own:
                incoming[m] = lax.ppermute(sent[m], "section", [(own, own - 1)])
        if step == 0:
            placed = place_call(1 - early, slots, perm_dn, active, weights[2], (kept[2],), (placed,))
    groups = grads_call(at, x, scale, shuffled, active, placed, *kept)
    owned = scatter_factors(groups, (("x", "y"), ("y", "x")))
    results = jnp.concatenate(sent).reshape(acts.shape)
    left_up, right_dn, right_up, left_dn = [owned[i][None] for i in range(4)]
    return (results, left_up, right_up, right_dn, left_dn)


def solution(mesh):
    rows = P("section", "dp", None)
    return jax.shard_map(
        shards,
        mesh=mesh,
        in_specs=(
            P("section", None, "dp", None),
            P(None, "dp", None),
            P("section", None),
            P("section", None),
            rows,
            rows,
            rows,
            rows,
        ),
        out_specs=(P("section", None, "dp", None), rows, rows, rows, rows),
        check_vma=False,
    )
```

```python
import functools
import jax
import jax.numpy as jnp
from jax import lax
from jax.experimental import pallas as pl
from jax.experimental.pallas import tpu as pltpu
from jax.sharding import PartitionSpec as P

D = 4096
W = 256
NARROW = 64
NB = 16
NH = 64
GROUP = W // NARROW
CHUNK = 64
epsilon = 1e-06
BF = jnp.bfloat16
F32 = jnp.float32
ANY = pl.BlockSpec(memory_space=pl.ANY)
SMEM = pl.BlockSpec(memory_space=pltpu.SMEM)
VMEM = pl.BlockSpec(memory_space=pltpu.VMEM)
ROWS_PER_STEP = 4


def in_hbm(*arrays):
    return [pltpu.with_memory_space_constraint(a, pltpu.HBM) for a in arrays]


def room(mebibytes):
    return pltpu.CompilerParams(vmem_limit_bytes=mebibytes * 2**20)


def cost(microseconds):
    return pl.CostEstimate(flops=0, transcendentals=0, bytes_accessed=int(microseconds * 3.3e6))


Z_LO, X, Y, CORE = 2, 4, 4, 2
EXTENT = {"z": Z_LO, "x": X, "y": Y, "c": CORE}
STRIDE = {"z": X * Y * CORE, "x": Y * CORE, "y": CORE, "c": 1}


def place(axis):
    return lax.rem(lax.axis_index("dp") // STRIDE[axis], EXTENT[axis])


def shifted(block, axis, distance):
    stride, extent = STRIDE[axis], EXTENT[axis]
    route = []
    for device in range(Z_LO * X * Y * CORE):
        at = device // stride % extent
        route.append((device, device + ((at + distance) % extent - at) * stride))
    return lax.ppermute(block, "dp", route)


def gather_ring(block, axis):
    return jnp.stack([block] + [shifted(block, axis, -d) for d in range(1, EXTENT[axis])])


def slot_tables():
    k = jnp.arange(Z_LO * X * Y * CORE, dtype=jnp.int32)
    dz = (k // STRIDE["z"] - place("z")) % Z_LO
    dx = (k // STRIDE["x"] - place("x")) % X
    dy = (k // STRIDE["y"] - place("y")) % Y
    dc = (k - place("c")) % CORE
    return jnp.concatenate(
        [((dc * X + dx) * Y + dy) * Z_LO + dz, ((dc * Y + dy) * X + dx) * Z_LO + dz]
    ).astype(jnp.int32)


def both_cores(own):
    return own, shifted(own, "c", 1)


def gather_factors(left_up, right_up, right_dn, left_dn):
    packed = jnp.concatenate([left_up, right_up, right_dn, left_dn]).reshape(4, NARROW, W)
    packed = gather_ring(packed, "z")
    up = gather_ring(packed[:, :2], "y")
    down = gather_ring(packed[:, 2:], "x")
    up = gather_ring(up, "x").reshape(-1, 2, NARROW, W)
    down = gather_ring(down, "y").reshape(-1, 2, NARROW, W)
    return both_cores(up), both_cores(down)


def total_of(pieces):
    total = pieces[0].astype(F32)
    for piece in pieces[1:]:
        total = total + piece.astype(F32)
    return total


def reduce_ring(pieces, axis):
    return [pieces[0]] + [shifted(pieces[d], axis, d) for d in range(1, EXTENT[axis])]


def scatter_factors(groups, orders):
    arrived = [shifted(other, "c", 1) for mine, other in groups]
    rings = []
    for (mine, other), got, axes in zip(groups, arrived, orders):
        pieces = [total_of([mine[d], got[d]]).astype(BF) for d in range(EXTENT[axes[0]])]
        rings.append(reduce_ring(pieces, axes[0]))
    ends = []
    for ring, axes in zip(rings, orders):
        pieces = [total_of([r[d] for r in ring]).astype(BF) for d in range(EXTENT[axes[1]])]
        ends.append(reduce_ring(pieces, axes[1]))
    sums = jnp.concatenate([total_of(ring) for ring in ends])
    far = shifted(sums[:, 1].astype(BF), "z", 1)
    return sums[:, 0] + far.astype(F32)


def dot(a, b, contract):
    return lax.dot_general(a, b, ((contract[:1], contract[1:]), ((), ())), preferred_element_type=F32)


def gather_rows(index, source, target):
    def body(step, carry):
        base = step * ROWS_PER_STEP
        for u in range(ROWS_PER_STEP):
            target[pl.ds(base + u, 1), :] = source[pl.ds(index[base + u], 1), :]
        return carry

    lax.fori_loop(0, D // ROWS_PER_STEP, body, 0)


def scale_of(x_ref):
    total = jnp.zeros((x_ref.shape[0], W), F32)
    for j in range(NB):
        x = x_ref[:, j * W:(j + 1) * W].astype(F32)
        total = total + x * x
    return lax.rsqrt(jnp.sum(total, axis=1, keepdims=True) * (1.0 / D) + epsilon)


def left_block(ref, slots, table, j):
    return jnp.concatenate([ref[slots[table + j * GROUP + r]] for r in range(GROUP)], axis=0)


def loads_of(own, other, which, target, sem):
    half = own.shape[0]
    return (
        pltpu.make_async_copy(own.at[:, which], target.at[pl.ds(0, half)], sem.at[0]),
        pltpu.make_async_copy(other.at[:, which], target.at[pl.ds(half, half)], sem.at[1]),
    )


def start(copies):
    for copy in copies:
        copy.start()


def wait(copies):
    for copy in copies:
        copy.wait()


UP, DOWN = 0, NH


def scatter_group(index, base, source, target):
    for u in range(W):
        target[pl.ds(index[base + u], 1), :] = source[pl.ds(u, 1), :]


def gather_group(index, base, source, target):
    for u in range(W):
        target[pl.ds(u, 1), :] = source[pl.ds(index[base + u], 1), :]


def up_body(slots, perm_up, x_ref, own, other, shuffled_hbm, active_hbm, slope_hbm, scale_ref,
             left, right, mixed, even, odd, shuffled, active, slope, sems):
    load_l = loads_of(own, other, 0, left, sems.at[pl.ds(0, 2)])
    load_r = loads_of(own, other, 1, right, sems.at[pl.ds(2, 2)])
    start(load_l)
    start(load_r)
    scale = scale_of(x_ref)
    scale_ref[...] = scale
    wait(load_l)
    for j in range(NB):
        normed = (x_ref[:, j * W:(j + 1) * W].astype(F32) * scale).astype(BF)
        mixed[j * W:(j + 1) * W, :] = dot(normed, left_block(left, slots, UP, j), (1, 0)).T
    wait(load_r)

    def store(source, target, q, sem):
        n = pl.ds(pl.multiple_of(q * GROUP, GROUP), GROUP)
        return pltpu.make_async_copy(source.at[n], target.at[n], sem)

    def hidden_group(q, source):
        for r in range(GROUP):
            rows = pl.ds(pl.multiple_of(q * W + r * NARROW, NARROW), NARROW)
            k = q * GROUP + r
            piece = source[r * NARROW:(r + 1) * NARROW, :].astype(BF)
            shuffled[rows, :] = piece
            hidden = dot(piece, right[slots[UP + k]], (0, 0))
            squashed = jax.nn.sigmoid(hidden)
            active[k] = (hidden * squashed).astype(BF)
            slope[k] = (squashed * (1.0 + hidden * (1.0 - squashed))).astype(BF)
        store(active, active_hbm, q, sems.at[4]).start()
        store(slope, slope_hbm, q, sems.at[5]).start()

    def pair(p, carry):
        q = 2 * p
        gather_group(perm_up, q * W + W, mixed, odd)
        hidden_group(q, even)
        gather_group(perm_up, jnp.minimum(q + 2, NB - 1) * W, mixed, even)
        hidden_group(q + 1, odd)
        return carry

    gather_group(perm_up, 0, mixed, even)
    lax.fori_loop(0, NB // 2, pair, 0)
    last = pltpu.make_async_copy(shuffled, shuffled_hbm, sems.at[6])
    last.start()
    pltpu.make_async_copy(active, active_hbm, sems.at[4]).wait()
    pltpu.make_async_copy(slope, slope_hbm, sems.at[5]).wait()
    last.wait()


def up_call(slots, perm_up, x, up):
    count = x.shape[0]
    return pl.pallas_call(
        up_body,
        name="up_projection",
        cost_estimate=cost(12),
        out_shape=(
            pltpu.HBM((D, count), BF),
            pltpu.HBM((NH, count, W), BF),
            pltpu.HBM((NH, count, W), BF),
            jax.ShapeDtypeStruct((count, 1), F32),
        ),
        in_specs=[SMEM, SMEM, VMEM] + [ANY] * 2,
        out_specs=(ANY, ANY, ANY, VMEM),
        scratch_shapes=[
            pltpu.VMEM((NH, NARROW, W), BF),
            pltpu.VMEM((NH, NARROW, W), BF),
            pltpu.VMEM((D, count), F32),
            pltpu.VMEM((W, count), F32),
            pltpu.VMEM((W, count), F32),
            pltpu.VMEM((D, count), BF),
            pltpu.VMEM((NH, count, W), BF),
            pltpu.VMEM((NH, count, W), BF),
            pltpu.SemaphoreType.DMA((7,)),
        ],
        compiler_params=room(24),
    )(slots, perm_up, x, *in_hbm(*up))


def place_body(flag, slots, perm_dn, active_hbm, own, other, *rest):
    placed_hbm, active, right, mixed, moved, placed, sems = rest[-7:]

    @pl.when(flag[0] == 1)
    def work():
        loads = loads_of(own, other, 0, right, sems.at[pl.ds(0, 2)])
        loads += (pltpu.make_async_copy(active_hbm, active, sems.at[2]),)
        start(loads)
        wait(loads)

        def block(q, carry):
            for r in range(8):
                k = q * 8 + r
                rows = pl.ds(pl.multiple_of(k * NARROW, NARROW), NARROW)
                mixed[rows, :] = dot(right[slots[DOWN + k]], active[k], (1, 1))
            return carry

        lax.fori_loop(0, NH // 8, block, 0)
        gather_rows(perm_dn, mixed, moved)
        for j in range(NB):
            placed[j * W:(j + 1) * W, :] = moved[j * W:(j + 1) * W, :].astype(BF)
        store = pltpu.make_async_copy(placed, placed_hbm, sems.at[0])
        store.start()
        store.wait()


def place_call(flag, slots, perm_dn, active, down, after, before):
    count = active.shape[1]
    ins = (flag, slots, perm_dn, *in_hbm(active, *down, *after))
    return pl.pallas_call(
        place_body,
        name="placed_rows",
        cost_estimate=cost(12),
        out_shape=pltpu.HBM((D, count), BF),
        in_specs=[SMEM] * 3 + [ANY] * (len(ins) - 3 + len(before)),
        out_specs=ANY,
        input_output_aliases={len(ins): 0} if before else {},
        scratch_shapes=[
            pltpu.VMEM((NH, count, W), BF),
            pltpu.VMEM((NH, NARROW, W), BF),
            pltpu.VMEM((D, count), F32),
            pltpu.VMEM((D, count), F32),
            pltpu.VMEM((D, count), BF),
            pltpu.SemaphoreType.DMA((3,)),
        ],
        compiler_params=room(18),
    )(*ins, *in_hbm(*before))


def back_body(part, parts_per, flag, slots, perm_up, perm_dn, g_hbm, acts_hbm, slope_hbm, up_own, up_other,
              down_own, down_other, *rest):
    (out_hbm, keep_hbm, gdown_hbm, ghidden_hbm,
     g, x, slope, left_up, right_up, right_dn, left_dn, even, odd, down, up, gdown, ghidden, gup, gnorm, out, sems) = rest[-21:]
    count = g.shape[0]
    tokens = pl.ds(part * count, count)

    @pl.when(flag[0] == 1)
    def work():
        load_g = pltpu.make_async_copy(g_hbm.at[pl.ds((part % parts_per) * count, count), :], g, sems.at[0])
        load_ld = loads_of(down_own, down_other, 1, left_dn, sems.at[pl.ds(1, 2)])
        load_rd = loads_of(down_own, down_other, 0, right_dn, sems.at[pl.ds(3, 2)])
        load_slope = pltpu.make_async_copy(slope_hbm.at[:, tokens, :], slope, sems.at[9])
        load_ru = loads_of(up_own, up_other, 1, right_up, sems.at[pl.ds(5, 2)])
        load_lu = loads_of(up_own, up_other, 0, left_up, sems.at[pl.ds(7, 2)])
        load_x = pltpu.make_async_copy(acts_hbm.at[tokens, :], x, sems.at[10])
        load_g.start()
        start(load_ld)
        start(load_rd)
        load_slope.start()
        start(load_ru)
        start(load_lu)
        load_x.start()
        load_g.wait()
        wait(load_ld)

        def placed_block(j, target):
            rows = pl.ds(pl.multiple_of(j * W, W), W)
            target[...] = dot(left_block(left_dn, slots, DOWN, j), g[:, rows], (1, 1))

        def left_pair(p, carry):
            j = 2 * p
            placed_block(j + 1, odd)
            scatter_group(perm_dn, j * W, even, down)
            placed_block(jnp.minimum(j + 2, NB - 1), even)
            scatter_group(perm_dn, j * W + W, odd, down)
            return carry

        placed_block(0, even)
        lax.fori_loop(0, NB // 2, left_pair, 0)
        wait(load_rd)
        load_slope.wait()
        wait(load_ru)

        def hidden_group(q, target):
            for r in range(GROUP):
                rows = pl.ds(pl.multiple_of(q * W + r * NARROW, NARROW), NARROW)
                k = q * GROUP + r
                piece = down[rows, :].astype(BF)
                gdown[rows, :] = piece
                gactive = dot(piece, right_dn[slots[DOWN + k]], (0, 0)).astype(BF)
                gh = (gactive.astype(F32) * slope[k].astype(F32)).astype(BF)
                ghidden[k] = gh
                target[r * NARROW:(r + 1) * NARROW, :] = dot(right_up[slots[UP + k]], gh, (1, 1))

        def right_pair(p, carry):
            q = 2 * p
            hidden_group(q + 1, odd)
            scatter_group(perm_up, q * W, even, up)
            hidden_group(jnp.minimum(q + 2, NB - 1), even)
            scatter_group(perm_up, q * W + W, odd, up)
            return carry

        hidden_group(0, even)
        lax.fori_loop(0, NB // 2, right_pair, 0)
        store_h = pltpu.make_async_copy(ghidden, ghidden_hbm.at[:, tokens, :], sems.at[11])
        store_g = pltpu.make_async_copy(g, keep_hbm.at[0, tokens, :], sems.at[12])
        store_d = pltpu.make_async_copy(gdown, gdown_hbm.at[part], sems.at[0])
        store_h.start()
        store_d.start()
        store_g.start()
        wait(load_lu)
        load_x.wait()
        scale = scale_of(x)
        inner = jnp.zeros((count, W), F32)
        for j in range(NB):
            cols = slice(j * W, (j + 1) * W)
            gu = up[cols, :].T.astype(BF)
            gup[:, cols] = gu
            gn = dot(gu, left_block(left_up, slots, UP, j), (1, 1))
            gnorm[:, cols] = gn
            inner = inner + gn * (x[:, cols].astype(F32) * scale)
        mean = jnp.sum(inner, axis=1, keepdims=True) * (1.0 / D)
        for j in range(NB):
            cols = slice(j * W, (j + 1) * W)
            normf = x[:, cols].astype(F32) * scale
            out[:, cols] = (g[:, cols].astype(F32) + scale * (gnorm[:, cols] - normf * mean)).astype(BF)
        store_out = pltpu.make_async_copy(out, out_hbm, sems.at[13])
        store_out.start()
        store_up = pltpu.make_async_copy(gup, keep_hbm.at[1, tokens, :], sems.at[14])
        store_up.start()
        store_h.wait()
        store_d.wait()
        store_g.wait()
        store_out.wait()
        store_up.wait()


def back_call(part, flag, slots, perm_up, perm_dn, g, acts, slope, weights, after, state, count):
    up, down = weights
    total = acts.shape[0]
    out_shape = (
        pltpu.HBM((count, D), BF),
        pltpu.HBM((2, total, D), BF),
        pltpu.HBM((total // count, D, count), BF),
        pltpu.HBM((NH, total, W), BF),
    )
    g = pltpu.with_memory_space_constraint(g, pltpu.VMEM)
    hbm = in_hbm(acts, slope, *up, *down, *after)
    ins = (flag, slots, perm_up, perm_dn, g, *hbm)
    kept = [(i, s) for i, s in enumerate(state) if s is not None]
    return pl.pallas_call(
        functools.partial(back_body, part, g.shape[0] // count),
        name="backward_step",
        cost_estimate=cost(14),
        out_shape=out_shape,
        in_specs=[SMEM] * 4 + [ANY] * (len(ins) - 4 + len(kept)),
        out_specs=(ANY,) * 4,
        input_output_aliases={len(ins) + n: i for n, (i, s) in enumerate(kept)},
        scratch_shapes=[
            pltpu.VMEM((count, D), BF),
            pltpu.VMEM((count, D), BF),
            pltpu.VMEM((NH, count, W), BF),
            pltpu.VMEM((NH, NARROW, W), BF),
            pltpu.VMEM((NH, NARROW, W), BF),
            pltpu.VMEM((NH, NARROW, W), BF),
            pltpu.VMEM((NH, NARROW, W), BF),
            pltpu.VMEM((W, count), F32),
            pltpu.VMEM((W, count), F32),
            pltpu.VMEM((D, count), F32),
            pltpu.VMEM((D, count), F32),
            pltpu.VMEM((D, count), BF),
            pltpu.VMEM((NH, count, W), BF),
            pltpu.VMEM((count, D), BF),
            pltpu.VMEM((count, D), F32),
            pltpu.VMEM((count, D), BF),
            pltpu.SemaphoreType.DMA((15,)),
        ],
        compiler_params=room(48),
    )(*ins, *in_hbm(*[s for i, s in kept]))


def core_split(core, pieces):
    mine = [jnp.where(core == 0, pieces[2 * y], pieces[2 * y + 1]).astype(BF) for y in range(Y)]
    other = [jnp.where(core == 0, pieces[2 * y + 1], pieces[2 * y]).astype(BF) for y in range(Y)]
    return mine, other


def put(at, factor, target, other, pieces, y_leads):
    own, rest = core_split(at[3], pieces)
    for y in range(Y):
        d = lax.rem(y - at[2] + Y, Y)
        if y_leads:
            target[d, 0, factor, 0] = own[y]
            other[d, 0, factor, 0] = rest[y]
        else:
            target[0, d, factor, 0] = own[y]
            other[0, d, factor, 0] = rest[y]


def pieces_of(block):
    return [block[r * NARROW:(r + 1) * NARROW] for r in range(GROUP)]


def grads_body(at, x, scale, shuffled, active, placed, keep, keep_down, gh, x_mine, x_other, y_mine, y_other):
    left_up, left_dn, right_up, right_dn = [], [], [], []
    for b in range(2):
        cols = slice(b * W, (b + 1) * W)
        normed = (x[:, cols].astype(F32) * scale[...]).astype(BF)
        left_up += pieces_of(dot(normed, keep[1, :, cols], (0, 0)))
        left_dn += pieces_of(dot(placed[cols, :], keep[0, :, cols], (1, 0)))
        gdown = jnp.concatenate([keep_down[p, cols, :] for p in range(keep_down.shape[0])], axis=1)
        for r in range(GROUP):
            rows = slice(r * NARROW, (r + 1) * NARROW)
            right_up.append(dot(shuffled[cols, :][rows], gh[b * GROUP + r], (1, 0)))
            right_dn.append(dot(gdown[rows], active[b * GROUP + r], (1, 0)))
    put(at, 0, x_mine, x_other, left_up, False)
    put(at, 1, x_mine, x_other, right_dn, False)
    put(at, 0, y_mine, y_other, right_up, True)
    put(at, 1, y_mine, y_other, left_dn, True)


def grads_call(at, x, scale, shuffled, active, placed, keep, keep_down, ghidden):
    count = x.shape[0]
    parts, _, part = keep_down.shape
    rows = pl.BlockSpec((2 * W, count), lambda i, w: (i, 0))
    cube = pl.BlockSpec((2 * GROUP, count, W), lambda i, w: (i, 0, 0))

    def distances(i, w):
        return lax.rem(i % X - w[1] + X, X), lax.rem(i // X - w[0] + Z_LO, Z_LO)

    def x_leads(i, w):
        dx, dz = distances(i, w)
        return dx, 0, 0, dz, 0, 0

    def y_leads(i, w):
        dx, dz = distances(i, w)
        return 0, dx, 0, dz, 0, 0

    x_block = pl.BlockSpec((1, Y, 2, 1, NARROW, W), x_leads)
    y_block = pl.BlockSpec((Y, 1, 2, 1, NARROW, W), y_leads)
    shape = jax.ShapeDtypeStruct((X, Y, 2, Z_LO, NARROW, W), BF)
    outs = pl.pallas_call(
        grads_body,
        name="factor_gradients",
        cost_estimate=cost(12),
        grid_spec=pltpu.PrefetchScalarGridSpec(
            num_scalar_prefetch=1,
            grid=(Z_LO * X,),
            in_specs=[
                pl.BlockSpec((count, 2 * W), lambda i, w: (0, i)),
                pl.BlockSpec((count, 1), lambda i, w: (0, 0)),
                rows, cube, rows,
                pl.BlockSpec((2, count, 2 * W), lambda i, w: (0, 0, i)),
                pl.BlockSpec((parts, 2 * W, part), lambda i, w: (0, i, 0)),
                cube,
            ],
            out_specs=[x_block, x_block, y_block, y_block],
        ),
        out_shape=(shape,) * 4,
        compiler_params=room(24),
    )(at, *in_hbm(x, scale, shuffled, active, placed, keep, keep_down, ghidden))
    return outs[:2], outs[2:]


def shards(acts, cotangent, perm_up, perm_dn, left_up, right_up, right_dn, left_dn):
    weights = gather_factors(left_up[0], right_up[0], right_dn[0], left_dn[0])
    slots = slot_tables()
    at = jnp.stack([place(axis) for axis in ("z", "x", "y", "c")]).astype(jnp.int32)
    perm_up, perm_dn = perm_up[0], perm_dn[0]
    section_count = lax.axis_size("section")
    section_index = lax.axis_index("section")
    final_section = section_count - 1
    micro_count, tok_rows = acts.shape[1:3]
    x = acts[0].reshape(micro_count * tok_rows, D)
    parts = x.shape[0] // CHUNK
    shuffled, active, slope, scale = up_call(slots, perm_up, x, weights[0])
    incoming = [cotangent.reshape(x.shape)] * parts
    kept = [None] * 3
    sent = [None] * parts
    early = (at[:1] == 1).astype(jnp.int32)
    placed = place_call(early, slots, perm_dn, active, weights[1], (), ())
    for step in range(section_count):
        own = final_section - step
        flag = (section_index == own).astype(jnp.int32).reshape(1)
        for m in range(parts):
            after = (placed,) if m == 0 else ()
            sent[m], *kept = back_call(
                m, flag, slots, perm_up, perm_dn, incoming[m], x, slope, weights, after, [sent[m]] + kept, CHUNK
            )
            if own:
                incoming[m] = lax.ppermute(sent[m], "section", [(own, own - 1)])
        if step == 0:
            placed = place_call(1 - early, slots, perm_dn, active, weights[1], (kept[2],), (placed,))
    groups = grads_call(at, x, scale, shuffled, active, placed, *kept)
    owned = scatter_factors(groups, (("x", "y"), ("y", "x")))
    results = jnp.concatenate(sent).reshape(acts.shape)
    left_up, right_dn, right_up, left_dn = [owned[i][None] for i in range(4)]
    return (results, left_up, right_up, right_dn, left_dn)


def solution(mesh):
    rows = P("section", "dp", None)
    return jax.shard_map(
        shards,
        mesh=mesh,
        in_specs=(
            P("section", None, "dp", None),
            P(None, "dp", None),
            P("section", None),
            P("section", None),
            rows,
            rows,
            rows,
            rows,
        ),
        out_specs=(P("section", None, "dp", None), rows, rows, rows, rows),
        check_vma=False,
    )
```

```python
import functools
import jax
import jax.numpy as jnp
from jax import lax
from jax.experimental import pallas as pl
from jax.experimental.pallas import tpu as pltpu
from jax.sharding import PartitionSpec as P

D = 4096
W = 256
NARROW = 64
NB = 16
NH = 64
GROUP = W // NARROW
CHUNK = 64
epsilon = 1e-06
BF = jnp.bfloat16
F32 = jnp.float32
ANY = pl.BlockSpec(memory_space=pl.ANY)
SMEM = pl.BlockSpec(memory_space=pltpu.SMEM)
VMEM = pl.BlockSpec(memory_space=pltpu.VMEM)
ROWS_PER_STEP = 4


def in_hbm(*arrays):
    return [pltpu.with_memory_space_constraint(a, pltpu.HBM) for a in arrays]


def room(mebibytes):
    return pltpu.CompilerParams(vmem_limit_bytes=mebibytes * 2**20)


def cost(microseconds):
    return pl.CostEstimate(flops=0, transcendentals=0, bytes_accessed=int(microseconds * 3.3e6))


Z_LO, X, Y, CORE = 2, 4, 4, 2
EXTENT = {"z": Z_LO, "x": X, "y": Y, "c": CORE}
STRIDE = {"z": X * Y * CORE, "x": Y * CORE, "y": CORE, "c": 1}


def place(axis):
    return lax.rem(lax.axis_index("dp") // STRIDE[axis], EXTENT[axis])


def shifted(block, axes, distance):
    route = []
    for device in range(Z_LO * X * Y * CORE):
        axis = axes if isinstance(axes, str) else axes[device % CORE]
        stride, extent = STRIDE[axis], EXTENT[axis]
        at = device // stride % extent
        route.append((device, device + ((at + distance) % extent - at) * stride))
    return lax.ppermute(block, "dp", route)


def gather_ring(block, axes, extent):
    return jnp.stack([block] + [shifted(block, axes, -d) for d in range(1, extent)])


def slot_table():
    k = jnp.arange(Z_LO * X * Y * CORE, dtype=jnp.int32)
    dz = (k // STRIDE["z"] - place("z")) % Z_LO
    dx = (k // STRIDE["x"] - place("x")) % X
    dy = (k // STRIDE["y"] - place("y")) % Y
    dc = (k - place("c")) % CORE
    ring = jnp.where(k % CORE == 0, dx * Y + dy, dy * X + dx)
    return ((dc * X * Y + ring) * Z_LO + dz).astype(jnp.int32)


def both_cores(own):
    return own, shifted(own, "c", 1)


def gather_factors(left_up, right_up, right_dn, left_dn):
    packed = jnp.concatenate([left_up, right_up, right_dn, left_dn]).reshape(4, NARROW, W)
    packed = gather_ring(gather_ring(packed, "z", Z_LO), ("y", "x"), X)
    up, down = lax.optimization_barrier((packed[:, :, :2], packed[:, :, 2:]))
    up = gather_ring(up, ("x", "y"), X)
    up, down = lax.optimization_barrier((up, down))
    down = [down] + [shifted(down, ("x", "y"), -d) for d in range(1, X)]
    return both_cores(up.reshape(-1, 2, NARROW, W)), down


def total_of(pieces):
    total = pieces[0].astype(F32)
    for piece in pieces[1:]:
        total = total + piece.astype(F32)
    return total


def reduce_ring(pieces, axes):
    return [pieces[0]] + [shifted(pieces[d], axes, d) for d in range(1, X)]


def scatter_factors(mine, other):
    got = shifted(other, "c", 1)
    ring = reduce_ring([total_of([mine[d], got[d]]).astype(BF) for d in range(X)], ("x", "y"))
    ring = reduce_ring([total_of([piece[d] for piece in ring]).astype(BF) for d in range(X)], ("y", "x"))
    sums = total_of(ring)
    far = shifted(sums[:, 1].astype(BF), "z", 1)
    return sums[:, 0] + far.astype(F32)


def dot(a, b, contract):
    return lax.dot_general(a, b, ((contract[:1], contract[1:]), ((), ())), preferred_element_type=F32)


def gather_rows(index, source, target):
    def body(step, carry):
        base = step * ROWS_PER_STEP
        for u in range(ROWS_PER_STEP):
            target[pl.ds(base + u, 1), :] = source[pl.ds(index[base + u], 1), :]
        return carry

    lax.fori_loop(0, D // ROWS_PER_STEP, body, 0)


def scale_of(x_ref):
    total = jnp.zeros((x_ref.shape[0], W), F32)
    for j in range(NB):
        x = x_ref[:, j * W:(j + 1) * W].astype(F32)
        total = total + x * x
    return lax.rsqrt(jnp.sum(total, axis=1, keepdims=True) * (1.0 / D) + epsilon)


def left_block(ref, slots, j):
    return jnp.concatenate([ref[slots[j * GROUP + r]] for r in range(GROUP)], axis=0)


def loads_of(own, other, which, target, sem):
    half = own.shape[0]
    return (
        pltpu.make_async_copy(own.at[:, which], target.at[pl.ds(0, half)], sem.at[0]),
        pltpu.make_async_copy(other.at[:, which], target.at[pl.ds(half, half)], sem.at[1]),
    )


def start(copies):
    for copy in copies:
        copy.start()


def wait(copies):
    for copy in copies:
        copy.wait()


def scatter_group(index, base, source, target):
    for u in range(W):
        target[pl.ds(index[base + u], 1), :] = source[pl.ds(u, 1), :]


def gather_group(index, base, source, target):
    for u in range(W):
        target[pl.ds(u, 1), :] = source[pl.ds(index[base + u], 1), :]


def join_body(*refs):
    pieces, whole, sems = refs[:X], refs[-2], refs[-1]
    rows = whole.shape[0] // X
    copies = [pltpu.make_async_copy(pieces[d], whole.at[pl.ds(d * rows, rows)], sems.at[d]) for d in range(X)]
    start(copies)
    wait(copies)


def join_call(pieces, after):
    pieces = [piece.reshape(-1, 2, NARROW, W) for piece in pieces]
    return pl.pallas_call(
        join_body,
        name="joined_pieces",
        cost_estimate=cost(1),
        out_shape=pltpu.HBM((X * pieces[0].shape[0], 2, NARROW, W), BF),
        in_specs=[ANY] * (X + 1),
        out_specs=ANY,
        scratch_shapes=[pltpu.SemaphoreType.DMA((X,))],
        compiler_params=room(8),
    )(*pieces, after)


def up_body(slots, perm_up, x_ref, own, other, shuffled_hbm, active_hbm, slope_hbm, scale_ref,
             left, right, mixed, even, odd, shuffled, active, slope, sems):
    load_l = loads_of(own, other, 0, left, sems.at[pl.ds(0, 2)])
    load_r = loads_of(own, other, 1, right, sems.at[pl.ds(2, 2)])
    start(load_l)
    start(load_r)
    scale = scale_of(x_ref)
    scale_ref[...] = scale
    wait(load_l)
    for j in range(NB):
        normed = (x_ref[:, j * W:(j + 1) * W].astype(F32) * scale).astype(BF)
        mixed[j * W:(j + 1) * W, :] = dot(normed, left_block(left, slots, j), (1, 0)).T
    wait(load_r)

    def store(source, target, q, sem):
        n = pl.ds(pl.multiple_of(q * GROUP, GROUP), GROUP)
        return pltpu.make_async_copy(source.at[n], target.at[n], sem)

    def hidden_group(q, source):
        for r in range(GROUP):
            rows = pl.ds(pl.multiple_of(q * W + r * NARROW, NARROW), NARROW)
            k = q * GROUP + r
            piece = source[r * NARROW:(r + 1) * NARROW, :].astype(BF)
            shuffled[rows, :] = piece
            hidden = dot(piece, right[slots[k]], (0, 0))
            squashed = jax.nn.sigmoid(hidden)
            active[k] = (hidden * squashed).astype(BF)
            slope[k] = (squashed * (1.0 + hidden * (1.0 - squashed))).astype(BF)
        store(active, active_hbm, q, sems.at[4]).start()
        store(slope, slope_hbm, q, sems.at[5]).start()

    def pair(p, carry):
        q = 2 * p
        gather_group(perm_up, q * W + W, mixed, odd)
        hidden_group(q, even)
        gather_group(perm_up, jnp.minimum(q + 2, NB - 1) * W, mixed, even)
        hidden_group(q + 1, odd)
        return carry

    gather_group(perm_up, 0, mixed, even)
    lax.fori_loop(0, NB // 2, pair, 0)
    last = pltpu.make_async_copy(shuffled, shuffled_hbm, sems.at[6])
    last.start()
    pltpu.make_async_copy(active, active_hbm, sems.at[4]).wait()
    pltpu.make_async_copy(slope, slope_hbm, sems.at[5]).wait()
    last.wait()


def up_call(slots, perm_up, x, up):
    count = x.shape[0]
    return pl.pallas_call(
        up_body,
        name="up_projection",
        cost_estimate=cost(12),
        out_shape=(
            pltpu.HBM((D, count), BF),
            pltpu.HBM((NH, count, W), BF),
            pltpu.HBM((NH, count, W), BF),
            jax.ShapeDtypeStruct((count, 1), F32),
        ),
        in_specs=[SMEM, SMEM, VMEM] + [ANY] * 2,
        out_specs=(ANY, ANY, ANY, VMEM),
        scratch_shapes=[
            pltpu.VMEM((NH, NARROW, W), BF),
            pltpu.VMEM((NH, NARROW, W), BF),
            pltpu.VMEM((D, count), F32),
            pltpu.VMEM((W, count), F32),
            pltpu.VMEM((W, count), F32),
            pltpu.VMEM((D, count), BF),
            pltpu.VMEM((NH, count, W), BF),
            pltpu.VMEM((NH, count, W), BF),
            pltpu.SemaphoreType.DMA((7,)),
        ],
        compiler_params=room(24),
    )(slots, perm_up, x, *in_hbm(*up))


def place_body(flag, slots, perm_dn, active_hbm, own, other, *rest):
    placed_hbm, active, right, mixed, moved, placed, sems = rest[-7:]

    @pl.when(flag[0] == 1)
    def work():
        loads = loads_of(own, other, 0, right, sems.at[pl.ds(0, 2)])
        loads += (pltpu.make_async_copy(active_hbm, active, sems.at[2]),)
        start(loads)
        wait(loads)

        def block(q, carry):
            for r in range(8):
                k = q * 8 + r
                rows = pl.ds(pl.multiple_of(k * NARROW, NARROW), NARROW)
                mixed[rows, :] = dot(right[slots[k]], active[k], (1, 1))
            return carry

        lax.fori_loop(0, NH // 8, block, 0)
        gather_rows(perm_dn, mixed, moved)
        for j in range(NB):
            placed[j * W:(j + 1) * W, :] = moved[j * W:(j + 1) * W, :].astype(BF)
        store = pltpu.make_async_copy(placed, placed_hbm, sems.at[0])
        store.start()
        store.wait()


def place_call(flag, slots, perm_dn, active, down, after, before):
    count = active.shape[1]
    ins = (flag, slots, perm_dn, *in_hbm(active, *down, *after))
    return pl.pallas_call(
        place_body,
        name="placed_rows",
        cost_estimate=cost(12),
        out_shape=pltpu.HBM((D, count), BF),
        in_specs=[SMEM] * 3 + [ANY] * (len(ins) - 3 + len(before)),
        out_specs=ANY,
        input_output_aliases={len(ins): 0} if before else {},
        scratch_shapes=[
            pltpu.VMEM((NH, count, W), BF),
            pltpu.VMEM((NH, NARROW, W), BF),
            pltpu.VMEM((D, count), F32),
            pltpu.VMEM((D, count), F32),
            pltpu.VMEM((D, count), BF),
            pltpu.SemaphoreType.DMA((3,)),
        ],
        compiler_params=room(18),
    )(*ins, *in_hbm(*before))


def back_body(part, parts_per, flag, slots, perm_up, perm_dn, g_hbm, acts_hbm, slope_hbm, up_own, up_other,
              down_own, down_other, *rest):
    (out_hbm, keep_hbm, gdown_hbm, ghidden_hbm,
     g, x, slope, left_up, right_up, right_dn, left_dn, even, odd, down, up, gdown, ghidden, gup, gnorm, out, sems) = rest[-21:]
    count = g.shape[0]
    tokens = pl.ds(part * count, count)

    @pl.when(flag[0] == 1)
    def work():
        load_g = pltpu.make_async_copy(g_hbm.at[pl.ds((part % parts_per) * count, count), :], g, sems.at[0])
        load_ld = loads_of(down_own, down_other, 1, left_dn, sems.at[pl.ds(1, 2)])
        load_rd = loads_of(down_own, down_other, 0, right_dn, sems.at[pl.ds(3, 2)])
        load_slope = pltpu.make_async_copy(slope_hbm.at[:, tokens, :], slope, sems.at[9])
        load_ru = loads_of(up_own, up_other, 1, right_up, sems.at[pl.ds(5, 2)])
        load_lu = loads_of(up_own, up_other, 0, left_up, sems.at[pl.ds(7, 2)])
        load_x = pltpu.make_async_copy(acts_hbm.at[tokens, :], x, sems.at[10])
        load_g.start()
        start(load_ld)
        start(load_rd)
        load_slope.start()
        start(load_ru)
        start(load_lu)
        load_x.start()
        load_g.wait()
        wait(load_ld)

        def placed_block(j, target):
            rows = pl.ds(pl.multiple_of(j * W, W), W)
            target[...] = dot(left_block(left_dn, slots, j), g[:, rows], (1, 1))

        def left_pair(p, carry):
            j = 2 * p
            placed_block(j + 1, odd)
            scatter_group(perm_dn, j * W, even, down)
            placed_block(jnp.minimum(j + 2, NB - 1), even)
            scatter_group(perm_dn, j * W + W, odd, down)
            return carry

        placed_block(0, even)
        lax.fori_loop(0, NB // 2, left_pair, 0)
        wait(load_rd)
        load_slope.wait()
        wait(load_ru)

        def hidden_group(q, target):
            for r in range(GROUP):
                rows = pl.ds(pl.multiple_of(q * W + r * NARROW, NARROW), NARROW)
                k = q * GROUP + r
                piece = down[rows, :].astype(BF)
                gdown[rows, :] = piece
                gactive = dot(piece, right_dn[slots[k]], (0, 0)).astype(BF)
                gh = (gactive.astype(F32) * slope[k].astype(F32)).astype(BF)
                ghidden[k] = gh
                target[r * NARROW:(r + 1) * NARROW, :] = dot(right_up[slots[k]], gh, (1, 1))

        def right_pair(p, carry):
            q = 2 * p
            hidden_group(q + 1, odd)
            scatter_group(perm_up, q * W, even, up)
            hidden_group(jnp.minimum(q + 2, NB - 1), even)
            scatter_group(perm_up, q * W + W, odd, up)
            return carry

        hidden_group(0, even)
        lax.fori_loop(0, NB // 2, right_pair, 0)
        store_h = pltpu.make_async_copy(ghidden, ghidden_hbm.at[:, tokens, :], sems.at[11])
        store_g = pltpu.make_async_copy(g, keep_hbm.at[0, tokens, :], sems.at[12])
        store_d = pltpu.make_async_copy(gdown, gdown_hbm.at[part], sems.at[0])
        store_h.start()
        store_d.start()
        store_g.start()
        wait(load_lu)
        load_x.wait()
        scale = scale_of(x)
        inner = jnp.zeros((count, W), F32)
        for j in range(NB):
            cols = slice(j * W, (j + 1) * W)
            gu = up[cols, :].T.astype(BF)
            gup[:, cols] = gu
            gn = dot(gu, left_block(left_up, slots, j), (1, 1))
            gnorm[:, cols] = gn
            inner = inner + gn * (x[:, cols].astype(F32) * scale)
        mean = jnp.sum(inner, axis=1, keepdims=True) * (1.0 / D)
        for j in range(NB):
            cols = slice(j * W, (j + 1) * W)
            normf = x[:, cols].astype(F32) * scale
            out[:, cols] = (g[:, cols].astype(F32) + scale * (gnorm[:, cols] - normf * mean)).astype(BF)
        store_out = pltpu.make_async_copy(out, out_hbm, sems.at[13])
        store_out.start()
        store_up = pltpu.make_async_copy(gup, keep_hbm.at[1, tokens, :], sems.at[14])
        store_up.start()
        store_h.wait()
        store_d.wait()
        store_g.wait()
        store_out.wait()
        store_up.wait()


def back_call(part, flag, slots, perm_up, perm_dn, g, acts, slope, weights, after, state, count):
    up, down = weights
    total = acts.shape[0]
    out_shape = (
        pltpu.HBM((count, D), BF),
        pltpu.HBM((2, total, D), BF),
        pltpu.HBM((total // count, D, count), BF),
        pltpu.HBM((NH, total, W), BF),
    )
    g = pltpu.with_memory_space_constraint(g, pltpu.VMEM)
    hbm = in_hbm(acts, slope, *up, *down, *after)
    ins = (flag, slots, perm_up, perm_dn, g, *hbm)
    kept = [(i, s) for i, s in enumerate(state) if s is not None]
    return pl.pallas_call(
        functools.partial(back_body, part, g.shape[0] // count),
        name="backward_step",
        cost_estimate=cost(14),
        out_shape=out_shape,
        in_specs=[SMEM] * 4 + [ANY] * (len(ins) - 4 + len(kept)),
        out_specs=(ANY,) * 4,
        input_output_aliases={len(ins) + n: i for n, (i, s) in enumerate(kept)},
        scratch_shapes=[
            pltpu.VMEM((count, D), BF),
            pltpu.VMEM((count, D), BF),
            pltpu.VMEM((NH, count, W), BF),
            pltpu.VMEM((NH, NARROW, W), BF),
            pltpu.VMEM((NH, NARROW, W), BF),
            pltpu.VMEM((NH, NARROW, W), BF),
            pltpu.VMEM((NH, NARROW, W), BF),
            pltpu.VMEM((W, count), F32),
            pltpu.VMEM((W, count), F32),
            pltpu.VMEM((D, count), F32),
            pltpu.VMEM((D, count), F32),
            pltpu.VMEM((D, count), BF),
            pltpu.VMEM((NH, count, W), BF),
            pltpu.VMEM((count, D), BF),
            pltpu.VMEM((count, D), F32),
            pltpu.VMEM((count, D), BF),
            pltpu.SemaphoreType.DMA((15,)),
        ],
        compiler_params=room(48),
    )(*ins, *in_hbm(*[s for i, s in kept]))


def core_split(core, pieces):
    mine = [jnp.where(core == 0, pieces[2 * y], pieces[2 * y + 1]).astype(BF) for y in range(Y)]
    other = [jnp.where(core == 0, pieces[2 * y + 1], pieces[2 * y]).astype(BF) for y in range(Y)]
    return mine, other


def put(at, factor, mine, other, pieces):
    own, rest = core_split(at[3], pieces)
    step = pl.program_id(0)
    dz = lax.rem(step // X - at[0] + Z_LO, Z_LO)
    dx = lax.rem(lax.rem(step, X) - at[1] + X, X)
    for y in range(Y):
        dy = lax.rem(y - at[2] + Y, Y)
        one = jnp.where(at[3] == 0, dx, dy)
        two = jnp.where(at[3] == 0, dy, dx)
        mine[one, two, factor, dz] = own[y]
        other[two, one, factor, dz] = rest[y]


def pieces_of(block):
    return [block[r * NARROW:(r + 1) * NARROW] for r in range(GROUP)]


def grads_body(at, x, scale, shuffled, active, placed, keep, keep_down, gh, mine, other):
    left_up, left_dn, right_up, right_dn = [], [], [], []
    for b in range(2):
        cols = slice(b * W, (b + 1) * W)
        normed = (x[:, cols].astype(F32) * scale[...]).astype(BF)
        left_up += pieces_of(dot(normed, keep[1, :, cols], (0, 0)))
        left_dn += pieces_of(dot(placed[cols, :], keep[0, :, cols], (1, 0)))
        gdown = jnp.concatenate([keep_down[p, cols, :] for p in range(keep_down.shape[0])], axis=1)
        for r in range(GROUP):
            rows = slice(r * NARROW, (r + 1) * NARROW)
            right_up.append(dot(shuffled[cols, :][rows], gh[b * GROUP + r], (1, 0)))
            right_dn.append(dot(gdown[rows], active[b * GROUP + r], (1, 0)))
    for factor, pieces in enumerate((left_up, right_up, right_dn, left_dn)):
        put(at, factor, mine, other, pieces)


def grads_call(at, x, scale, shuffled, active, placed, keep, keep_down, ghidden):
    count = x.shape[0]
    parts, _, part = keep_down.shape
    rows = pl.BlockSpec((2 * W, count), lambda i, w: (i, 0))
    cube = pl.BlockSpec((2 * GROUP, count, W), lambda i, w: (i, 0, 0))

    shape = (X, Y, 4, Z_LO, NARROW, W)
    whole = pl.BlockSpec(shape, lambda i, w: (0,) * 6)
    return pl.pallas_call(
        grads_body,
        name="factor_gradients",
        cost_estimate=cost(12),
        grid_spec=pltpu.PrefetchScalarGridSpec(
            num_scalar_prefetch=1,
            grid=(Z_LO * X,),
            in_specs=[
                pl.BlockSpec((count, 2 * W), lambda i, w: (0, i)),
                pl.BlockSpec((count, 1), lambda i, w: (0, 0)),
                rows, cube, rows,
                pl.BlockSpec((2, count, 2 * W), lambda i, w: (0, 0, i)),
                pl.BlockSpec((parts, 2 * W, part), lambda i, w: (0, i, 0)),
                cube,
            ],
            out_specs=[whole, whole],
        ),
        out_shape=(jax.ShapeDtypeStruct(shape, BF),) * 2,
        compiler_params=room(36),
    )(at, *in_hbm(x, scale, shuffled, active, placed, keep, keep_down, ghidden))


def shards(acts, cotangent, perm_up, perm_dn, left_up, right_up, right_dn, left_dn):
    up, down = gather_factors(left_up[0], right_up[0], right_dn[0], left_dn[0])
    slots = slot_table()
    at = jnp.stack([place(axis) for axis in ("z", "x", "y", "c")]).astype(jnp.int32)
    perm_up, perm_dn = perm_up[0], perm_dn[0]
    section_count = lax.axis_size("section")
    section_index = lax.axis_index("section")
    final_section = section_count - 1
    micro_count, tok_rows = acts.shape[1:3]
    x = acts[0].reshape(micro_count * tok_rows, D)
    parts = x.shape[0] // CHUNK
    shuffled, active, slope, scale = up_call(slots, perm_up, x, up)
    down = both_cores(join_call(down, scale))
    weights = (up, down)
    incoming = [cotangent.reshape(x.shape)] * parts
    kept = [None] * 3
    sent = [None] * parts
    early = (at[:1] == 1).astype(jnp.int32)
    placed = place_call(early, slots, perm_dn, active, down, (), ())
    for step in range(section_count):
        own = final_section - step
        flag = (section_index == own).astype(jnp.int32).reshape(1)
        for m in range(parts):
            after = (placed,) if m == 0 else ()
            sent[m], *kept = back_call(
                m, flag, slots, perm_up, perm_dn, incoming[m], x, slope, weights, after, [sent[m]] + kept, CHUNK
            )
            if own:
                incoming[m] = lax.ppermute(sent[m], "section", [(own, own - 1)])
        if step == 0:
            placed = place_call(1 - early, slots, perm_dn, active, down, (kept[2],), (placed,))
    mine, other = grads_call(at, x, scale, shuffled, active, placed, *kept)
    owned = scatter_factors(mine, other)
    results = jnp.concatenate(sent).reshape(acts.shape)
    left_up, right_up, right_dn, left_dn = [owned[i][None] for i in range(4)]
    return (results, left_up, right_up, right_dn, left_dn)


def solution(mesh):
    rows = P("section", "dp", None)
    return jax.shard_map(
        shards,
        mesh=mesh,
        in_specs=(
            P("section", None, "dp", None),
            P(None, "dp", None),
            P("section", None),
            P("section", None),
            rows,
            rows,
            rows,
            rows,
        ),
        out_specs=(P("section", None, "dp", None), rows, rows, rows, rows),
        check_vma=False,
    )
```

```python
import functools
import jax
import jax.numpy as jnp
from jax import lax
from jax.experimental import pallas as pl
from jax.experimental.pallas import tpu as pltpu
from jax.sharding import PartitionSpec as P

D = 4096
W = 256
NARROW = 64
NB = 16
NH = 64
GROUP = W // NARROW
CHUNK = 64
epsilon = 1e-06
BF = jnp.bfloat16
F32 = jnp.float32
ANY = pl.BlockSpec(memory_space=pl.ANY)
SMEM = pl.BlockSpec(memory_space=pltpu.SMEM)
VMEM = pl.BlockSpec(memory_space=pltpu.VMEM)
ROWS_PER_STEP = 4


def in_hbm(*arrays):
    return [pltpu.with_memory_space_constraint(a, pltpu.HBM) for a in arrays]


def room(mebibytes):
    return pltpu.CompilerParams(vmem_limit_bytes=mebibytes * 2**20)


def cost(microseconds):
    return pl.CostEstimate(flops=0, transcendentals=0, bytes_accessed=int(microseconds * 3.3e6))


Z_LO, X, Y, CORE = 2, 4, 4, 2
EXTENT = {"z": Z_LO, "x": X, "y": Y, "c": CORE}
STRIDE = {"z": X * Y * CORE, "x": Y * CORE, "y": CORE, "c": 1}


def place(axis):
    return lax.rem(lax.axis_index("dp") // STRIDE[axis], EXTENT[axis])


def shifted(block, axes, distance):
    route = []
    for device in range(Z_LO * X * Y * CORE):
        axis = axes if isinstance(axes, str) else axes[device % CORE]
        stride, extent = STRIDE[axis], EXTENT[axis]
        at = device // stride % extent
        route.append((device, device + ((at + distance) % extent - at) * stride))
    return lax.ppermute(block, "dp", route)


def gather_ring(block, axes, extent):
    return jnp.stack([block] + [shifted(block, axes, -d) for d in range(1, extent)])


def slot_table():
    k = jnp.arange(Z_LO * X * Y * CORE, dtype=jnp.int32)
    dz = (k // STRIDE["z"] - place("z")) % Z_LO
    dx = (k // STRIDE["x"] - place("x")) % X
    dy = (k // STRIDE["y"] - place("y")) % Y
    dc = (k - place("c")) % CORE
    ring = jnp.where(k % CORE == 0, dx * Y + dy, dy * X + dx)
    return ((dc * X * Y + ring) * Z_LO + dz).astype(jnp.int32)


def both_cores(own):
    return own, shifted(own, "c", 1)


def gather_factors(left_up, right_up, right_dn, left_dn):
    packed = jnp.concatenate([left_up, right_up, right_dn, left_dn]).reshape(4, NARROW, W)
    packed = gather_ring(gather_ring(packed, "z", Z_LO), ("y", "x"), X)
    up, down = lax.optimization_barrier((packed[:, :, :2], packed[:, :, 2:]))
    up = gather_ring(up, ("x", "y"), X)
    up, down = lax.optimization_barrier((up, down))
    down = [down] + [shifted(down, ("x", "y"), -d) for d in range(1, X)]
    return both_cores(up.reshape(-1, 2, NARROW, W)), down


def total_of(pieces):
    total = pieces[0].astype(F32)
    for piece in pieces[1:]:
        total = total + piece.astype(F32)
    return total


def reduce_ring(pieces, axes):
    return [pieces[0]] + [shifted(pieces[d], axes, d) for d in range(1, X)]


def fold_cores(mine, other):
    got = shifted(other, "c", 1)
    return [total_of([mine[d], got[d]]).astype(BF) for d in range(X)]


def finish_factors(rings):
    pieces = [
        jnp.concatenate([total_of([piece[d] for piece in ring]) for ring in rings]).astype(BF) for d in range(X)
    ]
    sums = total_of(reduce_ring(pieces, ("y", "x")))
    far = shifted(sums[:, 1].astype(BF), "z", 1)
    return sums[:, 0] + far.astype(F32)


def dot(a, b, contract):
    return lax.dot_general(a, b, ((contract[:1], contract[1:]), ((), ())), preferred_element_type=F32)


def gather_rows(index, source, target):
    def body(step, carry):
        base = step * ROWS_PER_STEP
        for u in range(ROWS_PER_STEP):
            target[pl.ds(base + u, 1), :] = source[pl.ds(index[base + u], 1), :]
        return carry

    lax.fori_loop(0, D // ROWS_PER_STEP, body, 0)


def scale_of(x_ref):
    total = jnp.zeros((x_ref.shape[0], W), F32)
    for j in range(NB):
        x = x_ref[:, j * W:(j + 1) * W].astype(F32)
        total = total + x * x
    return lax.rsqrt(jnp.sum(total, axis=1, keepdims=True) * (1.0 / D) + epsilon)


def left_block(ref, slots, j):
    return jnp.concatenate([ref[slots[j * GROUP + r]] for r in range(GROUP)], axis=0)


def loads_of(own, other, which, target, sem):
    half = own.shape[0]
    return (
        pltpu.make_async_copy(own.at[:, which], target.at[pl.ds(0, half)], sem.at[0]),
        pltpu.make_async_copy(other.at[:, which], target.at[pl.ds(half, half)], sem.at[1]),
    )


def start(copies):
    for copy in copies:
        copy.start()


def wait(copies):
    for copy in copies:
        copy.wait()


def scatter_group(index, base, source, target):
    for u in range(W):
        target[pl.ds(index[base + u], 1), :] = source[pl.ds(u, 1), :]


def gather_group(index, base, source, target):
    for u in range(W):
        target[pl.ds(u, 1), :] = source[pl.ds(index[base + u], 1), :]


def join_body(*refs):
    pieces, whole, sems = refs[:X], refs[-2], refs[-1]
    rows = whole.shape[0] // X
    copies = [pltpu.make_async_copy(pieces[d], whole.at[pl.ds(d * rows, rows)], sems.at[d]) for d in range(X)]
    start(copies)
    wait(copies)


def join_call(pieces, after):
    pieces = [piece.reshape(-1, 2, NARROW, W) for piece in pieces]
    return pl.pallas_call(
        join_body,
        name="joined_pieces",
        cost_estimate=cost(1),
        out_shape=pltpu.HBM((X * pieces[0].shape[0], 2, NARROW, W), BF),
        in_specs=[ANY] * (X + 1),
        out_specs=ANY,
        scratch_shapes=[pltpu.SemaphoreType.DMA((X,))],
        compiler_params=room(8),
    )(*pieces, after)


def up_body(slots, perm_up, x_ref, own, other, shuffled_hbm, active_hbm, slope_hbm, scale_ref,
             left, right, mixed, even, odd, shuffled, active, slope, sems):
    load_l = loads_of(own, other, 0, left, sems.at[pl.ds(0, 2)])
    load_r = loads_of(own, other, 1, right, sems.at[pl.ds(2, 2)])
    start(load_l)
    start(load_r)
    scale = scale_of(x_ref)
    scale_ref[...] = scale
    wait(load_l)
    for j in range(NB):
        normed = (x_ref[:, j * W:(j + 1) * W].astype(F32) * scale).astype(BF)
        mixed[j * W:(j + 1) * W, :] = dot(normed, left_block(left, slots, j), (1, 0)).T
    wait(load_r)

    def store(source, target, q, sem):
        n = pl.ds(pl.multiple_of(q * GROUP, GROUP), GROUP)
        return pltpu.make_async_copy(source.at[n], target.at[n], sem)

    def hidden_group(q, source):
        for r in range(GROUP):
            rows = pl.ds(pl.multiple_of(q * W + r * NARROW, NARROW), NARROW)
            k = q * GROUP + r
            piece = source[r * NARROW:(r + 1) * NARROW, :].astype(BF)
            shuffled[rows, :] = piece
            hidden = dot(piece, right[slots[k]], (0, 0))
            squashed = jax.nn.sigmoid(hidden)
            active[k] = (hidden * squashed).astype(BF)
            slope[k] = (squashed * (1.0 + hidden * (1.0 - squashed))).astype(BF)
        store(active, active_hbm, q, sems.at[4]).start()
        store(slope, slope_hbm, q, sems.at[5]).start()

    def pair(p, carry):
        q = 2 * p
        gather_group(perm_up, q * W + W, mixed, odd)
        hidden_group(q, even)
        gather_group(perm_up, jnp.minimum(q + 2, NB - 1) * W, mixed, even)
        hidden_group(q + 1, odd)
        return carry

    gather_group(perm_up, 0, mixed, even)
    lax.fori_loop(0, NB // 2, pair, 0)
    last = pltpu.make_async_copy(shuffled, shuffled_hbm, sems.at[6])
    last.start()
    pltpu.make_async_copy(active, active_hbm, sems.at[4]).wait()
    pltpu.make_async_copy(slope, slope_hbm, sems.at[5]).wait()
    last.wait()


def up_call(slots, perm_up, x, up):
    count = x.shape[0]
    return pl.pallas_call(
        up_body,
        name="up_projection",
        cost_estimate=cost(12),
        out_shape=(
            pltpu.HBM((D, count), BF),
            pltpu.HBM((NH, count, W), BF),
            pltpu.HBM((NH, count, W), BF),
            jax.ShapeDtypeStruct((count, 1), F32),
        ),
        in_specs=[SMEM, SMEM, VMEM] + [ANY] * 2,
        out_specs=(ANY, ANY, ANY, VMEM),
        scratch_shapes=[
            pltpu.VMEM((NH, NARROW, W), BF),
            pltpu.VMEM((NH, NARROW, W), BF),
            pltpu.VMEM((D, count), F32),
            pltpu.VMEM((W, count), F32),
            pltpu.VMEM((W, count), F32),
            pltpu.VMEM((D, count), BF),
            pltpu.VMEM((NH, count, W), BF),
            pltpu.VMEM((NH, count, W), BF),
            pltpu.SemaphoreType.DMA((7,)),
        ],
        compiler_params=room(24),
    )(slots, perm_up, x, *in_hbm(*up))


def place_body(flag, slots, perm_dn, active_hbm, own, other, *rest):
    placed_hbm, active, right, mixed, moved, placed, sems = rest[-7:]

    @pl.when(flag[0] == 1)
    def work():
        loads = loads_of(own, other, 0, right, sems.at[pl.ds(0, 2)])
        loads += (pltpu.make_async_copy(active_hbm, active, sems.at[2]),)
        start(loads)
        wait(loads)

        def block(q, carry):
            for r in range(8):
                k = q * 8 + r
                rows = pl.ds(pl.multiple_of(k * NARROW, NARROW), NARROW)
                mixed[rows, :] = dot(right[slots[k]], active[k], (1, 1))
            return carry

        lax.fori_loop(0, NH // 8, block, 0)
        gather_rows(perm_dn, mixed, moved)
        for j in range(NB):
            placed[j * W:(j + 1) * W, :] = moved[j * W:(j + 1) * W, :].astype(BF)
        store = pltpu.make_async_copy(placed, placed_hbm, sems.at[0])
        store.start()
        store.wait()


def place_call(flag, slots, perm_dn, active, down, after, before):
    count = active.shape[1]
    ins = (flag, slots, perm_dn, *in_hbm(active, *down, *after))
    return pl.pallas_call(
        place_body,
        name="placed_rows",
        cost_estimate=cost(12),
        out_shape=pltpu.HBM((D, count), BF),
        in_specs=[SMEM] * 3 + [ANY] * (len(ins) - 3 + len(before)),
        out_specs=ANY,
        input_output_aliases={len(ins): 0} if before else {},
        scratch_shapes=[
            pltpu.VMEM((NH, count, W), BF),
            pltpu.VMEM((NH, NARROW, W), BF),
            pltpu.VMEM((D, count), F32),
            pltpu.VMEM((D, count), F32),
            pltpu.VMEM((D, count), BF),
            pltpu.SemaphoreType.DMA((3,)),
        ],
        compiler_params=room(18),
    )(*ins, *in_hbm(*before))


def back_body(part, parts_per, flag, slots, perm_up, perm_dn, g_hbm, acts_hbm, slope_hbm, up_own, up_other,
              down_own, down_other, *rest):
    (out_hbm, keep_hbm, gdown_hbm, ghidden_hbm,
     g, x, slope, left_up, right_up, right_dn, left_dn, even, odd, down, up, gdown, ghidden, gup, gnorm, out, sems) = rest[-21:]
    count = g.shape[0]
    tokens = pl.ds(part * count, count)

    @pl.when(flag[0] == 1)
    def work():
        load_g = pltpu.make_async_copy(g_hbm.at[pl.ds((part % parts_per) * count, count), :], g, sems.at[0])
        load_ld = loads_of(down_own, down_other, 1, left_dn, sems.at[pl.ds(1, 2)])
        load_rd = loads_of(down_own, down_other, 0, right_dn, sems.at[pl.ds(3, 2)])
        load_slope = pltpu.make_async_copy(slope_hbm.at[:, tokens, :], slope, sems.at[9])
        load_ru = loads_of(up_own, up_other, 1, right_up, sems.at[pl.ds(5, 2)])
        load_lu = loads_of(up_own, up_other, 0, left_up, sems.at[pl.ds(7, 2)])
        load_x = pltpu.make_async_copy(acts_hbm.at[tokens, :], x, sems.at[10])
        load_g.start()
        start(load_ld)
        start(load_rd)
        load_slope.start()
        start(load_ru)
        start(load_lu)
        load_x.start()
        load_g.wait()
        wait(load_ld)

        def placed_block(j, target):
            rows = pl.ds(pl.multiple_of(j * W, W), W)
            target[...] = dot(left_block(left_dn, slots, j), g[:, rows], (1, 1))

        def left_pair(p, carry):
            j = 2 * p
            placed_block(j + 1, odd)
            scatter_group(perm_dn, j * W, even, down)
            placed_block(jnp.minimum(j + 2, NB - 1), even)
            scatter_group(perm_dn, j * W + W, odd, down)
            return carry

        placed_block(0, even)
        lax.fori_loop(0, NB // 2, left_pair, 0)
        wait(load_rd)
        load_slope.wait()
        wait(load_ru)

        def hidden_group(q, target):
            for r in range(GROUP):
                rows = pl.ds(pl.multiple_of(q * W + r * NARROW, NARROW), NARROW)
                k = q * GROUP + r
                piece = down[rows, :].astype(BF)
                gdown[rows, :] = piece
                gactive = dot(piece, right_dn[slots[k]], (0, 0)).astype(BF)
                gh = (gactive.astype(F32) * slope[k].astype(F32)).astype(BF)
                ghidden[k] = gh
                target[r * NARROW:(r + 1) * NARROW, :] = dot(right_up[slots[k]], gh, (1, 1))

        def right_pair(p, carry):
            q = 2 * p
            hidden_group(q + 1, odd)
            scatter_group(perm_up, q * W, even, up)
            hidden_group(jnp.minimum(q + 2, NB - 1), even)
            scatter_group(perm_up, q * W + W, odd, up)
            return carry

        hidden_group(0, even)
        lax.fori_loop(0, NB // 2, right_pair, 0)
        store_h = pltpu.make_async_copy(ghidden, ghidden_hbm.at[:, tokens, :], sems.at[11])
        store_g = pltpu.make_async_copy(g, keep_hbm.at[0, tokens, :], sems.at[12])
        store_d = pltpu.make_async_copy(gdown, gdown_hbm.at[part], sems.at[0])
        store_h.start()
        store_d.start()
        store_g.start()
        wait(load_lu)
        load_x.wait()
        scale = scale_of(x)
        inner = jnp.zeros((count, W), F32)
        for j in range(NB):
            cols = slice(j * W, (j + 1) * W)
            gu = up[cols, :].T.astype(BF)
            gup[:, cols] = gu
            gn = dot(gu, left_block(left_up, slots, j), (1, 1))
            gnorm[:, cols] = gn
            inner = inner + gn * (x[:, cols].astype(F32) * scale)
        mean = jnp.sum(inner, axis=1, keepdims=True) * (1.0 / D)
        for j in range(NB):
            cols = slice(j * W, (j + 1) * W)
            normf = x[:, cols].astype(F32) * scale
            out[:, cols] = (g[:, cols].astype(F32) + scale * (gnorm[:, cols] - normf * mean)).astype(BF)
        store_out = pltpu.make_async_copy(out, out_hbm, sems.at[13])
        store_out.start()
        store_up = pltpu.make_async_copy(gup, keep_hbm.at[1, tokens, :], sems.at[14])
        store_up.start()
        store_h.wait()
        store_d.wait()
        store_g.wait()
        store_out.wait()
        store_up.wait()


def back_call(part, flag, slots, perm_up, perm_dn, g, acts, slope, weights, after, state, count):
    up, down = weights
    total = acts.shape[0]
    out_shape = (
        pltpu.HBM((count, D), BF),
        pltpu.HBM((2, total, D), BF),
        pltpu.HBM((total // count, D, count), BF),
        pltpu.HBM((NH, total, W), BF),
    )
    g = pltpu.with_memory_space_constraint(g, pltpu.VMEM if g.shape[0] == count else pltpu.HBM)
    hbm = in_hbm(acts, slope, *up, *down, *after)
    ins = (flag, slots, perm_up, perm_dn, g, *hbm)
    kept = [(i, s) for i, s in enumerate(state) if s is not None]
    return pl.pallas_call(
        functools.partial(back_body, part, g.shape[0] // count),
        name="backward_step",
        cost_estimate=cost(14),
        out_shape=out_shape,
        in_specs=[SMEM] * 4 + [ANY] * (len(ins) - 4 + len(kept)),
        out_specs=(ANY,) * 4,
        input_output_aliases={len(ins) + n: i for n, (i, s) in enumerate(kept)},
        scratch_shapes=[
            pltpu.VMEM((count, D), BF),
            pltpu.VMEM((count, D), BF),
            pltpu.VMEM((NH, count, W), BF),
            pltpu.VMEM((NH, NARROW, W), BF),
            pltpu.VMEM((NH, NARROW, W), BF),
            pltpu.VMEM((NH, NARROW, W), BF),
            pltpu.VMEM((NH, NARROW, W), BF),
            pltpu.VMEM((W, count), F32),
            pltpu.VMEM((W, count), F32),
            pltpu.VMEM((D, count), F32),
            pltpu.VMEM((D, count), F32),
            pltpu.VMEM((D, count), BF),
            pltpu.VMEM((NH, count, W), BF),
            pltpu.VMEM((count, D), BF),
            pltpu.VMEM((count, D), F32),
            pltpu.VMEM((count, D), BF),
            pltpu.SemaphoreType.DMA((15,)),
        ],
        compiler_params=room(48),
    )(*ins, *in_hbm(*[s for i, s in kept]))


def core_split(core, pieces):
    mine = [jnp.where(core == 0, pieces[2 * y], pieces[2 * y + 1]).astype(BF) for y in range(Y)]
    other = [jnp.where(core == 0, pieces[2 * y + 1], pieces[2 * y]).astype(BF) for y in range(Y)]
    return mine, other


def put(at, factor, mine, other, pieces):
    own, rest = core_split(at[3], pieces)
    step = pl.program_id(0)
    dz = lax.rem(step // X - at[0] + Z_LO, Z_LO)
    dx = lax.rem(lax.rem(step, X) - at[1] + X, X)
    for y in range(Y):
        dy = lax.rem(y - at[2] + Y, Y)
        one = jnp.where(at[3] == 0, dx, dy)
        two = jnp.where(at[3] == 0, dy, dx)
        mine[one, two, factor, dz] = own[y]
        other[two, one, factor, dz] = rest[y]


def pieces_of(block):
    return [block[r * NARROW:(r + 1) * NARROW] for r in range(GROUP)]


def left_body(at, x, scale, placed, keep, mine, other):
    left_up, left_dn = [], []
    for b in range(2):
        cols = slice(b * W, (b + 1) * W)
        normed = (x[:, cols].astype(F32) * scale[...]).astype(BF)
        left_up += pieces_of(dot(normed, keep[1, :, cols], (0, 0)))
        left_dn += pieces_of(dot(placed[cols, :], keep[0, :, cols], (1, 0)))
    put(at, 0, mine, other, left_up)
    put(at, 1, mine, other, left_dn)


def right_body(at, shuffled, active, keep_down, gh, mine, other):
    right_up, right_dn = [], []
    for b in range(2):
        cols = slice(b * W, (b + 1) * W)
        gdown = jnp.concatenate([keep_down[p, cols, :] for p in range(keep_down.shape[0])], axis=1)
        for r in range(GROUP):
            rows = slice(r * NARROW, (r + 1) * NARROW)
            right_up.append(dot(shuffled[cols, :][rows], gh[b * GROUP + r], (1, 0)))
            right_dn.append(dot(gdown[rows], active[b * GROUP + r], (1, 0)))
    put(at, 0, mine, other, right_up)
    put(at, 1, mine, other, right_dn)


def grads_call(body, name, at, ins, specs):
    shape = (X, Y, 2, Z_LO, NARROW, W)
    whole = pl.BlockSpec(shape, lambda i, w: (0,) * 6)
    return pl.pallas_call(
        body,
        name=name,
        cost_estimate=cost(6),
        grid_spec=pltpu.PrefetchScalarGridSpec(
            num_scalar_prefetch=1,
            grid=(Z_LO * X,),
            in_specs=specs,
            out_specs=[whole, whole],
        ),
        out_shape=(jax.ShapeDtypeStruct(shape, BF),) * 2,
        compiler_params=room(36),
    )(at, *ins)


def left_grads(at, x, scale, placed, keep):
    count = x.shape[0]
    specs = [
        pl.BlockSpec((count, 2 * W), lambda i, w: (0, i)),
        pl.BlockSpec((count, 1), lambda i, w: (0, 0)),
        pl.BlockSpec((2 * W, count), lambda i, w: (i, 0)),
        pl.BlockSpec((2, count, 2 * W), lambda i, w: (0, 0, i)),
    ]
    return grads_call(left_body, "left_gradients", at, in_hbm(x, scale, placed, keep), specs)


def right_grads(at, shuffled, active, keep_down, ghidden):
    count = shuffled.shape[1]
    parts, _, part = keep_down.shape
    cube = pl.BlockSpec((2 * GROUP, count, W), lambda i, w: (i, 0, 0))
    specs = [
        pl.BlockSpec((2 * W, count), lambda i, w: (i, 0)),
        cube,
        pl.BlockSpec((parts, 2 * W, part), lambda i, w: (0, i, 0)),
        cube,
    ]
    return grads_call(right_body, "right_gradients", at, in_hbm(shuffled, active, keep_down, ghidden), specs)


def shards(acts, cotangent, perm_up, perm_dn, left_up, right_up, right_dn, left_dn):
    up, down = gather_factors(left_up[0], right_up[0], right_dn[0], left_dn[0])
    slots = slot_table()
    at = jnp.stack([place(axis) for axis in ("z", "x", "y", "c")]).astype(jnp.int32)
    perm_up, perm_dn = perm_up[0], perm_dn[0]
    section_count = lax.axis_size("section")
    section_index = lax.axis_index("section")
    final_section = section_count - 1
    micro_count, tok_rows = acts.shape[1:3]
    x = acts[0].reshape(micro_count * tok_rows, D)
    parts = x.shape[0] // CHUNK
    shuffled, active, slope, scale = up_call(slots, perm_up, x, up)
    down = both_cores(join_call(down, scale))
    weights = (up, down)
    incoming = [cotangent.reshape(x.shape)] * parts
    kept = [None] * 3
    sent = [None] * parts
    early = (at[:1] == 1).astype(jnp.int32)
    placed = place_call(early, slots, perm_dn, active, down, (), ())
    for step in range(section_count):
        own = final_section - step
        flag = (section_index == own).astype(jnp.int32).reshape(1)
        for m in range(parts):
            after = (placed,) if m == 0 else ()
            sent[m], *kept = back_call(
                m, flag, slots, perm_up, perm_dn, incoming[m], x, slope, weights, after, [sent[m]] + kept, CHUNK
            )
            if own:
                incoming[m] = lax.ppermute(sent[m], "section", [(own, own - 1)])
        if step == 0:
            placed = place_call(1 - early, slots, perm_dn, active, down, (kept[2],), (placed,))
    keep, keep_down, ghidden = kept
    lefts = fold_cores(*left_grads(at, x, scale, placed, keep))
    left_ring = reduce_ring(lefts, ("x", "y"))
    rights = fold_cores(*right_grads(at, shuffled, active, keep_down, ghidden))
    right_ring = reduce_ring(rights, ("x", "y"))
    owned = finish_factors((left_ring, right_ring))
    results = jnp.concatenate(sent).reshape(acts.shape)
    left_up, left_dn, right_up, right_dn = [owned[i][None] for i in range(4)]
    return (results, left_up, right_up, right_dn, left_dn)


def solution(mesh):
    rows = P("section", "dp", None)
    return jax.shard_map(
        shards,
        mesh=mesh,
        in_specs=(
            P("section", None, "dp", None),
            P(None, "dp", None),
            P("section", None),
            P("section", None),
            rows,
            rows,
            rows,
            rows,
        ),
        out_specs=(P("section", None, "dp", None), rows, rows, rows, rows),
        check_vma=False,
    )
```

```python
import functools
import jax
import jax.numpy as jnp
from jax import lax
from jax.experimental import pallas as pl
from jax.experimental.pallas import tpu as pltpu
from jax.sharding import PartitionSpec as P

D = 4096
W = 256
NARROW = 64
NB = 16
NH = 64
GROUP = W // NARROW
CHUNK = 64
epsilon = 1e-06
BF = jnp.bfloat16
F32 = jnp.float32
ANY = pl.BlockSpec(memory_space=pl.ANY)
SMEM = pl.BlockSpec(memory_space=pltpu.SMEM)
VMEM = pl.BlockSpec(memory_space=pltpu.VMEM)
ROWS_PER_STEP = 8


def in_hbm(*arrays):
    return [pltpu.with_memory_space_constraint(a, pltpu.HBM) for a in arrays]


def room(mebibytes):
    return pltpu.CompilerParams(vmem_limit_bytes=mebibytes * 2**20)


def cost(microseconds):
    return pl.CostEstimate(flops=0, transcendentals=0, bytes_accessed=int(microseconds * 3.3e6))


Z_LO, X, Y, CORE = 2, 4, 4, 2
EXTENT = {"z": Z_LO, "x": X, "y": Y, "c": CORE}
STRIDE = {"z": X * Y * CORE, "x": Y * CORE, "y": CORE, "c": 1}


def place(axis):
    return lax.rem(lax.axis_index("dp") // STRIDE[axis], EXTENT[axis])


def shifted(block, axes, distance):
    route = []
    for device in range(Z_LO * X * Y * CORE):
        axis = axes if isinstance(axes, str) else axes[device % CORE]
        stride, extent = STRIDE[axis], EXTENT[axis]
        at = device // stride % extent
        route.append((device, device + ((at + distance) % extent - at) * stride))
    return lax.ppermute(block, "dp", route)


def gather_ring(block, axes, extent):
    return jnp.stack([block] + [shifted(block, axes, -d) for d in range(1, extent)])


def slot_table():
    k = jnp.arange(Z_LO * X * Y * CORE, dtype=jnp.int32)
    dz = (k // STRIDE["z"] - place("z")) % Z_LO
    dx = (k // STRIDE["x"] - place("x")) % X
    dy = (k // STRIDE["y"] - place("y")) % Y
    dc = (k - place("c")) % CORE
    ring = jnp.where(k % CORE == 0, dx * Y + dy, dy * X + dx)
    return ((dc * X * Y + ring) * Z_LO + dz).astype(jnp.int32)


def both_cores(own):
    return own, shifted(own, "c", 1)


def gather_factors(left_up, right_up, right_dn, left_dn):
    packed = jnp.concatenate([left_up, right_up, right_dn, left_dn]).reshape(4, NARROW, W)
    packed = gather_ring(gather_ring(packed, "z", Z_LO), ("y", "x"), X)
    up, down = lax.optimization_barrier((packed[:, :, :2], packed[:, :, 2:]))
    up = gather_ring(up, ("x", "y"), X)
    up, down = lax.optimization_barrier((up, down))
    down = [down] + [shifted(down, ("x", "y"), -d) for d in range(1, X)]
    return both_cores(up.reshape(-1, 2, NARROW, W)), down


def total_of(pieces):
    total = pieces[0].astype(F32)
    for piece in pieces[1:]:
        total = total + piece.astype(F32)
    return total


def reduce_ring(pieces, axes):
    return [pieces[0]] + [shifted(pieces[d], axes, d) for d in range(1, X)]


def fold_cores(mine, other):
    got = shifted(other, "c", 1)
    return [total_of([mine[d], got[d]]).astype(BF) for d in range(X)]


def finish_factors(rings):
    pieces = [
        jnp.concatenate([total_of([piece[d] for piece in ring]) for ring in rings]).astype(BF) for d in range(X)
    ]
    sums = total_of(reduce_ring(pieces, ("y", "x")))
    far = shifted(sums[:, 1].astype(BF), "z", 1)
    return sums[:, 0] + far.astype(F32)


def dot(a, b, contract):
    return lax.dot_general(a, b, ((contract[:1], contract[1:]), ((), ())), preferred_element_type=F32)


def gather_rows(index, source, target):
    def body(step, carry):
        base = step * ROWS_PER_STEP
        for u in range(ROWS_PER_STEP):
            target[pl.ds(base + u, 1), :] = source[pl.ds(index[base + u], 1), :]
        return carry

    lax.fori_loop(0, D // ROWS_PER_STEP, body, 0)


def scale_of(x_ref):
    total = jnp.zeros((x_ref.shape[0], W), F32)
    for j in range(NB):
        x = x_ref[:, j * W:(j + 1) * W].astype(F32)
        total = total + x * x
    return lax.rsqrt(jnp.sum(total, axis=1, keepdims=True) * (1.0 / D) + epsilon)


def left_block(ref, slots, j):
    return jnp.concatenate([ref[slots[j * GROUP + r]] for r in range(GROUP)], axis=0)


def loads_of(own, other, which, target, sem):
    half = own.shape[0]
    return (
        pltpu.make_async_copy(own.at[:, which], target.at[pl.ds(0, half)], sem.at[0]),
        pltpu.make_async_copy(other.at[:, which], target.at[pl.ds(half, half)], sem.at[1]),
    )


def start(copies):
    for copy in copies:
        copy.start()


def wait(copies):
    for copy in copies:
        copy.wait()


def scatter_group(index, base, source, target):
    for u in range(W):
        target[pl.ds(index[base + u], 1), :] = source[pl.ds(u, 1), :]


def gather_group(index, base, source, target):
    for u in range(W):
        target[pl.ds(u, 1), :] = source[pl.ds(index[base + u], 1), :]


def join_body(*refs):
    pieces, whole, sems = refs[:X], refs[-2], refs[-1]
    rows = whole.shape[0] // X
    copies = [pltpu.make_async_copy(pieces[d], whole.at[pl.ds(d * rows, rows)], sems.at[d]) for d in range(X)]
    start(copies)
    wait(copies)


def join_call(pieces, after):
    pieces = [piece.reshape(-1, 2, NARROW, W) for piece in pieces]
    return pl.pallas_call(
        join_body,
        name="joined_pieces",
        cost_estimate=cost(1),
        out_shape=pltpu.HBM((X * pieces[0].shape[0], 2, NARROW, W), BF),
        in_specs=[ANY] * (X + 1),
        out_specs=ANY,
        scratch_shapes=[pltpu.SemaphoreType.DMA((X,))],
        compiler_params=room(8),
    )(*pieces, after)


def up_body(slots, perm_up, x_ref, own, other, shuffled_hbm, active_hbm, slope_hbm, scale_ref,
             left, right, mixed, even, odd, shuffled, active, slope, sems):
    load_l = loads_of(own, other, 0, left, sems.at[pl.ds(0, 2)])
    load_r = loads_of(own, other, 1, right, sems.at[pl.ds(2, 2)])
    start(load_l)
    start(load_r)
    scale = scale_of(x_ref)
    scale_ref[...] = scale
    wait(load_l)
    for j in range(NB):
        normed = (x_ref[:, j * W:(j + 1) * W].astype(F32) * scale).astype(BF)
        mixed[j * W:(j + 1) * W, :] = dot(normed, left_block(left, slots, j), (1, 0)).T
    wait(load_r)

    def store(source, target, q, sem):
        n = pl.ds(pl.multiple_of(q * GROUP, GROUP), GROUP)
        return pltpu.make_async_copy(source.at[n], target.at[n], sem)

    def hidden_group(q, source):
        for r in range(GROUP):
            rows = pl.ds(pl.multiple_of(q * W + r * NARROW, NARROW), NARROW)
            k = q * GROUP + r
            piece = source[r * NARROW:(r + 1) * NARROW, :].astype(BF)
            shuffled[rows, :] = piece
            hidden = dot(piece, right[slots[k]], (0, 0))
            squashed = jax.nn.sigmoid(hidden)
            active[k] = (hidden * squashed).astype(BF)
            slope[k] = (squashed * (1.0 + hidden * (1.0 - squashed))).astype(BF)
        store(active, active_hbm, q, sems.at[4]).start()
        store(slope, slope_hbm, q, sems.at[5]).start()

    def pair(p, carry):
        q = 2 * p
        gather_group(perm_up, q * W + W, mixed, odd)
        hidden_group(q, even)
        gather_group(perm_up, jnp.minimum(q + 2, NB - 1) * W, mixed, even)
        hidden_group(q + 1, odd)
        return carry

    gather_group(perm_up, 0, mixed, even)
    lax.fori_loop(0, NB // 2, pair, 0)
    last = pltpu.make_async_copy(shuffled, shuffled_hbm, sems.at[6])
    last.start()
    pltpu.make_async_copy(active, active_hbm, sems.at[4]).wait()
    pltpu.make_async_copy(slope, slope_hbm, sems.at[5]).wait()
    last.wait()


def up_call(slots, perm_up, x, up):
    count = x.shape[0]
    return pl.pallas_call(
        up_body,
        name="up_projection",
        cost_estimate=cost(12),
        out_shape=(
            pltpu.HBM((D, count), BF),
            pltpu.HBM((NH, count, W), BF),
            pltpu.HBM((NH, count, W), BF),
            jax.ShapeDtypeStruct((count, 1), F32),
        ),
        in_specs=[SMEM, SMEM, VMEM] + [ANY] * 2,
        out_specs=(ANY, ANY, ANY, VMEM),
        scratch_shapes=[
            pltpu.VMEM((NH, NARROW, W), BF),
            pltpu.VMEM((NH, NARROW, W), BF),
            pltpu.VMEM((D, count), F32),
            pltpu.VMEM((W, count), F32),
            pltpu.VMEM((W, count), F32),
            pltpu.VMEM((D, count), BF),
            pltpu.VMEM((NH, count, W), BF),
            pltpu.VMEM((NH, count, W), BF),
            pltpu.SemaphoreType.DMA((7,)),
        ],
        compiler_params=room(24),
    )(slots, perm_up, x, *in_hbm(*up))


def place_body(flag, slots, perm_dn, active_hbm, own, other, *rest):
    placed_hbm, active, right, mixed, moved, placed, sems = rest[-7:]

    @pl.when(flag[0] == 1)
    def work():
        loads = loads_of(own, other, 0, right, sems.at[pl.ds(0, 2)])
        loads += (pltpu.make_async_copy(active_hbm, active, sems.at[2]),)
        start(loads)
        wait(loads)

        def block(q, carry):
            for r in range(8):
                k = q * 8 + r
                rows = pl.ds(pl.multiple_of(k * NARROW, NARROW), NARROW)
                mixed[rows, :] = dot(right[slots[k]], active[k], (1, 1))
            return carry

        lax.fori_loop(0, NH // 8, block, 0)
        gather_rows(perm_dn, mixed, moved)
        for j in range(NB):
            placed[j * W:(j + 1) * W, :] = moved[j * W:(j + 1) * W, :].astype(BF)
        store = pltpu.make_async_copy(placed, placed_hbm, sems.at[0])
        store.start()
        store.wait()


def place_call(flag, slots, perm_dn, active, down, after, before):
    count = active.shape[1]
    ins = (flag, slots, perm_dn, *in_hbm(active, *down, *after))
    return pl.pallas_call(
        place_body,
        name="placed_rows",
        cost_estimate=cost(12),
        out_shape=pltpu.HBM((D, count), BF),
        in_specs=[SMEM] * 3 + [ANY] * (len(ins) - 3 + len(before)),
        out_specs=ANY,
        input_output_aliases={len(ins): 0} if before else {},
        scratch_shapes=[
            pltpu.VMEM((NH, count, W), BF),
            pltpu.VMEM((NH, NARROW, W), BF),
            pltpu.VMEM((D, count), F32),
            pltpu.VMEM((D, count), F32),
            pltpu.VMEM((D, count), BF),
            pltpu.SemaphoreType.DMA((3,)),
        ],
        compiler_params=room(18),
    )(*ins, *in_hbm(*before))


def back_body(part, parts_per, flag, slots, perm_up, perm_dn, g_hbm, acts_hbm, slope_hbm, up_own, up_other,
              down_own, down_other, *rest):
    (out_hbm, keep_hbm, gdown_hbm, ghidden_hbm,
     g, x, slope, left_up, right_up, right_dn, left_dn, even, odd, down, up, gdown, ghidden, gup, gnorm, out, sems) = rest[-21:]
    count = g.shape[0]
    tokens = pl.ds(part * count, count)

    @pl.when(flag[0] == 1)
    def work():
        load_g = pltpu.make_async_copy(g_hbm.at[pl.ds((part % parts_per) * count, count), :], g, sems.at[0])
        load_ld = loads_of(down_own, down_other, 1, left_dn, sems.at[pl.ds(1, 2)])
        load_rd = loads_of(down_own, down_other, 0, right_dn, sems.at[pl.ds(3, 2)])
        load_slope = pltpu.make_async_copy(slope_hbm.at[:, tokens, :], slope, sems.at[9])
        load_ru = loads_of(up_own, up_other, 1, right_up, sems.at[pl.ds(5, 2)])
        load_lu = loads_of(up_own, up_other, 0, left_up, sems.at[pl.ds(7, 2)])
        load_x = pltpu.make_async_copy(acts_hbm.at[tokens, :], x, sems.at[10])
        load_g.start()
        start(load_ld)
        start(load_rd)
        load_slope.start()
        start(load_ru)
        start(load_lu)
        load_x.start()
        load_g.wait()
        wait(load_ld)

        def placed_block(j, target):
            rows = pl.ds(pl.multiple_of(j * W, W), W)
            target[...] = dot(left_block(left_dn, slots, j), g[:, rows], (1, 1))

        def left_pair(p, carry):
            j = 2 * p
            placed_block(j + 1, odd)
            scatter_group(perm_dn, j * W, even, down)
            placed_block(jnp.minimum(j + 2, NB - 1), even)
            scatter_group(perm_dn, j * W + W, odd, down)
            return carry

        placed_block(0, even)
        lax.fori_loop(0, NB // 2, left_pair, 0)
        wait(load_rd)
        load_slope.wait()
        wait(load_ru)

        def hidden_group(q, target):
            for r in range(GROUP):
                rows = pl.ds(pl.multiple_of(q * W + r * NARROW, NARROW), NARROW)
                k = q * GROUP + r
                piece = down[rows, :].astype(BF)
                gdown[rows, :] = piece
                gactive = dot(piece, right_dn[slots[k]], (0, 0)).astype(BF)
                gh = (gactive.astype(F32) * slope[k].astype(F32)).astype(BF)
                ghidden[k] = gh
                target[r * NARROW:(r + 1) * NARROW, :] = dot(right_up[slots[k]], gh, (1, 1))

        def right_pair(p, carry):
            q = 2 * p
            hidden_group(q + 1, odd)
            scatter_group(perm_up, q * W, even, up)
            hidden_group(jnp.minimum(q + 2, NB - 1), even)
            scatter_group(perm_up, q * W + W, odd, up)
            return carry

        hidden_group(0, even)
        lax.fori_loop(0, NB // 2, right_pair, 0)
        store_h = pltpu.make_async_copy(ghidden, ghidden_hbm.at[:, tokens, :], sems.at[11])
        store_g = pltpu.make_async_copy(g, keep_hbm.at[0, tokens, :], sems.at[12])
        store_d = pltpu.make_async_copy(gdown, gdown_hbm.at[part], sems.at[0])
        store_h.start()
        store_d.start()
        store_g.start()
        wait(load_lu)
        load_x.wait()
        scale = scale_of(x)
        inner = jnp.zeros((count, W), F32)
        for j in range(NB):
            cols = slice(j * W, (j + 1) * W)
            gu = up[cols, :].T.astype(BF)
            gup[:, cols] = gu
            gn = dot(gu, left_block(left_up, slots, j), (1, 1))
            gnorm[:, cols] = gn
            inner = inner + gn * (x[:, cols].astype(F32) * scale)
        mean = jnp.sum(inner, axis=1, keepdims=True) * (1.0 / D)
        for j in range(NB):
            cols = slice(j * W, (j + 1) * W)
            normf = x[:, cols].astype(F32) * scale
            out[:, cols] = (g[:, cols].astype(F32) + scale * (gnorm[:, cols] - normf * mean)).astype(BF)
        store_out = pltpu.make_async_copy(out, out_hbm, sems.at[13])
        store_out.start()
        store_up = pltpu.make_async_copy(gup, keep_hbm.at[1, tokens, :], sems.at[14])
        store_up.start()
        store_h.wait()
        store_d.wait()
        store_g.wait()
        store_out.wait()
        store_up.wait()


def back_call(part, flag, slots, perm_up, perm_dn, g, acts, slope, weights, after, state, count):
    up, down = weights
    total = acts.shape[0]
    out_shape = (
        pltpu.HBM((count, D), BF),
        pltpu.HBM((2, total, D), BF),
        pltpu.HBM((total // count, D, count), BF),
        pltpu.HBM((NH, total, W), BF),
    )
    g = pltpu.with_memory_space_constraint(g, pltpu.VMEM if g.shape[0] == count else pltpu.HBM)
    hbm = in_hbm(acts, slope, *up, *down, *after)
    ins = (flag, slots, perm_up, perm_dn, g, *hbm)
    kept = [(i, s) for i, s in enumerate(state) if s is not None]
    return pl.pallas_call(
        functools.partial(back_body, part, g.shape[0] // count),
        name="backward_step",
        cost_estimate=cost(14),
        out_shape=out_shape,
        in_specs=[SMEM] * 4 + [ANY] * (len(ins) - 4 + len(kept)),
        out_specs=(ANY,) * 4,
        input_output_aliases={len(ins) + n: i for n, (i, s) in enumerate(kept)},
        scratch_shapes=[
            pltpu.VMEM((count, D), BF),
            pltpu.VMEM((count, D), BF),
            pltpu.VMEM((NH, count, W), BF),
            pltpu.VMEM((NH, NARROW, W), BF),
            pltpu.VMEM((NH, NARROW, W), BF),
            pltpu.VMEM((NH, NARROW, W), BF),
            pltpu.VMEM((NH, NARROW, W), BF),
            pltpu.VMEM((W, count), F32),
            pltpu.VMEM((W, count), F32),
            pltpu.VMEM((D, count), F32),
            pltpu.VMEM((D, count), F32),
            pltpu.VMEM((D, count), BF),
            pltpu.VMEM((NH, count, W), BF),
            pltpu.VMEM((count, D), BF),
            pltpu.VMEM((count, D), F32),
            pltpu.VMEM((count, D), BF),
            pltpu.SemaphoreType.DMA((15,)),
        ],
        compiler_params=room(48),
    )(*ins, *in_hbm(*[s for i, s in kept]))


def core_split(core, pieces):
    mine = [jnp.where(core == 0, pieces[2 * y], pieces[2 * y + 1]).astype(BF) for y in range(Y)]
    other = [jnp.where(core == 0, pieces[2 * y + 1], pieces[2 * y]).astype(BF) for y in range(Y)]
    return mine, other


def put(at, factor, mine, other, pieces):
    own, rest = core_split(at[3], pieces)
    step = pl.program_id(0)
    dz = lax.rem(step // X - at[0] + Z_LO, Z_LO)
    dx = lax.rem(lax.rem(step, X) - at[1] + X, X)
    for y in range(Y):
        dy = lax.rem(y - at[2] + Y, Y)
        one = jnp.where(at[3] == 0, dx, dy)
        two = jnp.where(at[3] == 0, dy, dx)
        mine[one, two, factor, dz] = own[y]
        other[two, one, factor, dz] = rest[y]


def pieces_of(block):
    return [block[r * NARROW:(r + 1) * NARROW] for r in range(GROUP)]


def left_body(at, x, scale, placed, keep, mine, other):
    left_up, left_dn = [], []
    for b in range(2):
        cols = slice(b * W, (b + 1) * W)
        normed = (x[:, cols].astype(F32) * scale[...]).astype(BF)
        left_up += pieces_of(dot(normed, keep[1, :, cols], (0, 0)))
        left_dn += pieces_of(dot(placed[cols, :], keep[0, :, cols], (1, 0)))
    put(at, 0, mine, other, left_up)
    put(at, 1, mine, other, left_dn)


def right_body(at, shuffled, active, keep_down, gh, mine, other):
    right_up, right_dn = [], []
    for b in range(2):
        cols = slice(b * W, (b + 1) * W)
        gdown = jnp.concatenate([keep_down[p, cols, :] for p in range(keep_down.shape[0])], axis=1)
        for r in range(GROUP):
            rows = slice(r * NARROW, (r + 1) * NARROW)
            right_up.append(dot(shuffled[cols, :][rows], gh[b * GROUP + r], (1, 0)))
            right_dn.append(dot(gdown[rows], active[b * GROUP + r], (1, 0)))
    put(at, 0, mine, other, right_up)
    put(at, 1, mine, other, right_dn)


def grads_call(body, name, at, ins, specs):
    shape = (X, Y, 2, Z_LO, NARROW, W)
    whole = pl.BlockSpec(shape, lambda i, w: (0,) * 6)
    return pl.pallas_call(
        body,
        name=name,
        cost_estimate=cost(6),
        grid_spec=pltpu.PrefetchScalarGridSpec(
            num_scalar_prefetch=1,
            grid=(Z_LO * X,),
            in_specs=specs,
            out_specs=[whole, whole],
        ),
        out_shape=(jax.ShapeDtypeStruct(shape, BF),) * 2,
        compiler_params=room(36),
    )(at, *ins)


def left_grads(at, x, scale, placed, keep):
    count = x.shape[0]
    specs = [
        pl.BlockSpec((count, 2 * W), lambda i, w: (0, i)),
        pl.BlockSpec((count, 1), lambda i, w: (0, 0)),
        pl.BlockSpec((2 * W, count), lambda i, w: (i, 0)),
        pl.BlockSpec((2, count, 2 * W), lambda i, w: (0, 0, i)),
    ]
    return grads_call(left_body, "left_gradients", at, in_hbm(x, scale, placed, keep), specs)


def right_grads(at, shuffled, active, keep_down, ghidden):
    count = shuffled.shape[1]
    parts, _, part = keep_down.shape
    cube = pl.BlockSpec((2 * GROUP, count, W), lambda i, w: (i, 0, 0))
    specs = [
        pl.BlockSpec((2 * W, count), lambda i, w: (i, 0)),
        cube,
        pl.BlockSpec((parts, 2 * W, part), lambda i, w: (0, i, 0)),
        cube,
    ]
    return grads_call(right_body, "right_gradients", at, in_hbm(shuffled, active, keep_down, ghidden), specs)


def shards(acts, cotangent, perm_up, perm_dn, left_up, right_up, right_dn, left_dn):
    up, down = gather_factors(left_up[0], right_up[0], right_dn[0], left_dn[0])
    slots = slot_table()
    at = jnp.stack([place(axis) for axis in ("z", "x", "y", "c")]).astype(jnp.int32)
    perm_up, perm_dn = perm_up[0], perm_dn[0]
    section_count = lax.axis_size("section")
    section_index = lax.axis_index("section")
    final_section = section_count - 1
    micro_count, tok_rows = acts.shape[1:3]
    x = acts[0].reshape(micro_count * tok_rows, D)
    parts = x.shape[0] // CHUNK
    shuffled, active, slope, scale = up_call(slots, perm_up, x, up)
    down = both_cores(join_call(down, scale))
    weights = (up, down)
    incoming = [cotangent.reshape(x.shape)] * parts
    kept = [None] * 3
    sent = [None] * parts
    early = (at[:1] == 1).astype(jnp.int32)
    placed = place_call(early, slots, perm_dn, active, down, (), ())
    for step in range(section_count):
        own = final_section - step
        flag = (section_index == own).astype(jnp.int32).reshape(1)
        for m in range(parts):
            after = (placed,) if m == 0 else ()
            sent[m], *kept = back_call(
                m, flag, slots, perm_up, perm_dn, incoming[m], x, slope, weights, after, [sent[m]] + kept, CHUNK
            )
            if own:
                incoming[m] = lax.ppermute(sent[m], "section", [(own, own - 1)])
        if step == 0:
            placed = place_call(1 - early, slots, perm_dn, active, down, (kept[2],), (placed,))
    keep, keep_down, ghidden = kept
    lefts = fold_cores(*left_grads(at, x, scale, placed, keep))
    left_ring = reduce_ring(lefts, ("x", "y"))
    rights = fold_cores(*right_grads(at, shuffled, active, keep_down, ghidden))
    right_ring = reduce_ring(rights, ("x", "y"))
    owned = finish_factors((left_ring, right_ring))
    results = jnp.concatenate(sent).reshape(acts.shape)
    left_up, left_dn, right_up, right_dn = [owned[i][None] for i in range(4)]
    return (results, left_up, right_up, right_dn, left_dn)


def solution(mesh):
    rows = P("section", "dp", None)
    return jax.shard_map(
        shards,
        mesh=mesh,
        in_specs=(
            P("section", None, "dp", None),
            P(None, "dp", None),
            P("section", None),
            P("section", None),
            rows,
            rows,
            rows,
            rows,
        ),
        out_specs=(P("section", None, "dp", None), rows, rows, rows, rows),
        check_vma=False,
    )
```
